32 devices in a mesh: wide: 8 (over z, x), narrow: 4 (over y, core).
Axes of the slice: x: 2, y: 2, z: 4, core: 2. Of those that a mesh axis runs over, the one named last changes fastest.
Arguments:
- tokens: bfloat16 [8192, 1024], P(('wide', 'narrow')), may hold values from -6 to 6
- lengths: int32 [8], P('wide'), may hold values from 128 to 1024, as said below
- attend_gain: bfloat16 [1024], P(('wide', 'narrow')), may hold values from 0.25 to 1.75
- query_heads: bfloat16 [1024, 96], P(('wide', 'narrow')), may hold values from -0.375 to 0.375
- query_basis: bfloat16 [1024, 384], P(('wide', 'narrow')), may hold values from -0.375 to 0.375
- key_heads: bfloat16 [1024, 32], P(('wide', 'narrow')), may hold values from -0.25 to 0.25
- key_basis: bfloat16 [1024, 128], P(('wide', 'narrow')), may hold values from -0.25 to 0.25
- value_heads: bfloat16 [1024, 32], P(('wide', 'narrow')), may hold values from -0.1875 to 0.1875
- value_basis: bfloat16 [1024, 128], P(('wide', 'narrow')), may hold values from -0.1875 to 0.1875
- merge_weight: bfloat16 [1024, 1024], P(('wide', 'narrow')), may hold values from -2 to 2
- feed_gain: bfloat16 [1024], P(('wide', 'narrow')), may hold values from 0.25 to 1.75
- gate_weight: bfloat16 [1024, 2816], P(('wide', 'narrow')), may hold values from -0.1875 to 0.1875
- up_weight: bfloat16 [1024, 2816], P(('wide', 'narrow')), may hold values from -0.1875 to 0.1875
- down_weight: bfloat16 [2816, 1024], P(('wide', 'narrow')), may hold values from -0.109375 to 0.109375
- cotangent: bfloat16 [8192, 1024], P(('wide', 'narrow')), may hold values from -6 to 6
Outputs:
- output: bfloat16 [8192, 1024], P(('wide', 'narrow'))
- tokens_gradient: float32 [8192, 1024], P(('wide', 'narrow'))
- attend_gain_gradient: float32 [1024], P(('wide', 'narrow'))
- query_heads_gradient: float32 [1024, 96], P(('wide', 'narrow'))
- query_basis_gradient: float32 [1024, 384], P(('wide', 'narrow'))
- key_heads_gradient: float32 [1024, 32], P(('wide', 'narrow'))
- key_basis_gradient: float32 [1024, 128], P(('wide', 'narrow'))
- value_heads_gradient: float32 [1024, 32], P(('wide', 'narrow'))
- value_basis_gradient: float32 [1024, 128], P(('wide', 'narrow'))
- merge_weight_gradient: float32 [1024, 1024], P(('wide', 'narrow'))
- feed_gain_gradient: float32 [1024], P(('wide', 'narrow'))
- gate_weight_gradient: float32 [1024, 2816], P(('wide', 'narrow'))
- up_weight_gradient: float32 [1024, 2816], P(('wide', 'narrow'))
- down_weight_gradient: float32 [2816, 1024], P(('wide', 'narrow'))
The draws below stay inside these ranges and needn't reach their ends.
Inputs may be any that keep to these rules, and one draw needn't show every extreme that they name: `lengths`: some row has all 1024 slots valid in every draw.
All inputs are finite; a program needn't handle non-finite values.
Results may differ from the reference program's by a relative error of at most 0.017.
The reference program's roundings to bfloat16 on the way count: a program that leaves them out, or rounds other values in their place, can miss the bound.
Values may be sent and summed in bfloat16 or wider, within the bound.
No kernel may reach another device: no remote copies, remote signals or barrier semaphores. Data moves between devices by JAX's collectives and lax.ppermute only.
A program may use at most 192 MiB of HBM per device.

```python
import jax
import jax.numpy as jnp
from jax import lax

D = 1024
H = 16
DH = 64
RQ = 6
RK = 2
FF = 2816
MINLEN = 128
SLOTS = 1024
TOKENS = 8192
ROWS = 8


def draw_lengths(key, part):
    first_key, second_key, third_key, fourth_key = jax.random.split(key, 4)
    first_draw = jax.random.randint(first_key, (ROWS,), MINLEN, SLOTS + 1)
    second_draw = jax.random.randint(second_key, (ROWS,), MINLEN, SLOTS + 1)
    third_draw = jax.random.randint(third_key, (ROWS,), MINLEN, SLOTS + 1)
    shortest = jnp.minimum(first_draw, jnp.minimum(second_draw, third_draw))
    chosen = jax.random.randint(fourth_key, (), 0, ROWS)
    return jnp.where(jnp.arange(ROWS) == chosen, SLOTS, shortest).astype(jnp.int32)


def strengthened(drawn, rng, source, target, blocks, factor):
    owner, partner = [(jnp.arange(drawn.shape[axis_at]) // (drawn.shape[axis_at] // blocks)).reshape([-1 if axis == axis_at else 1 for axis in range(drawn.ndim)]) for axis_at in (source, target)]
    chosen = jax.random.permutation(rng, blocks)[partner]
    strong = (owner == chosen) | (owner == (partner + blocks // 2) % blocks)
    return jnp.where(strong, factor * drawn, drawn)


def shard_levels(rng, extent, pieces, low, top_value):
    factor_of = 1.0
    for axis_at, shards_of in pieces:
        draws = jax.random.uniform(jax.random.fold_in(jax.random.fold_in(rng, 6), axis_at), (shards_of,), jnp.float32, low / len(pieces), top_value / len(pieces))
        factor_of = factor_of * jnp.repeat(jnp.exp(draws), extent[axis_at] // shards_of).reshape((-1,) + (1,) * (len(extent) - 1 - axis_at))
    return factor_of


def bell_draw(own_key, dims, deviation, limit, pieces=(), kind=jnp.bfloat16):
    values = deviation * jax.random.normal(own_key, dims, jnp.float32)
    if pieces:
        values = values * shard_levels(own_key, dims, pieces, -0.22, 0.18)
    return jnp.clip(values, -limit, limit).astype(kind)


def heavy_noise(key, shape, scale, bound, shards, heavy, held_as=jnp.bfloat16):
    entries = scale * jax.random.normal(key, shape, jnp.float32)
    if shards:
        entries = entries * shard_levels(key, shape, shards, -0.22, 0.18)
    return jnp.clip(strengthened(entries, jax.random.fold_in(key, 3), *heavy), -bound, bound).astype(held_as)


def setup_inputs(seed: int = 0) -> dict:
    key_of = jax.random.split(jax.random.key(seed), 16)
    return {
        "tokens": heavy_noise(key_of[0], (TOKENS, D), 1.0, 6.0, ((0, 32),), (0, 1, 32, 2.75)),
        "lengths": draw_lengths(jax.random.fold_in(key_of[15], 71), 0),
        "attend_gain": jnp.clip(1.0 + 0.15 * jax.random.normal(key_of[2], (D,), jnp.float32), 0.25, 1.75).astype(jnp.bfloat16),
        "query_heads": bell_draw(key_of[3], (D, H * RQ), (D // 4) ** -0.5, 0.375, ((0, 32),)),
        "query_basis": bell_draw(key_of[4], (D, RQ * DH), (D // 4) ** -0.5, 0.375, ((0, 32),)),
        "key_heads": bell_draw(key_of[5], (D, H * RK), (D // 2) ** -0.5, 0.25, ((0, 32),)),
        "key_basis": bell_draw(key_of[6], (D, RK * DH), (D // 2) ** -0.5, 0.25, ((0, 32),)),
        "value_heads": bell_draw(key_of[7], (D, H * RK), D ** -0.5, 0.1875, ((0, 32),)),
        "value_basis": bell_draw(key_of[8], (D, RK * DH), D ** -0.5, 0.1875, ((0, 32),)),
        "merge_weight": bell_draw(key_of[9], (H * DH, D), (max(D // 128, 1)) ** -0.5, 2.0, ((0, 32),)),
        "feed_gain": jnp.clip(1.0 + 0.15 * jax.random.normal(key_of[10], (D,), jnp.float32), 0.25, 1.75).astype(jnp.bfloat16),
        "gate_weight": bell_draw(key_of[11], (D, FF), D ** -0.5, 0.1875, ((0, 32),)),
        "up_weight": bell_draw(key_of[12], (D, FF), D ** -0.5, 0.1875, ((0, 32),)),
        "down_weight": bell_draw(key_of[13], (FF, D), FF ** -0.5, 0.109375, ((0, 32),)),
        "cotangent": bell_draw(key_of[14], (TOKENS, D), 1.0, 6.0, ((0, 32),)),
    }


EPS = 1e-06
NEG = -1e+30
HIGH = lax.Precision.HIGHEST

@jax.custom_vjp
def low(v):
    return lax.optimization_barrier(v.astype(jnp.bfloat16)).astype(jnp.float32)

@jax.custom_vjp
def low_back(v):
    return v

def low_keep(v):
    return (low(v), None)

def low_pass(kept, grad):
    return (grad,)

def back_keep(v):
    return (v, None)

def back_low(kept, grad):
    return (low(grad),)
low.defvjp(low_keep, low_pass)
low_back.defvjp(back_keep, back_low)

def normalize(value):
    return value * lax.rsqrt(lax.optimization_barrier(jnp.mean(value * value, -1, keepdims=True)) + EPS)

def matmul(left, right):
    return jnp.dot(left, right, precision=HIGH)

def rotate(basis, cosine, sine):
    middle_cut = basis.shape[-1] // 2
    leading = basis[..., :middle_cut]
    trailing = basis[..., middle_cut:]
    cosine_b = cosine[:, None, :]
    sine_b = sine[:, None, :]
    return jnp.concatenate([leading * cosine_b - trailing * sine_b, leading * sine_b + trailing * cosine_b], -1)

def row_layer(row, length, weights):
    attend_gain, query_heads, query_basis, key_heads, key_basis, value_heads, value_basis, merge_weight, feed_gain, gate_weight, up_weight, down_weight = weights
    positions = jnp.arange(SLOTS, dtype=jnp.int32)
    allowed = (positions[None, :] <= positions[:, None]) & (positions[None, :] < length)
    frequency = jnp.power(10000.0, -2.0 * jnp.arange(DH // 2, dtype=jnp.float32) / DH)
    angles = positions.astype(jnp.float32)[:, None] * frequency[None, :]
    cosine = jnp.cos(angles)
    sine = jnp.sin(angles)
    hidden_one = low(normalize(row) * attend_gain)
    query_mix = low_back(matmul(hidden_one, query_heads)).reshape(SLOTS, H, RQ)
    query_turned = rotate(low_back(matmul(hidden_one, query_basis)).reshape(SLOTS, RQ, DH), cosine, sine)
    key_mix = low(low_back(matmul(hidden_one, key_heads))).reshape(SLOTS, H, RK)
    key_turned = low(rotate(low_back(matmul(hidden_one, key_basis)).reshape(SLOTS, RK, DH), cosine, sine))
    value_mix = low(low_back(matmul(hidden_one, value_heads))).reshape(SLOTS, H, RK)
    value_plain = low(low_back(matmul(hidden_one, value_basis))).reshape(SLOTS, RK, DH)
    queries = low(jnp.einsum('shr,srd->shd', query_mix, query_turned, precision=HIGH) / RQ)
    keys = low(jnp.einsum('shr,srd->shd', key_mix, key_turned, precision=HIGH) / RK)
    values = low(jnp.einsum('shr,srd->shd', value_mix, value_plain, precision=HIGH) / RK)
    scores = low_back(jnp.einsum('thd,shd->hts', queries, keys, precision=HIGH) * DH ** (-0.5))
    probs = low(jax.nn.softmax(jnp.where(allowed[None], scores, NEG), axis=-1))
    attended = low(low_back(jnp.einsum('hts,shd->thd', probs, values, precision=HIGH))).reshape(SLOTS, H * DH)
    middle = row + low_back(matmul(attended, merge_weight))
    hidden_two = low(normalize(middle) * feed_gain)
    gate = low_back(matmul(hidden_two, gate_weight))
    upward = low_back(matmul(hidden_two, up_weight))
    return middle + matmul(low(jax.nn.silu(gate) * upward), down_weight)

def reference(tokens, lengths, attend_gain, query_heads, query_basis, key_heads, key_basis, value_heads, value_basis, merge_weight, feed_gain, gate_weight, up_weight, down_weight, cotangent):
    weights = tuple((w.astype(jnp.float32) for w in (attend_gain, query_heads, query_basis, key_heads, key_basis, value_heads, value_basis, merge_weight, feed_gain, gate_weight, up_weight, down_weight)))
    source = tokens.astype(jnp.float32)

    def forward(inputs, params):
        rows = inputs.reshape(ROWS, SLOTS, D)

        def one_row(carry, pair):
            row, length = pair
            return (carry, jax.checkpoint(row_layer)(row, length, params))
        _, results = lax.scan(one_row, jnp.zeros((), jnp.float32), (rows, lengths))
        return results.reshape(TOKENS, D)
    result, pull = jax.vjp(forward, source, weights)
    slope_source, slopes = pull(cotangent.astype(jnp.float32))
    return (result.astype(jnp.bfloat16), slope_source, slopes[0], slopes[1], slopes[2], slopes[3], slopes[4], slopes[5], slopes[6], slopes[7], slopes[8], slopes[9], slopes[10], slopes[11])
```

```python
import functools

import jax
import jax.numpy as jnp
from jax import lax
from jax.experimental import pallas as pl
from jax.experimental.pallas import tpu as pltpu
from jax.sharding import PartitionSpec as P

H = 16
DH = 64
RQ = 6
RK = 2
PAIR = 2
EPS = 1e-06
NEG = -1e30
BF = jnp.bfloat16
F32 = jnp.float32


def dims(left, right, left_dim, right_dim):
    return lax.dot_general(
        left, right, (((left_dim,), (right_dim,)), ((), ())), preferred_element_type=F32
    )


def norm_back(slope, normed, inverse, gain):
    scaled = slope * gain
    return inverse * (scaled - normed * jnp.mean(scaled * normed, -1, keepdims=True))


def flip(value, axis, bit):
    size = lax.axis_size(axis)
    return lax.ppermute(value, axis, [(i, i ^ bit) for i in range(size)])


def turn(value, steps):
    size = lax.axis_size("wide")
    return lax.ppermute(value, "wide", [(i, (i + 2 * steps) % size) for i in range(size)])


def small_mesh():
    return lax.axis_size("wide") == 8 and lax.axis_size("narrow") == 4


def place_kernel(counts, where, *refs):
    pieces, out, sem = refs[: len(counts)], refs[-2], refs[-1]
    copies = []
    at = 0
    for piece, count in zip(pieces, counts):
        for k in range(count):
            copies.append(pltpu.make_async_copy(piece.at[k], out.at[where[at]], sem.at[at]))
            at += 1
    for copy in copies:
        copy.start()
    for copy in copies:
        copy.wait()


def place(pieces, where):
    counts = tuple(p.shape[0] for p in pieces)
    total = sum(counts)
    shape = (total,) + pieces[0].shape[1:]
    size = 2 * total * shape[1] * shape[2]
    return pl.pallas_call(
        functools.partial(place_kernel, counts),
        out_shape=jax.ShapeDtypeStruct(shape, pieces[0].dtype),
        in_specs=[pl.BlockSpec(memory_space=pltpu.SMEM)]
        + [pl.BlockSpec(memory_space=pl.ANY)] * len(pieces),
        out_specs=pl.BlockSpec(memory_space=pl.ANY),
        scratch_shapes=[pltpu.SemaphoreType.DMA((total,))],
        cost_estimate=pl.CostEstimate(flops=0, bytes_accessed=2 * size, transcendentals=0),
    )(jnp.stack(where).astype(jnp.int32), *pieces)


def wide_place():
    me = lax.axis_index("wide")
    return me // 2, me % 2


def gather_wide(value):
    if not small_mesh():
        return lax.all_gather(value, "wide", axis=0, tiled=True)
    high, low = wide_place()
    rounds = lax.axis_size("wide") // 2
    own = [value[None]]
    for _ in range(rounds - 1):
        own.append(turn(own[-1], 1))
    other = [flip(piece, "wide", 1) for piece in own]
    where = [((high - k) % rounds) * 2 + low for k in range(rounds)] + [
        ((high - k) % rounds) * 2 + 1 - low for k in range(rounds)
    ]
    return place(own + other, where).reshape(-1, value.shape[1])


def pick(value, index, axis):
    return lax.dynamic_index_in_dim(value, index, axis, keepdims=False)


def spread_high(value):
    high, _ = wide_place()
    rounds = value.shape[0]
    total = pick(value, high, 0).astype(F32)
    for k in range(1, rounds):
        total = total + turn(pick(value, (high + k) % rounds, 0), k).astype(F32)
    return total


def scatter_wide(value):
    size = lax.axis_size("wide")
    if not small_mesh():
        return lax.psum_scatter(value, "wide", scatter_dimension=0, tiled=True).astype(F32)
    high, low = wide_place()
    blocks = value.reshape(size // 2, 2, value.shape[0] // size, value.shape[1])
    came = flip(pick(blocks, 1 - low, 1), "wide", 1)
    half = (pick(blocks, low, 1).astype(F32) + came.astype(F32)).astype(BF)
    return spread_high(half)


def gather_all(value):
    if not small_mesh():
        return lax.all_gather(value, ("wide", "narrow"), axis=0, tiled=True)
    high, low = wide_place()
    rounds = lax.axis_size("wide") // 2
    near = lax.axis_index("narrow")
    first = jnp.concatenate([value[None]] + [turn(value[None], k) for k in range(1, rounds)], 0)
    second = flip(first, "narrow", 2)
    both = jnp.concatenate([first, second], 0)
    third = flip(both, "wide", 1)
    four = jnp.concatenate([both, third], 0)
    last = flip(four, "narrow", 1)
    where = []
    for c in (0, 1):
        for x in (0, 1):
            for y in (0, 2):
                for k in range(rounds):
                    zx = ((high - k) % rounds) * 2 + (low ^ x)
                    where.append(zx * 4 + (near ^ y ^ c))
    return place([four, last], where).reshape(-1, value.shape[1])


def scatter_all(value):
    if not small_mesh():
        return lax.psum_scatter(
            value, ("wide", "narrow"), scatter_dimension=0, tiled=True
        ).astype(F32)
    high, low = wide_place()
    rounds = lax.axis_size("wide") // 2
    near = lax.axis_index("narrow")
    core, far = near % 2, near // 2
    now = value.reshape(rounds, 2, 2, 2, value.shape[0] // (8 * rounds), value.shape[1])
    for axis, bit, mine, at in (("narrow", 1, core, 3), ("narrow", 2, far, 2), ("wide", 1, low, 1)):
        came = flip(pick(now, 1 - mine, at), axis, bit)
        now = (pick(now, mine, at).astype(F32) + came.astype(F32)).astype(BF)
    return spread_high(now)


def gather_narrow(value):
    pair = jnp.stack([value, flip(value, "narrow", 2)])
    return jnp.concatenate([pair, flip(pair, "narrow", 1)], 0)


def scatter_narrow(value):
    came = flip(value[2:].astype(BF), "narrow", 1)
    pair = value[:2] + came.astype(F32)
    return pair[0] + flip(pair[1].astype(BF), "narrow", 2).astype(F32)


def key_parts(kv_ref, head, at):
    base = at + H * RK
    row = at + head * RK
    total = kv_ref[pl.ds(row, 1), :] * kv_ref[base : base + DH, :]
    total = total + kv_ref[pl.ds(row + 1, 1), :] * kv_ref[base + DH : base + 2 * DH, :]
    return (total * (1.0 / RK)).astype(BF)


def query_parts(qm_ref, qt_ref, head):
    total = qm_ref[pl.ds(head * RQ, 1), :] * qt_ref[0:DH, :]
    for r in range(1, RQ):
        total = total + qm_ref[pl.ds(head * RQ + r, 1), :] * qt_ref[r * DH : (r + 1) * DH, :]
    queries = (total * (1.0 / RQ)).astype(BF)
    return (queries.astype(F32) * DH**-0.5).astype(BF)


def attend_kernel(place_ref, qm_ref, qt_ref, kv_ref, attended_ref, probs_ref, bias):
    pair = pl.program_id(0)
    tok, slots = bias.shape

    @pl.when(pair == 0)
    def _():
        near, length = place_ref[0], place_ref[1]
        rows = near * tok + lax.broadcasted_iota(jnp.int32, (tok, tok), 0)
        for block, bit in enumerate((0, 2, 1, 3)):
            keys = (near ^ bit) * tok + lax.broadcasted_iota(jnp.int32, (tok, tok), 1)
            allowed = (keys <= rows) & (keys < length)
            bias[:, block * tok : (block + 1) * tok] = jnp.where(allowed, 0.0, NEG)

    outs = []
    for inner in range(PAIR):
        head = pair * PAIR + inner
        keys = key_parts(kv_ref, head, 0)
        values = key_parts(kv_ref, head, H * RK + RK * DH)
        queries = query_parts(qm_ref, qt_ref, head)
        scores = dims(queries, keys, 0, 0) + bias[...]
        peak = jnp.max(scores, -1, keepdims=True)
        powers = jnp.exp(scores - peak)
        total = jnp.sum(powers, -1, keepdims=True)
        probs = (powers * (1.0 / total)).astype(BF)
        probs_ref[inner] = probs
        outs.append(dims(probs, values, 1, 1))
    attended_ref[...] = jnp.concatenate(outs, 1).astype(BF)


def attend(places, query_mix, query_turned, row_factors):
    tok = query_mix.shape[1]
    slots = row_factors.shape[1]
    whole = lambda array: pl.BlockSpec(array.shape, lambda i: (0, 0))
    return pl.pallas_call(
        attend_kernel,
        grid=(H // PAIR,),
        out_shape=(
            jax.ShapeDtypeStruct((tok, H * DH), BF),
            jax.ShapeDtypeStruct((H, tok, slots), BF),
        ),
        in_specs=[
            pl.BlockSpec(memory_space=pltpu.SMEM),
            whole(query_mix),
            whole(query_turned),
            whole(row_factors),
        ],
        out_specs=(
            pl.BlockSpec((tok, PAIR * DH), lambda i: (0, i)),
            pl.BlockSpec((PAIR, tok, slots), lambda i: (i, 0, 0)),
        ),
        scratch_shapes=[pltpu.VMEM((tok, slots), F32)],
        compiler_params=pltpu.CompilerParams(vmem_limit_bytes=48 * 2**20),
        cost_estimate=pl.CostEstimate(
            flops=16 * tok * slots * H * DH, bytes_accessed=2 * H * tok * slots, transcendentals=0
        ),
    )(places, query_mix, query_turned, row_factors)


def attend_back_kernel(
    qm_ref, qt_ref, kv_ref, slope_ref, probs_ref, mix_ref, basis_ref, qmix_ref, qbasis_ref
):
    pair = pl.program_id(0)
    vm = H * RK + RK * DH

    @pl.when(pair == 0)
    def _():
        basis_ref[...] = jnp.zeros_like(basis_ref)
        qbasis_ref[...] = jnp.zeros_like(qbasis_ref)

    for inner in range(PAIR):
        head = pair * PAIR + inner
        keys = key_parts(kv_ref, head, 0)
        values = key_parts(kv_ref, head, vm)
        queries = query_parts(qm_ref, qt_ref, head)
        slope = slope_ref[inner * DH : (inner + 1) * DH, :]
        probs_low = probs_ref[inner]
        slope_probs = dims(slope, values, 0, 0)
        probs = probs_low.astype(F32)
        weighted = probs * slope_probs
        total = jnp.sum(weighted, -1, keepdims=True)
        slope_scores = (weighted - probs * total).astype(BF)
        slope_query = dims(keys, slope_scores, 1, 1) * (DH**-0.5 / RQ)
        slope_key = dims(queries, slope_scores, 1, 0) * (1.0 / RK)
        slope_value = dims(slope, probs_low, 1, 0) * (1.0 / RK)
        for r in range(RK):
            row = head * RK + r
            for at, piece, side in ((0, slope_key, 0), (vm, slope_value, 1)):
                base = at + H * RK + r * DH
                here = side * RK + r
                basis_ref[here * DH : (here + 1) * DH, :] += kv_ref[pl.ds(at + row, 1), :] * piece
                mix_ref[pl.ds(side * H * RK + row, 1), :] = jnp.sum(
                    piece * kv_ref[base : base + DH, :], 0, keepdims=True
                )
        for r in range(RQ):
            row = head * RQ + r
            cut = slice(r * DH, (r + 1) * DH)
            qbasis_ref[cut, :] += qm_ref[pl.ds(row, 1), :] * slope_query
            qmix_ref[pl.ds(row, 1), :] = jnp.sum(slope_query * qt_ref[cut, :], 0, keepdims=True)


def attend_back(query_mix, query_turned, row_factors, slope_attended, probs):
    tok = query_mix.shape[1]
    slots = row_factors.shape[1]
    whole = lambda array: pl.BlockSpec(array.shape, lambda i: (0, 0))
    outs = (
        jax.ShapeDtypeStruct((2 * H * RK, slots), F32),
        jax.ShapeDtypeStruct((2 * RK * DH, slots), F32),
        jax.ShapeDtypeStruct((H * RQ, tok), F32),
        jax.ShapeDtypeStruct((RQ * DH, tok), F32),
    )
    return pl.pallas_call(
        attend_back_kernel,
        grid=(H // PAIR,),
        out_shape=outs,
        in_specs=[
            whole(query_mix),
            whole(query_turned),
            whole(row_factors),
            pl.BlockSpec((PAIR * DH, tok), lambda i: (i, 0)),
            pl.BlockSpec((PAIR, tok, slots), lambda i: (i, 0, 0)),
        ],
        out_specs=tuple(whole(o) for o in outs),
        compiler_params=pltpu.CompilerParams(vmem_limit_bytes=48 * 2**20),
        cost_estimate=pl.CostEstimate(
            flops=32 * tok * slots * H * DH, bytes_accessed=2 * H * tok * slots, transcendentals=0
        ),
    )(query_mix, query_turned, row_factors, slope_attended, probs)


def rotate(value, cosine, sine, sign):
    blocks = value.reshape(-1, 2, DH // 2, value.shape[1])
    first, second = blocks[:, 0], blocks[:, 1]
    turned = jnp.stack(
        [first * cosine - sign * second * sine, sign * first * sine + second * cosine], 1
    )
    return turned.reshape(value.shape)


QB, KB, VB = RQ * DH, RK * DH, RK * DH
QM, KM, VM = H * RQ, H * RK, H * RK
CUTS = (QB, KB, VB, QM, KM, VM)
FACTORS = sum(CUTS)
PACKED = 896


def per_device(
    tokens,
    lengths,
    attend_gain,
    query_heads,
    query_basis,
    key_heads,
    key_basis,
    value_heads,
    value_basis,
    merge_weight,
    feed_gain,
    gate_weight,
    up_weight,
    down_weight,
    cotangent,
):
    tok, width = tokens.shape
    wide_count = lax.axis_size("wide")
    narrow_count = lax.axis_size("narrow")
    near = lax.axis_index("narrow")
    rows = gate_weight.shape[0]
    cut = down_weight.shape[0]
    hidden = cut * wide_count

    positions = (near * tok + jnp.arange(tok, dtype=jnp.int32)).astype(F32)
    frequency = jnp.power(10000.0, -2.0 * jnp.arange(DH // 2, dtype=F32) / DH)
    angles = frequency[:, None] * positions[None, :]
    cosine, sine = jnp.cos(angles), jnp.sin(angles)

    packed = jnp.concatenate(
        [
            query_basis,
            key_basis,
            value_basis,
            query_heads,
            key_heads,
            value_heads,
            attend_gain[:, None],
            feed_gain[:, None],
            jnp.zeros((rows, PACKED - FACTORS - 2), BF),
        ],
        1,
    )
    packed = gather_all(packed)
    factor_weights = packed[:, :FACTORS]
    gain_first = packed[:, FACTORS].astype(F32)[None, :]
    gain_second = packed[:, FACTORS + 1].astype(F32)[None, :]
    merge = gather_all(merge_weight)

    def columns(weight):
        parts = weight.reshape(rows, wide_count, narrow_count, cut).transpose(2, 0, 1, 3)
        return parts.reshape(narrow_count, rows, hidden)

    halves = jnp.concatenate([columns(gate_weight), columns(up_weight)], 1)
    halves = lax.all_to_all(halves, "narrow", 0, 0, tiled=True)
    gate_mine = halves[:, :rows].reshape(narrow_count * rows, hidden)
    up_mine = halves[:, rows:].reshape(narrow_count * rows, hidden)
    gate_full = gather_wide(gate_mine)
    up_full = gather_wide(up_mine)
    down_full = gather_wide(down_weight)
    cotangents = gather_narrow(cotangent).reshape(narrow_count * tok, width)

    source = tokens.astype(F32)
    inverse_one = lax.rsqrt(jnp.mean(source * source, -1, keepdims=True) + EPS)
    normed_one = source * inverse_one
    hidden_one = (normed_one * gain_first).astype(BF)
    factors = dims(factor_weights, hidden_one, 0, 1)
    ends = [sum(CUTS[: i + 1]) for i in range(len(CUTS))]
    query_turned = rotate(factors[: ends[0]], cosine, sine, 1.0)
    key_turned = rotate(factors[ends[0] : ends[1]], cosine, sine, 1.0)
    value_plain = factors[ends[1] : ends[2]]
    query_mix = factors[ends[2] : ends[3]]
    key_mix = factors[ends[3] : ends[4]]
    value_mix = factors[ends[4] : ends[5]]
    own_factors = jnp.concatenate([key_mix, key_turned, value_mix, value_plain], 0).astype(BF)
    pair_factors = jnp.concatenate([own_factors, flip(own_factors, "narrow", 2)], 1)
    row_factors = jnp.concatenate(
        [pair_factors, flip(pair_factors, "narrow", 1)], 1
    ).astype(F32)
    places = jnp.stack([near.astype(jnp.int32), lengths[0].astype(jnp.int32)])
    attended, probs = attend(places, query_mix, query_turned, row_factors)
    middle = source + dims(attended, merge, 1, 0)
    inverse_two = lax.rsqrt(jnp.mean(middle * middle, -1, keepdims=True) + EPS)
    normed_two = middle * inverse_two
    hidden_two = (normed_two * gain_second).astype(BF)

    hidden_group = gather_narrow(hidden_two).reshape(narrow_count * tok, width)
    gate = dims(hidden_group, gate_full, 1, 0)
    upward = dims(hidden_group, up_full, 1, 0)
    sigmoid_gate = jax.nn.sigmoid(gate)
    hidden_feed = (gate * sigmoid_gate * upward).astype(BF)
    slope_feed = dims(cotangents, down_full, 1, 1)
    slope_up = (slope_feed * gate * sigmoid_gate).astype(BF)
    slope_gate = (slope_feed * upward * sigmoid_gate * (1.0 + gate * (1.0 - sigmoid_gate))).astype(
        BF
    )
    slope_group = dims(slope_gate, gate_full, 1, 1) + dims(slope_up, up_full, 1, 1)
    slope_normed_two = scatter_narrow(slope_group.reshape(narrow_count, tok, width))
    gate_slope = scatter_wide(dims(hidden_group, slope_gate, 0, 0).astype(BF))
    up_slope = scatter_wide(dims(hidden_group, slope_up, 0, 0).astype(BF))
    down_slope = scatter_wide(dims(hidden_feed, cotangents, 0, 0).astype(BF))
    fed = dims(hidden_feed, down_full, 1, 0)
    output = (middle + scatter_narrow(fed.reshape(narrow_count, tok, width))).astype(BF)

    slopes = jnp.concatenate(
        [
            gate_slope.reshape(narrow_count, rows, hidden),
            up_slope.reshape(narrow_count, rows, hidden),
        ],
        1,
    ).astype(BF)
    slopes = lax.all_to_all(slopes, "narrow", 0, 0, tiled=True)
    slopes = slopes.reshape(narrow_count, 2, rows, wide_count, cut).transpose(1, 2, 3, 0, 4)
    slopes = slopes.reshape(2, rows, hidden * narrow_count).astype(F32)

    slope_middle = cotangent.astype(F32) + norm_back(
        slope_normed_two, normed_two, inverse_two, gain_second
    )
    feed_gain_slope = jnp.sum(slope_normed_two * normed_two, 0)
    slope_low = slope_middle.astype(BF)
    merge_slope = scatter_all(dims(attended, slope_low, 0, 0).astype(BF))
    slope_attended = dims(merge, slope_low, 1, 1).astype(BF)
    mixes, bases, query_mix_slope, query_basis_slope = attend_back(
        query_mix, query_turned, row_factors, slope_attended, probs
    )
    kv_slopes = jnp.concatenate([mixes[:KM], bases[:KB], mixes[KM:], bases[KB:]], 0).astype(BF)
    came = flip(kv_slopes[:, 2 * tok :], "narrow", 1)
    kept = kv_slopes[:, : 2 * tok].astype(F32) + came.astype(F32)
    own_slope = kept[:, :tok] + flip(kept[:, tok:].astype(BF), "narrow", 2).astype(F32)
    slope_factors = jnp.concatenate(
        [
            rotate(query_basis_slope, cosine, sine, -1.0),
            rotate(own_slope[KM : KM + KB], cosine, sine, -1.0),
            own_slope[2 * KM + KB :],
            query_mix_slope,
            own_slope[:KM],
            own_slope[KM + KB : 2 * KM + KB],
        ],
        0,
    ).astype(BF)
    slope_normed_one = dims(slope_factors, factor_weights, 0, 1)
    attend_gain_slope = jnp.sum(slope_normed_one * normed_one, 0)
    tokens_slope = slope_middle + norm_back(slope_normed_one, normed_one, inverse_one, gain_first)
    factor_slopes = scatter_all(
        jnp.concatenate(
            [
                dims(hidden_one, slope_factors, 0, 1),
                attend_gain_slope[:, None],
                feed_gain_slope[:, None],
                jnp.zeros((width, PACKED - FACTORS - 2), F32),
            ],
            1,
        ).astype(BF)
    )
    return (
        output,
        tokens_slope,
        factor_slopes[:, FACTORS],
        factor_slopes[:, ends[2] : ends[3]],
        factor_slopes[:, : ends[0]],
        factor_slopes[:, ends[3] : ends[4]],
        factor_slopes[:, ends[0] : ends[1]],
        factor_slopes[:, ends[4] : ends[5]],
        factor_slopes[:, ends[1] : ends[2]],
        merge_slope,
        factor_slopes[:, FACTORS + 1],
        slopes[0],
        slopes[1],
        down_slope,
    )


def solution(mesh):
    both = ("wide", "narrow")
    row, vector = P(both, None), P(both)
    return jax.shard_map(
        per_device,
        mesh=mesh,
        in_specs=(row, P("wide"), vector) + (row,) * 7 + (vector,) + (row,) * 4,
        out_specs=(row, row, vector) + (row,) * 7 + (vector,) + (row,) * 3,
        check_vma=False,
    )
```

```python
import functools

import jax
import jax.numpy as jnp
from jax import lax
from jax.experimental import pallas as pl
from jax.experimental.pallas import tpu as pltpu
from jax.sharding import PartitionSpec as P

H = 16
DH = 64
RQ = 6
RK = 2
PAIR = 2
EPS = 1e-06
NEG = -1e30
BF = jnp.bfloat16
F32 = jnp.float32


def dims(left, right, left_dim, right_dim):
    return lax.dot_general(
        left, right, (((left_dim,), (right_dim,)), ((), ())), preferred_element_type=F32
    )


def norm_back(slope, normed, inverse, gain):
    scaled = slope * gain
    return inverse * (scaled - normed * jnp.mean(scaled * normed, -1, keepdims=True))


def flip(value, axis, bit):
    size = lax.axis_size(axis)
    return lax.ppermute(value, axis, [(i, i ^ bit) for i in range(size)])


def turn(value, steps):
    size = lax.axis_size("wide")
    return lax.ppermute(value, "wide", [(i, (i + 2 * steps) % size) for i in range(size)])


def small_mesh():
    return lax.axis_size("wide") == 8 and lax.axis_size("narrow") == 4


def wide_place():
    me = lax.axis_index("wide")
    return me // 2, me % 2


def after(value, *others):
    return lax.optimization_barrier((value, others))[0]


def pick(value, index, axis):
    return lax.dynamic_index_in_dim(value, index, axis, keepdims=False)


def spread_high(blocks):
    total = blocks[0].astype(F32)
    for k in range(1, len(blocks)):
        total = total + turn(blocks[k], k).astype(F32)
    return total


def ring_blocks(value):
    high, _ = wide_place()
    rounds = value.shape[0]
    return [pick(value, (high + k) % rounds, 0) for k in range(rounds)]


def scatter_wide(value):
    size = lax.axis_size("wide")
    if not small_mesh():
        return lax.psum_scatter(value, "wide", scatter_dimension=0, tiled=True).astype(F32)
    high, low = wide_place()
    blocks = value.reshape(size // 2, 2, value.shape[0] // size, value.shape[1])
    came = flip(pick(blocks, 1 - low, 1), "wide", 1)
    half = (pick(blocks, low, 1).astype(F32) + came.astype(F32)).astype(BF)
    return spread_high(ring_blocks(half))


def turned(value):
    rounds = lax.axis_size("wide") // 2
    return [value] + [turn(value, k) for k in range(1, rounds)]


def joined(value, axis, bit):
    return jnp.concatenate([value, flip(value, axis, bit)], 0)


def relative_blocks():
    high, low = wide_place()
    rounds = lax.axis_size("wide") // 2
    near = lax.axis_index("narrow")
    return [
        (((high - k) % rounds) * 2 + (low ^ x)) * 4 + (near ^ (2 * y) ^ c)
        for c in (0, 1)
        for x in (0, 1)
        for y in (0, 1)
        for k in range(rounds)
    ]


def scatter_all(value):
    return lax.psum_scatter(value, ("wide", "narrow"), scatter_dimension=0, tiled=True).astype(F32)


def scatter_order():
    high, low = wide_place()
    rounds = lax.axis_size("wide") // 2
    near = lax.axis_index("narrow")
    return [
        (((high + k) % rounds) * 2 + (low ^ x)) * 4 + (near ^ (2 * y) ^ c)
        for c in (0, 1)
        for y in (0, 1)
        for x in (0, 1)
        for k in range(rounds)
    ]


def spread_stages(now):
    for axis, bit in (("narrow", 2), ("wide", 1)):
        half = now.shape[0] // 2
        now = add_low(now[:half], flip(now[half:], axis, bit))
    return spread_high([now[k] for k in range(now.shape[0])])


def add_low(kept, came):
    return (kept.astype(F32) + came.astype(F32)).astype(BF)


def gather_narrow(value):
    far = flip(value, "narrow", 2)
    return [value, far, flip(value, "narrow", 1), flip(far, "narrow", 1)]


def scatter_narrow(kept, sent):
    pair = kept + flip(sent, "narrow", 1).astype(F32)
    return pair[0] + flip(pair[1].astype(BF), "narrow", 2).astype(F32)


def starts(stacks, where_ref, first, target, sem):
    copies = []
    for stack in stacks:
        for k in range(stack.shape[0]):
            at = len(copies)
            copies.append(
                pltpu.make_async_copy(
                    stack.at[k], target.at[where_ref[first + at]], sem.at[first + at]
                )
            )
            copies[-1].start()
    return copies


def count(stacks):
    return sum(stack.shape[0] for stack in stacks)


def whole(array):
    return pl.BlockSpec(array.shape, lambda *i: (0,) * len(array.shape))


ANYWHERE = pl.BlockSpec(memory_space=pl.ANY)
SCALARS = pl.BlockSpec(memory_space=pltpu.SMEM)


def scalars(*lists):
    return jnp.stack([jnp.asarray(v, jnp.int32) for one in lists for v in one])


def order_kernel(n, where, *refs):
    for copy in starts(refs[:n], where, 0, refs[n], refs[n + 1]):
        copy.wait()


def put_in_order(stacks, where):
    total = count(stacks)
    if total == 1:
        return stacks[0][0]
    shape = (total,) + stacks[0].shape[1:]
    out = jax.ShapeDtypeStruct(shape, stacks[0].dtype)
    return pl.pallas_call(
        functools.partial(order_kernel, len(stacks)),
        out_shape=out,
        in_specs=[SCALARS] + [ANYWHERE] * len(stacks),
        out_specs=pl.BlockSpec(memory_space=pltpu.VMEM),
        scratch_shapes=[pltpu.SemaphoreType.DMA((total,))],
        compiler_params=pltpu.CompilerParams(vmem_limit_bytes=16 * 2**20),
        cost_estimate=pl.CostEstimate(
            flops=0, bytes_accessed=4 * shape[0] * shape[1] * shape[2], transcendentals=0
        ),
    )(scalars(where), *stacks).reshape(-1, shape[2])


def project_kernel(n, where, tokens_ref, cos_ref, sin_ref, *refs):
    packed, refs = refs[:n], refs[n:]
    hidden_ref, inverse_ref, gains_ref, packed_ref, qm_ref, qt_ref, kv_ref, sem = refs
    copies = starts(packed, where, 0, packed_ref, sem)
    source = tokens_ref[...].astype(F32)
    inverse = lax.rsqrt(jnp.mean(source * source, -1, keepdims=True) + EPS)
    inverse_ref[...] = inverse
    normed = source * inverse
    for copy in copies:
        copy.wait()
    width = source.shape[1]
    weights = packed_ref[...].reshape(width, PACKED)
    gains = weights[:, PACKED - 128 :].astype(F32).T
    at = GAINS - (PACKED - 128)
    gains_ref[...] = gains[at : at + 8]
    hidden = (normed * gains[at : at + 1]).astype(BF)
    hidden_ref[...] = hidden
    factors = dims(hidden, weights, 1, 0).T
    cosine, sine = cos_ref[...], sin_ref[...]
    half = DH // 2
    for r in range(RQ + RK):
        base = r * DH if r < RQ else LEFT + (r - RQ) * DH
        one = factors[base : base + half]
        two = factors[base + half : base + DH]
        a, b = one * cosine - two * sine, one * sine + two * cosine
        if r < RQ:
            qt_ref[base : base + half, :] = a
            qt_ref[base + half : base + DH, :] = b
        else:
            row = KM + (r - RQ) * DH
            kv_ref[row : row + half, :] = a.astype(BF)
            kv_ref[row + half : row + DH, :] = b.astype(BF)
    qm_ref[...] = factors[QB : QB + QM]
    base = LEFT + KB
    kv_ref[2 * KM + KB :, :] = factors[base : base + VB].astype(BF)
    base += VB
    kv_ref[0:KM, :] = factors[base : base + KM].astype(BF)
    kv_ref[KM + KB : 2 * KM + KB, :] = factors[base + KM : base + 2 * KM].astype(BF)


VMEM = pl.BlockSpec(memory_space=pltpu.VMEM)


def project(tokens, cosine, sine, packed, where):
    tok, width = tokens.shape
    outs = (
        jax.ShapeDtypeStruct((tok, width), BF),
        jax.ShapeDtypeStruct((tok, 1), F32),
        jax.ShapeDtypeStruct((8, width), F32),
        jax.ShapeDtypeStruct((count(packed),) + packed[0].shape[1:], BF),
        jax.ShapeDtypeStruct((QM, tok), F32),
        jax.ShapeDtypeStruct((QB, tok), F32),
        jax.ShapeDtypeStruct((2 * (KM + KB), tok), BF),
    )
    return pl.pallas_call(
        functools.partial(project_kernel, len(packed)),
        out_shape=outs,
        in_specs=[SCALARS] + [VMEM] * 3 + [ANYWHERE] * len(packed),
        out_specs=tuple(VMEM for _ in outs),
        scratch_shapes=[pltpu.SemaphoreType.DMA((count(packed),))],
        compiler_params=pltpu.CompilerParams(vmem_limit_bytes=20 * 2**20),
        cost_estimate=pl.CostEstimate(
            flops=2 * tok * width * PACKED, bytes_accessed=6 * 2**20, transcendentals=0
        ),
    )(scalars(where), tokens, cosine, sine, *packed)


def halves_of(both_ref, width, hidden):
    rows = both_ref.shape[2] // 2
    return (
        both_ref[:, :, :rows, :].reshape(width, hidden),
        both_ref[:, :, rows:, :].reshape(width, hidden),
    )


def feed_kernel(nb, nd, where, *refs):
    pieces, refs = refs[:4], refs[4:]
    cots, refs = refs[:4], refs[4:]
    boths, refs = refs[:nb], refs[nb:]
    downs, refs = refs[:nd], refs[nd:]
    hf_ref, sg_ref, su_ref, kept_ref, sent_ref, hid, cot, wgu, wd, sem, psem = refs
    width, hidden = hid.shape[2], wgu.shape[3]
    loads = [
        [
            pltpu.make_async_copy(pieces[b], hid.at[b], psem.at[b]),
            pltpu.make_async_copy(cots[b], cot.at[b], psem.at[4 + b]),
        ]
        for b in range(4)
    ]
    loads[0][0].start()
    in_both = starts(boths, where, 0, wgu, sem)
    loads[0][1].start()
    in_down = starts(downs, where, count(boths), wd, sem)
    for b in range(1, 4):
        for copy in loads[b]:
            copy.start()
    for b in range(4):
        loads[b][0].wait()
        if b == 0:
            for copy in in_both:
                copy.wait()
        gate_all, up_all = halves_of(wgu, width, hidden)
        gate = dims(hid[b], gate_all, 1, 0)
        upward = dims(hid[b], up_all, 1, 0)
        loads[b][1].wait()
        if b == 0:
            for copy in in_down:
                copy.wait()
        down_all = wd[...].reshape(hidden, width)
        slope = dims(cot[b], down_all, 1, 1)
        sig = jax.nn.sigmoid(gate)
        silu = gate * sig
        hf_ref[b] = (silu * upward).astype(BF)
        slope_up = (slope * silu).astype(BF)
        slope_gate = (slope * upward * sig * (1.0 + gate * (1.0 - sig))).astype(BF)
        su_ref[b] = slope_up
        sg_ref[b] = slope_gate
        back = dims(slope_gate, gate_all, 1, 1) + dims(slope_up, up_all, 1, 1)
        if b < 2:
            kept_ref[b] = back
        else:
            sent_ref[b - 2] = back.astype(BF)


def feed(pieces, cots, boths, both_where, downs, down_where):
    tok, width = pieces[0].shape
    hidden = boths[0].shape[3]
    low = jax.ShapeDtypeStruct((4, tok, hidden), BF)
    outs = (
        low,
        low,
        low,
        jax.ShapeDtypeStruct((2, tok, width), F32),
        jax.ShapeDtypeStruct((2, tok, width), BF),
    )
    blocks = lambda stacks: pltpu.VMEM((count(stacks),) + stacks[0].shape[1:], BF)
    total = count(boths) + count(downs)
    return pl.pallas_call(
        functools.partial(feed_kernel, len(boths), len(downs)),
        out_shape=outs,
        in_specs=[SCALARS] + [ANYWHERE] * (8 + len(boths) + len(downs)),
        out_specs=tuple(VMEM for _ in outs),
        scratch_shapes=[
            pltpu.VMEM((4, tok, width), BF),
            pltpu.VMEM((4, tok, width), BF),
            blocks(boths),
            blocks(downs),
            pltpu.SemaphoreType.DMA((total,)),
            pltpu.SemaphoreType.DMA((8,)),
        ],
        compiler_params=pltpu.CompilerParams(vmem_limit_bytes=36 * 2**20),
        cost_estimate=pl.CostEstimate(
            flops=10 * 4 * tok * width * hidden, bytes_accessed=16 * 2**20, transcendentals=0
        ),
    )(scalars(both_where, down_where), *pieces, *cots, *boths, *downs)


def slopes_kernel(blocks, order, *refs):
    pieces = refs[:4]
    sg_ref, su_ref, out_g, out_u, hid, psem = refs[4:]
    copies = [pltpu.make_async_copy(pieces[b], hid.at[b], psem.at[b]) for b in range(4)]
    for copy in copies:
        copy.start()
    for copy in copies:
        copy.wait()
    rows = out_g.shape[2]
    columns = []
    for k in range(blocks):
        at = pl.multiple_of(order[k] * rows, 128)
        columns.append(jnp.concatenate([hid[b, :, pl.ds(at, rows)] for b in range(4)], 0))
    chosen = jnp.concatenate(columns, 1)
    for ref, out in ((sg_ref, out_g), (su_ref, out_u)):
        slope = ref[...].reshape(chosen.shape[0], ref.shape[2])
        result = dims(slope, chosen, 0, 0).astype(BF)
        for k in range(blocks):
            out[k] = result[:, k * rows : (k + 1) * rows]


def slopes_of(pieces, slope_gate, slope_up, order):
    tok, width = pieces[0].shape
    hidden = slope_gate.shape[2]
    rows = 128
    out = jax.ShapeDtypeStruct((len(order), hidden, rows), BF)
    return pl.pallas_call(
        functools.partial(slopes_kernel, len(order)),
        out_shape=(out, out),
        in_specs=[SCALARS] + [ANYWHERE] * 4 + [VMEM, VMEM],
        out_specs=(VMEM, VMEM),
        scratch_shapes=[pltpu.VMEM((4, tok, width), BF), pltpu.SemaphoreType.DMA((4,))],
        compiler_params=pltpu.CompilerParams(vmem_limit_bytes=24 * 2**20),
        cost_estimate=pl.CostEstimate(
            flops=4 * 4 * tok * len(order) * rows * hidden,
            bytes_accessed=8 * 2**20,
            transcendentals=0,
        ),
    )(scalars(order), *pieces, slope_gate, slope_up)


def down_kernel(hf_ref, c0, c1, c2, c3, down_ref):
    total = None
    for b, cot in enumerate((c0, c1, c2, c3)):
        part = dims(hf_ref[b], cot[...], 0, 0)
        total = part if total is None else total + part
    down_ref[...] = total.astype(BF)


def down_slopes(hidden_feed, cots):
    tok, width = cots[0].shape
    hidden = hidden_feed.shape[2]
    return pl.pallas_call(
        down_kernel,
        out_shape=jax.ShapeDtypeStruct((hidden, width), BF),
        in_specs=[VMEM] * 5,
        out_specs=VMEM,
        compiler_params=pltpu.CompilerParams(vmem_limit_bytes=24 * 2**20),
        cost_estimate=pl.CostEstimate(
            flops=2 * 4 * tok * width * hidden, bytes_accessed=6 * 2**20, transcendentals=0
        ),
    )(hidden_feed, *cots)


def feed_out_kernel(nd, where, *refs):
    downs, (hf_ref, kept_ref, sent_ref, wd, sem) = refs[:nd], refs[nd:]
    for copy in starts(downs, where, 0, wd, sem):
        copy.wait()
    down_all = wd[...].reshape(hf_ref.shape[2], wd.shape[2])
    for b in range(4):
        fed = dims(hf_ref[b], down_all, 1, 0)
        if b < 2:
            kept_ref[b] = fed
        else:
            sent_ref[b - 2] = fed.astype(BF)


def feed_out(hidden_feed, downs, down_where):
    tok, hidden = hidden_feed.shape[1:]
    width = downs[0].shape[2]
    outs = (
        jax.ShapeDtypeStruct((2, tok, width), F32),
        jax.ShapeDtypeStruct((2, tok, width), BF),
    )
    return pl.pallas_call(
        functools.partial(feed_out_kernel, len(downs)),
        out_shape=outs,
        in_specs=[SCALARS] + [ANYWHERE] * len(downs) + [VMEM],
        out_specs=(VMEM,) * 2,
        scratch_shapes=[
            pltpu.VMEM((count(downs),) + downs[0].shape[1:], BF),
            pltpu.SemaphoreType.DMA((count(downs),)),
        ],
        compiler_params=pltpu.CompilerParams(vmem_limit_bytes=24 * 2**20),
        cost_estimate=pl.CostEstimate(
            flops=2 * 4 * tok * width * hidden, bytes_accessed=8 * 2**20, transcendentals=0
        ),
    )(scalars(down_where), *downs, hidden_feed)


def emit(total, order, held, sent_ref, kept_ref):
    held[...] = total.reshape(held.shape)
    half = sent_ref.shape[0]
    for k in range(half):
        kept_ref[k] = held[order[k]].astype(kept_ref.dtype)
        sent_ref[k] = held[order[half + k]].astype(BF)


def outer_kernel(order, left_ref, right_ref, sent_ref, kept_ref, held):
    emit(dims(left_ref[...], right_ref[...], 0, 0), order, held, sent_ref, kept_ref)


def blocks_out(order, width, columns):
    half = len(order) // 2
    rows = width // len(order)
    out = jax.ShapeDtypeStruct((half, rows, columns), BF)
    return out, pltpu.VMEM((len(order), rows, columns), F32)


def outer_blocks(order, left, right):
    tok, width = left.shape
    columns = right.shape[1]
    out, held = blocks_out(order, width, columns)
    return pl.pallas_call(
        outer_kernel,
        out_shape=(out, out),
        in_specs=[SCALARS, VMEM, VMEM],
        out_specs=(VMEM, VMEM),
        scratch_shapes=[held],
        compiler_params=pltpu.CompilerParams(vmem_limit_bytes=20 * 2**20),
        cost_estimate=pl.CostEstimate(
            flops=2 * tok * width * columns, bytes_accessed=4 * 2**20, transcendentals=0
        ),
    )(scalars(order), left, right)


def unturn(value, cosine, sine):
    half = DH // 2
    one, two = value[:half], value[half:]
    return [one * cosine + two * sine, two * cosine - one * sine]


def query_end_kernel(
    order, qmix_ref, qbasis_ref, cos_ref, sin_ref, hidden_ref, weights_ref, *refs
):
    part_ref, outs = refs[0], refs[1:]
    cosine, sine = cos_ref[...], sin_ref[...]
    parts = []
    for r in range(RQ):
        parts += unturn(qbasis_ref[r * DH : (r + 1) * DH, :], cosine, sine)
    tok = cosine.shape[1]
    parts += [qmix_ref[...], jnp.zeros((LEFT - QB - QM, tok), F32)]
    slopes = jnp.concatenate(parts, 0).astype(BF)
    weights = weights_ref[...].reshape(hidden_ref.shape[1], PACKED)[:, :LEFT]
    part_ref[...] = dims(slopes, weights, 0, 1)
    total = dims(hidden_ref[...], slopes, 0, 1)
    if len(outs) == 1:
        outs[0][...] = total.astype(BF)
    else:
        emit(total, order, outs[2], outs[0], outs[1])


def query_end(order, qmix, qbasis, cosine, sine, hidden, weights):
    tok, width = hidden.shape
    outs = [jax.ShapeDtypeStruct((tok, width), F32)]
    scratch = []
    if len(order) > 1:
        out, held = blocks_out(order, width, LEFT)
        outs += [out, out]
        scratch = [held]
    else:
        outs += [jax.ShapeDtypeStruct((width, LEFT), BF)]
    return pl.pallas_call(
        query_end_kernel,
        out_shape=tuple(outs),
        in_specs=[SCALARS] + [VMEM] * 6,
        out_specs=(VMEM,) * len(outs),
        scratch_shapes=scratch,
        compiler_params=pltpu.CompilerParams(vmem_limit_bytes=20 * 2**20),
        cost_estimate=pl.CostEstimate(
            flops=4 * tok * width * LEFT, bytes_accessed=6 * 2**20, transcendentals=0
        ),
    )(scalars(order), qmix, qbasis, cosine, sine, hidden, weights)


def key_end_kernel(
    order,
    kept_ref,
    came_ref,
    cos_ref,
    sin_ref,
    hidden_ref,
    weights_ref,
    part_ref,
    tokens_ref,
    inverse_ref,
    gains_ref,
    middle_ref,
    feed_gain_ref,
    out_ref,
    *outs
):
    cosine, sine = cos_ref[...], sin_ref[...]
    own = kept_ref[...] + came_ref[...].astype(F32)
    parts = []
    for r in range(RK):
        parts += unturn(own[KM + r * DH : KM + (r + 1) * DH], cosine, sine)
    tok, width = hidden_ref.shape
    parts += [own[2 * KM + KB :], own[:KM], own[KM + KB : 2 * KM + KB]]
    parts += [jnp.zeros((PACKED - GAINS, tok), F32)]
    slopes = jnp.concatenate(parts, 0).astype(BF)
    weights = weights_ref[...].reshape(width, PACKED)[:, LEFT:]
    slope = part_ref[...] + dims(slopes, weights, 0, 1)
    inverse = inverse_ref[...]
    normed = tokens_ref[...].astype(F32) * inverse
    scaled = slope * gains_ref[0:1, :]
    mean = jnp.mean(scaled * normed, -1, keepdims=True)
    out_ref[...] = middle_ref[...] + inverse * (scaled - normed * mean)
    gain_slope = jnp.sum(slope * normed, 0, keepdims=True)
    total = dims(hidden_ref[...], slopes, 0, 1)
    rows = jnp.concatenate(
        [gain_slope, feed_gain_ref[...], jnp.zeros((PACKED - GAINS - 2, width), F32)], 0
    )
    columns = jnp.concatenate([jnp.zeros((128 - rows.shape[0], width), F32), rows], 0).T
    total = jnp.concatenate([total[:, :-128], total[:, -128:] + columns], 1)
    if len(outs) == 1:
        outs[0][...] = total.astype(BF)
    else:
        emit(total, order, outs[2], outs[0], outs[1])


def key_end(order, *args):
    tok, width = args[4].shape
    outs = [jax.ShapeDtypeStruct((tok, width), F32)]
    scratch = []
    if len(order) > 1:
        out, held = blocks_out(order, width, PACKED - LEFT)
        outs += [out, out]
        scratch = [held]
    else:
        outs += [jax.ShapeDtypeStruct((width, PACKED - LEFT), BF)]
    return pl.pallas_call(
        key_end_kernel,
        out_shape=tuple(outs),
        in_specs=[SCALARS] + [VMEM] * len(args),
        out_specs=(VMEM,) * len(outs),
        scratch_shapes=scratch,
        compiler_params=pltpu.CompilerParams(vmem_limit_bytes=24 * 2**20),
        cost_estimate=pl.CostEstimate(
            flops=4 * tok * width * PACKED, bytes_accessed=6 * 2**20, transcendentals=0
        ),
    )(scalars(order), *args)


def key_parts(kv_ref, head, at):
    base = at + H * RK
    row = at + head * RK
    total = kv_ref[pl.ds(row, 1), :] * kv_ref[base : base + DH, :]
    total = total + kv_ref[pl.ds(row + 1, 1), :] * kv_ref[base + DH : base + 2 * DH, :]
    return (total * (1.0 / RK)).astype(BF)


def query_parts(qm_ref, qt_ref, head):
    total = qm_ref[pl.ds(head * RQ, 1), :] * qt_ref[0:DH, :]
    for r in range(1, RQ):
        total = total + qm_ref[pl.ds(head * RQ + r, 1), :] * qt_ref[r * DH : (r + 1) * DH, :]
    queries = (total * (1.0 / RQ)).astype(BF)
    return (queries.astype(F32) * DH**-0.5).astype(BF)


def attend_kernel(
    place_ref, qm_ref, qt_ref, k0, k1, k2, k3, attended_ref, probs_ref, kv_ref, bias
):
    pair = pl.program_id(0)
    tok, slots = bias.shape

    @pl.when(pair == 0)
    def _():
        for block, part in enumerate((k0, k1, k2, k3)):
            kv_ref[:, block * tok : (block + 1) * tok] = part[...].astype(F32)
        near, length = place_ref[0], place_ref[1]
        rows = near * tok + lax.broadcasted_iota(jnp.int32, (tok, tok), 0)
        for block, bit in enumerate((0, 2, 1, 3)):
            keys = (near ^ bit) * tok + lax.broadcasted_iota(jnp.int32, (tok, tok), 1)
            allowed = (keys <= rows) & (keys < length)
            bias[:, block * tok : (block + 1) * tok] = jnp.where(allowed, 0.0, NEG)

    outs = []
    for inner in range(PAIR):
        head = pair * PAIR + inner
        keys = key_parts(kv_ref, head, 0)
        values = key_parts(kv_ref, head, H * RK + RK * DH)
        queries = query_parts(qm_ref, qt_ref, head)
        scores = dims(queries, keys, 0, 0) + bias[...]
        peak = jnp.max(scores, -1, keepdims=True)
        powers = jnp.exp(scores - peak)
        total = jnp.sum(powers, -1, keepdims=True)
        probs = (powers * (1.0 / total)).astype(BF)
        probs_ref[inner] = probs
        outs.append(dims(probs, values, 1, 1))
    attended_ref[...] = jnp.concatenate(outs, 1).astype(BF)


def attend(places, query_mix, query_turned, factors):
    tok = query_mix.shape[1]
    slots = 4 * tok
    table = jax.ShapeDtypeStruct((factors[0].shape[0], slots), F32)
    return pl.pallas_call(
        attend_kernel,
        grid=(H // PAIR,),
        out_shape=(
            jax.ShapeDtypeStruct((tok, H * DH), BF),
            jax.ShapeDtypeStruct((H, tok, slots), BF),
            table,
        ),
        in_specs=[SCALARS, whole(query_mix), whole(query_turned)] + [whole(f) for f in factors],
        out_specs=(
            pl.BlockSpec((tok, PAIR * DH), lambda i: (0, i)),
            pl.BlockSpec((PAIR, tok, slots), lambda i: (i, 0, 0)),
            whole(table),
        ),
        scratch_shapes=[pltpu.VMEM((tok, slots), F32)],
        compiler_params=pltpu.CompilerParams(vmem_limit_bytes=24 * 2**20),
        cost_estimate=pl.CostEstimate(
            flops=16 * tok * slots * H * DH, bytes_accessed=2 * H * tok * slots, transcendentals=0
        ),
    )(places, query_mix, query_turned, *factors)


def attend_back_kernel(
    qm_ref,
    qt_ref,
    kv_ref,
    slope_ref,
    probs_ref,
    kept_ref,
    sent_ref,
    qmix_ref,
    qbasis_ref,
    mix_ref,
    basis_ref,
):
    pair = pl.program_id(0)
    vm = H * RK + RK * DH
    kb = RK * DH

    @pl.when(pair == 0)
    def _():
        basis_ref[...] = jnp.zeros_like(basis_ref)
        qbasis_ref[...] = jnp.zeros_like(qbasis_ref)

    for inner in range(PAIR):
        head = pair * PAIR + inner
        keys = key_parts(kv_ref, head, 0)
        values = key_parts(kv_ref, head, vm)
        queries = query_parts(qm_ref, qt_ref, head)
        slope = slope_ref[inner * DH : (inner + 1) * DH, :]
        probs_low = probs_ref[inner]
        slope_probs = dims(slope, values, 0, 0)
        probs = probs_low.astype(F32)
        weighted = probs * slope_probs
        total = jnp.sum(weighted, -1, keepdims=True)
        slope_scores = (weighted - probs * total).astype(BF)
        slope_query = dims(keys, slope_scores, 1, 1) * (DH**-0.5 / RQ)
        slope_key = dims(queries, slope_scores, 1, 0) * (1.0 / RK)
        slope_value = dims(slope, probs_low, 1, 0) * (1.0 / RK)
        for r in range(RK):
            row = head * RK + r
            for at, piece, side in ((0, slope_key, 0), (vm, slope_value, 1)):
                base = at + H * RK + r * DH
                here = side * RK + r
                basis_ref[here * DH : (here + 1) * DH, :] += kv_ref[pl.ds(at + row, 1), :] * piece
                mix_ref[pl.ds(side * H * RK + row, 1), :] = jnp.sum(
                    piece * kv_ref[base : base + DH, :], 0, keepdims=True
                )
        for r in range(RQ):
            row = head * RQ + r
            cut = slice(r * DH, (r + 1) * DH)
            qbasis_ref[cut, :] += qm_ref[pl.ds(row, 1), :] * slope_query
            qmix_ref[pl.ds(row, 1), :] = jnp.sum(slope_query * qt_ref[cut, :], 0, keepdims=True)

    @pl.when(pair == pl.num_programs(0) - 1)
    def _():
        half = kept_ref.shape[2] * 2
        tok = kept_ref.shape[2]
        km = H * RK
        for base, ref, first, rows in (
            (0, mix_ref, 0, km),
            (km, basis_ref, 0, kb),
            (vm, mix_ref, km, km),
            (vm + km, basis_ref, kb, kb),
        ):
            part = ref[first : first + rows, :]
            for block in range(2):
                kept_ref[block, base : base + rows, :] = part[:, block * tok : (block + 1) * tok]
            sent_ref[base : base + rows, :] = part[:, half:].astype(BF)


def attend_back(query_mix, query_turned, row_factors, slope_attended, probs):
    tok = query_mix.shape[1]
    rows, slots = row_factors.shape
    outs = (
        jax.ShapeDtypeStruct((2, rows, tok), F32),
        jax.ShapeDtypeStruct((rows, slots // 2), BF),
        jax.ShapeDtypeStruct((H * RQ, tok), F32),
        jax.ShapeDtypeStruct((RQ * DH, tok), F32),
    )
    return pl.pallas_call(
        attend_back_kernel,
        grid=(H // PAIR,),
        out_shape=outs,
        in_specs=[
            whole(query_mix),
            whole(query_turned),
            whole(row_factors),
            pl.BlockSpec((PAIR * DH, tok), lambda i: (i, 0)),
            pl.BlockSpec((PAIR, tok, slots), lambda i: (i, 0, 0)),
        ],
        out_specs=tuple(whole(o) for o in outs),
        scratch_shapes=[pltpu.VMEM((2 * H * RK, slots), F32), pltpu.VMEM((2 * RK * DH, slots), F32)],
        compiler_params=pltpu.CompilerParams(vmem_limit_bytes=24 * 2**20),
        cost_estimate=pl.CostEstimate(
            flops=32 * tok * slots * H * DH, bytes_accessed=2 * H * tok * slots, transcendentals=0
        ),
    )(query_mix, query_turned, row_factors, slope_attended, probs)


QB, KB, VB = RQ * DH, RK * DH, RK * DH
QM, KM, VM = H * RQ, H * RK, H * RK
LEFT = 512
GAINS = LEFT + KB + VB + KM + VM
PACKED = 896


def per_device(
    tokens,
    lengths,
    attend_gain,
    query_heads,
    query_basis,
    key_heads,
    key_basis,
    value_heads,
    value_basis,
    merge_weight,
    feed_gain,
    gate_weight,
    up_weight,
    down_weight,
    cotangent,
):
    tok, width = tokens.shape
    wide_count = lax.axis_size("wide")
    narrow_count = lax.axis_size("narrow")
    near = lax.axis_index("narrow")
    rows = gate_weight.shape[0]
    cut = down_weight.shape[0]
    hidden = cut * wide_count
    small = small_mesh()
    high, low = wide_place()
    rounds = wide_count // 2

    positions = (near * tok + jnp.arange(tok, dtype=jnp.int32)).astype(F32)
    frequency = jnp.power(10000.0, -2.0 * jnp.arange(DH // 2, dtype=F32) / DH)
    angles = frequency[:, None] * positions[None, :]
    cosine, sine = jnp.cos(angles), jnp.sin(angles)

    packed = jnp.concatenate(
        [
            query_basis,
            query_heads,
            jnp.zeros((rows, LEFT - QB - QM), BF),
            key_basis,
            value_basis,
            key_heads,
            value_heads,
            attend_gain[:, None],
            feed_gain[:, None],
            jnp.zeros((rows, PACKED - GAINS - 2), BF),
        ],
        1,
    )

    def columns(weight):
        parts = weight.reshape(rows, wide_count, narrow_count, cut).transpose(2, 0, 1, 3)
        return parts.reshape(narrow_count, rows, hidden)

    def exchange(gate, up):
        both = jnp.concatenate([columns(gate), columns(up)], 1)
        return lax.all_to_all(both, "narrow", 0, 0, tiled=True)

    if small:
        stage = jnp.concatenate(turned(packed[None]), 0)
        gate_up = after((gate_weight, up_weight), stage)
        stage = joined(stage, "narrow", 2)
        merge_own = after(merge_weight, stage)
        stage = joined(stage, "wide", 1)
        packed = [stage, flip(stage, "narrow", 1)]
        where = relative_blocks()
        both = exchange(*gate_up)
        pieces = turned(both[None])
        boths = pieces + [flip(piece, "wide", 1) for piece in pieces]
        both_where = [((high - k) % rounds) * 2 + low for k in range(rounds)] + [
            ((high - k) % rounds) * 2 + 1 - low for k in range(rounds)
        ]
        own = after(down_weight, stage)
        came = flip(own, "wide", 1)
        pair = jnp.where(low == 0, jnp.stack([own, came]), jnp.stack([came, own]))
        downs = turned(pair.reshape(1, 2 * cut, width))
        down_where = [(high - k) % rounds for k in range(rounds)]
        merge_stage = jnp.concatenate(turned(merge_own[None]), 0)
        merge_stage = joined(merge_stage, "narrow", 2)
        merge_stage = joined(merge_stage, "wide", 1)
        merge_stacks = [merge_stage, flip(merge_stage, "narrow", 1)]
    else:
        both_axes = ("wide", "narrow")
        packed = [lax.all_gather(packed, both_axes, axis=0, tiled=True)[None]]
        merge_stacks = [lax.all_gather(merge_weight, both_axes, axis=0, tiled=True)[None]]
        where = [0]
        both = lax.all_gather(exchange(gate_weight, up_weight), "wide", axis=0, tiled=False)
        both = both.reshape(-1, 2, rows, hidden).transpose(1, 0, 2, 3)
        both = both.reshape(2, 8, 4, width // 32, hidden).transpose(1, 2, 0, 3, 4)
        boths, both_where = [both.reshape(8, 4, width // 16, hidden)], list(range(8))
        downs = [lax.all_gather(down_weight, "wide", axis=0, tiled=True)[None]]
        down_where = [0]

    hidden_one, inverse_one, gains, weights, query_mix, query_turned, own_factors = project(
        tokens, cosine, sine, packed, where
    )
    gain_second = gains[1:2]
    places = jnp.stack([near.astype(jnp.int32), lengths[0].astype(jnp.int32)])
    factors = gather_narrow(own_factors)
    cots = gather_narrow(after(cotangent, factors[3]))
    attended, probs, row_factors = attend(places, query_mix, query_turned, factors)
    merge_full = put_in_order(merge_stacks, where)
    source = tokens.astype(F32)
    middle = source + dims(attended, merge_full, 1, 0)
    inverse_two = lax.rsqrt(jnp.mean(middle * middle, -1, keepdims=True) + EPS)
    normed_two = middle * inverse_two
    hidden_two = (normed_two * gain_second).astype(BF)

    pieces = gather_narrow(hidden_two)
    hidden_feed, slope_gate, slope_up, kept, sent = feed(
        pieces, cots, boths, both_where, downs, down_where
    )
    pair = kept + flip(sent, "narrow", 1).astype(F32)
    for_far = pair[1].astype(BF)
    slope_normed_two = pair[0] + flip(for_far, "narrow", 2).astype(F32)
    hidden_feed, slope_gate, slope_up = after((hidden_feed, slope_gate, slope_up), for_far)
    if small:
        turns = [(high + k) % rounds for k in range(rounds)]
        to_send = slopes_of(pieces, slope_gate, slope_up, [2 * t + 1 - low for t in turns])
        down_full = down_slopes(after(hidden_feed, to_send[0]), cots)
        down_blocks = down_full.reshape(rounds, 2, cut, width)
        down_send = pick(down_blocks, 1 - low, 1)
        gate_low, up_low = after((slope_gate, slope_up), down_send)
        to_keep = slopes_of(pieces, gate_low, up_low, [2 * t + low for t in turns])
        came = [flip(away, "wide", 1) for away in to_send]
        down_came = flip(down_send, "wide", 1)
    fed_kept, fed_sent = feed_out(hidden_feed, downs, down_where)
    output = (middle + scatter_narrow(fed_kept, fed_sent)).astype(BF)

    slope_middle = cotangent.astype(F32) + norm_back(
        slope_normed_two, normed_two, inverse_two, gain_second
    )
    feed_gain_slope = jnp.sum(slope_normed_two * normed_two, 0, keepdims=True)
    slope_low = slope_middle.astype(BF)
    slope_attended = dims(merge_full, slope_low, 1, 1).astype(BF)
    order = scatter_order() if small else [0]
    if small:
        merge_sent, merge_kept = outer_blocks(order, attended, slope_low)
        merge_sum = add_low(merge_kept, flip(merge_sent, "narrow", 1))
    key_kept, key_sent, query_mix_slope, query_basis_slope = attend_back(
        query_mix, query_turned, row_factors, slope_attended, probs
    )
    key_pair = key_kept + flip(key_sent, "narrow", 1).reshape(-1, 2, tok).transpose(1, 0, 2).astype(F32)
    key_far = key_pair[1].astype(BF)
    key_came = flip(key_far, "narrow", 2)
    query_basis_slope = after(query_basis_slope, key_far)
    query_outs = query_end(
        order, query_mix_slope, query_basis_slope, cosine, sine, hidden_one, weights
    )
    key_outs = key_end(
        order,
        key_pair[0],
        key_came,
        cosine,
        sine,
        hidden_one,
        weights,
        query_outs[0],
        tokens,
        inverse_one,
        gains,
        slope_middle,
        feed_gain_slope,
    )
    tokens_slope = key_outs[0]
    if small:
        merge_slope = spread_stages(merge_sum)
        query_slopes = spread_stages(add_low(query_outs[2], flip(query_outs[1], "narrow", 1)))
        key_slopes = spread_stages(add_low(key_outs[2], flip(key_outs[1], "narrow", 1)))
        gate_half, up_half = (add_low(a, b) for a, b in zip(to_keep, came))
        gate_slope, up_slope = (
            spread_high([half[k] for k in range(rounds)]).T for half in (gate_half, up_half)
        )
        down_half = add_low(pick(down_blocks, low, 1), down_came)
        down_slope = spread_high(ring_blocks(down_half))
    else:
        merge_slope = scatter_all(dims(attended, slope_low, 0, 0).astype(BF))
        query_slopes = scatter_all(query_outs[1])
        key_slopes = scatter_all(key_outs[1])
        full = slopes_of(pieces, slope_gate, slope_up, list(range(width // 128)))
        gate_slope, up_slope = (
            scatter_wide(s.transpose(0, 2, 1).reshape(width, hidden)) for s in full
        )
        down_slope = scatter_wide(down_slopes(hidden_feed, cots))

    slopes = jnp.concatenate(
        [
            gate_slope.reshape(narrow_count, rows, hidden),
            up_slope.reshape(narrow_count, rows, hidden),
        ],
        1,
    ).astype(BF)
    slopes = lax.all_to_all(slopes, "narrow", 0, 0, tiled=True)
    slopes = slopes.reshape(narrow_count, 2, rows, wide_count, cut).transpose(1, 2, 3, 0, 4)
    slopes = slopes.reshape(2, rows, hidden * narrow_count).astype(F32)

    base = GAINS - LEFT
    return (
        output,
        tokens_slope,
        key_slopes[:, base],
        query_slopes[:, QB : QB + QM],
        query_slopes[:, :QB],
        key_slopes[:, KB + VB : KB + VB + KM],
        key_slopes[:, :KB],
        key_slopes[:, KB + VB + KM : KB + VB + KM + VM],
        key_slopes[:, KB : KB + VB],
        merge_slope,
        key_slopes[:, base + 1],
        slopes[0],
        slopes[1],
        down_slope,
    )


def solution(mesh):
    both = ("wide", "narrow")
    row, vector = P(both, None), P(both)
    return jax.shard_map(
        per_device,
        mesh=mesh,
        in_specs=(row, P("wide"), vector) + (row,) * 7 + (vector,) + (row,) * 4,
        out_specs=(row, row, vector) + (row,) * 7 + (vector,) + (row,) * 3,
        check_vma=False,
    )
```

```python
import functools

import jax
import jax.numpy as jnp
from jax import lax
from jax.experimental import pallas as pl
from jax.experimental.pallas import tpu as pltpu
from jax.sharding import PartitionSpec as P

H = 16
DH = 64
RQ = 6
RK = 2
PAIR = 2
EPS = 1e-06
NEG = -1e30
BF = jnp.bfloat16
F32 = jnp.float32


def dims(left, right, left_dim, right_dim):
    return lax.dot_general(
        left, right, (((left_dim,), (right_dim,)), ((), ())), preferred_element_type=F32
    )


def flip(value, axis, bit):
    size = lax.axis_size(axis)
    return lax.ppermute(value, axis, [(i, i ^ bit) for i in range(size)])


def turn(value, steps):
    size = lax.axis_size("wide")
    return lax.ppermute(value, "wide", [(i, (i + 2 * steps) % size) for i in range(size)])


def small_mesh():
    return lax.axis_size("wide") == 8 and lax.axis_size("narrow") == 4


def wide_place():
    me = lax.axis_index("wide")
    return me // 2, me % 2


def tie(*values):
    return lax.optimization_barrier(values)


def after(value, *others):
    return lax.optimization_barrier((value, others))[0]


def ring_groups():
    size = lax.axis_size("wide")
    return [list(range(x, size, 2)) for x in range(2)]


def ring_all_to_all(value):
    return lax.all_to_all(value, "wide", 0, 0, axis_index_groups=ring_groups(), tiled=True)


def spread_high(blocks):
    return jnp.sum(ring_all_to_all(blocks).astype(F32), 0)


def scatter_wide(value):
    return lax.psum_scatter(value, "wide", scatter_dimension=0, tiled=True).astype(F32)


def turned(value):
    rounds = lax.axis_size("wide") // 2
    return [value] + [turn(value, k) for k in range(1, rounds)]


def joined(value, axis, bit):
    return jnp.concatenate([value, flip(value, axis, bit)], 0)


def relative_blocks(swapped=False):
    high, low = wide_place()
    rounds = lax.axis_size("wide") // 2
    near = lax.axis_index("narrow")
    return [
        (((high - k) % rounds) * 2 + (low ^ x)) * 4 + (near ^ (2 * y) ^ c)
        for c in (0, 1)
        for x, y in ([(0, 0), (1, 0), (0, 1), (1, 1)] if swapped else [(0, 0), (0, 1), (1, 0), (1, 1)])
        for k in range(rounds)
    ]


def scatter_all(value):
    return lax.psum_scatter(value, ("wide", "narrow"), scatter_dimension=0, tiled=True).astype(F32)


def scatter_order(turning):
    high, low = wide_place()
    rounds = lax.axis_size("wide") // 2
    near = lax.axis_index("narrow")
    return [
        (((high + k) % rounds if turning else k) * 2 + (low ^ x)) * 4 + (near ^ (2 * y) ^ c)
        for c in (0, 1)
        for y in (0, 1)
        for x in (0, 1)
        for k in range(rounds)
    ]


def spread_turns(blocks):
    total = blocks[0].astype(F32)
    for k in range(1, blocks.shape[0]):
        total = total + turn(blocks[k], k).astype(F32)
    return total


def add_low(kept, came):
    return (kept.astype(F32) + came.astype(F32)).astype(BF)


def gather_narrow(value):
    far = flip(value, "narrow", 2)
    return [value, far, flip(value, "narrow", 1), flip(far, "narrow", 1)]


def starts(stacks, where_ref, first, target, sem):
    copies = []
    for stack in stacks:
        for k in range(stack.shape[0]):
            at = len(copies)
            copies.append(
                pltpu.make_async_copy(
                    stack.at[k], target.at[where_ref[first + at]], sem.at[first + at]
                )
            )
            copies[-1].start()
    return copies


def count(stacks):
    return sum(stack.shape[0] for stack in stacks)


def whole(array):
    return pl.BlockSpec(array.shape, lambda *i: (0,) * len(array.shape))


ANYWHERE = pl.BlockSpec(memory_space=pl.ANY)


def pinned(*arrays):
    return [pltpu.with_memory_space_constraint(a, pltpu.HBM) for a in arrays]


SCALARS = pl.BlockSpec(memory_space=pltpu.SMEM)
SMALL = pl.CostEstimate(flops=3 * 10**9, bytes_accessed=2**22, transcendentals=0)


def scalars(*lists):
    return jnp.stack([jnp.asarray(v, jnp.int32) for one in lists for v in one])


def project_kernel(n, where, tokens_ref, cos_ref, sin_ref, *refs):
    packed, refs = refs[:n], refs[n:]
    hidden_ref, inverse_ref, gains_ref, packed_ref, qm_ref, qt_ref, kv_ref, sem = refs
    copies = starts(packed, where, 0, packed_ref, sem)
    source = tokens_ref[...].astype(F32)
    inverse = lax.rsqrt(jnp.mean(source * source, -1, keepdims=True) + EPS)
    inverse_ref[...] = inverse
    normed = source * inverse
    for copy in copies:
        copy.wait()
    width = source.shape[1]
    weights = packed_ref[...].reshape(width, PACKED)
    gains = weights[:, PACKED - 128 :].astype(F32).T
    at = GAINS - (PACKED - 128)
    gains_ref[...] = gains[at : at + 8]
    hidden = (normed * gains[at : at + 1]).astype(BF)
    hidden_ref[...] = hidden
    factors = dims(hidden, weights, 1, 0).T
    cosine, sine = cos_ref[...], sin_ref[...]
    half = DH // 2
    for r in range(RQ + RK):
        base = r * DH if r < RQ else LEFT + (r - RQ) * DH
        one = factors[base : base + half]
        two = factors[base + half : base + DH]
        a, b = one * cosine - two * sine, one * sine + two * cosine
        if r < RQ:
            qt_ref[base : base + half, :] = a
            qt_ref[base + half : base + DH, :] = b
        else:
            row = KM + (r - RQ) * DH
            kv_ref[row : row + half, :] = a.astype(BF)
            kv_ref[row + half : row + DH, :] = b.astype(BF)
    qm_ref[...] = factors[QB : QB + QM]
    base = LEFT + KB
    kv_ref[2 * KM + KB :, :] = factors[base : base + VB].astype(BF)
    base += VB
    kv_ref[0:KM, :] = factors[base : base + KM].astype(BF)
    kv_ref[KM + KB : 2 * KM + KB, :] = factors[base + KM : base + 2 * KM].astype(BF)


VMEM = pl.BlockSpec(memory_space=pltpu.VMEM)


def project(tokens, cosine, sine, packed, where):
    tok, width = tokens.shape
    outs = (
        jax.ShapeDtypeStruct((tok, width), BF),
        jax.ShapeDtypeStruct((tok, 1), F32),
        jax.ShapeDtypeStruct((8, width), F32),
        jax.ShapeDtypeStruct((count(packed),) + packed[0].shape[1:], BF),
        jax.ShapeDtypeStruct((QM, tok), F32),
        jax.ShapeDtypeStruct((QB, tok), F32),
        jax.ShapeDtypeStruct((2 * (KM + KB), tok), BF),
    )
    return pl.pallas_call(
        functools.partial(project_kernel, len(packed)),
        out_shape=outs,
        in_specs=[SCALARS] + [VMEM] * 3 + [ANYWHERE] * len(packed),
        out_specs=tuple(VMEM for _ in outs),
        scratch_shapes=[pltpu.SemaphoreType.DMA((count(packed),))],
        compiler_params=pltpu.CompilerParams(vmem_limit_bytes=14 * 2**20),
        cost_estimate=SMALL,
    )(scalars(where), tokens, cosine, sine, *packed)


def halves_of(both_ref, width, hidden):
    rows = both_ref.shape[2] // 2
    return (
        both_ref[:, :, :rows, :].reshape(width, hidden),
        both_ref[:, :, rows:, :].reshape(width, hidden),
    )


def feed_kernel(nb, nd, where, *refs):
    pieces, refs = refs[:2], refs[2:]
    cots, refs = refs[:2], refs[2:]
    boths, refs = refs[:nb], refs[nb:]
    downs, refs = refs[:nd], refs[nd:]
    hf_out, sg_out, su_out, kept_ref, sent_ref, hid, cot, wgu, wd, held, sem, psem, osem = refs
    outgoing = []
    width, hidden = hid.shape[2], wgu.shape[3]
    loads = [
        [
            pltpu.make_async_copy(pieces[b], hid.at[b], psem.at[b]),
            pltpu.make_async_copy(cots[b], cot.at[b], psem.at[2 + b]),
        ]
        for b in range(2)
    ]
    loads[0][0].start()
    in_both = starts(boths, where, 0, wgu, sem)
    loads[0][1].start()
    in_down = starts(downs, where, count(boths), wd, sem)
    for copy in loads[1]:
        copy.start()
    for b in range(2):
        loads[b][0].wait()
        if b == 0:
            for copy in in_both:
                copy.wait()
        gate_all, up_all = halves_of(wgu, width, hidden)
        gate = dims(hid[b], gate_all, 1, 0)
        upward = dims(hid[b], up_all, 1, 0)
        loads[b][1].wait()
        if b == 0:
            for copy in in_down:
                copy.wait()
        down_all = wd[...].reshape(hidden, width)
        slope = dims(cot[b], down_all, 1, 1)
        sig = jax.nn.sigmoid(gate)
        silu = gate * sig
        held[0, b] = (silu * upward).astype(BF)
        slope_up = (slope * silu).astype(BF)
        slope_gate = (slope * upward * sig * (1.0 + gate * (1.0 - sig))).astype(BF)
        held[1, b] = slope_gate
        held[2, b] = slope_up
        for k, out in enumerate((hf_out, sg_out, su_out)):
            outgoing.append(pltpu.make_async_copy(held.at[k, b], out.at[b], osem.at[k, b]))
            outgoing[-1].start()
        back = dims(slope_gate, gate_all, 1, 1) + dims(slope_up, up_all, 1, 1)
        if b == 0:
            kept_ref[...] = back
        else:
            sent_ref[...] = back.astype(BF)
    for copy in outgoing:
        copy.wait()


def feed(pieces, cots, boths, both_where, downs, down_where):
    tok, width = pieces[0].shape
    hidden = boths[0].shape[3]
    low = pltpu.HBM((2, tok, hidden), BF)
    outs = (
        low,
        low,
        low,
        jax.ShapeDtypeStruct((tok, width), F32),
        jax.ShapeDtypeStruct((tok, width), BF),
    )
    blocks = lambda stacks: pltpu.VMEM((count(stacks),) + stacks[0].shape[1:], BF)
    total = count(boths) + count(downs)
    return pl.pallas_call(
        functools.partial(feed_kernel, len(boths), len(downs)),
        out_shape=outs,
        in_specs=[SCALARS] + [ANYWHERE] * (4 + len(boths) + len(downs)),
        out_specs=(ANYWHERE,) * 3 + (VMEM,) * 2,
        scratch_shapes=[
            pltpu.VMEM((2, tok, width), BF),
            pltpu.VMEM((2, tok, width), BF),
            blocks(boths),
            blocks(downs),
            pltpu.VMEM((3, 2, tok, hidden), BF),
            pltpu.SemaphoreType.DMA((total,)),
            pltpu.SemaphoreType.DMA((4,)),
            pltpu.SemaphoreType.DMA((3, 2)),
        ],
        compiler_params=pltpu.CompilerParams(vmem_limit_bytes=20 * 2**20),
        cost_estimate=SMALL,
    )(scalars(both_where, down_where), *pinned(*pieces, *cots, *boths, *downs))


def bring(sources, target, sem):
    copies = []
    at = 0
    for source in sources:
        parts = [source] if len(source.shape) == 2 else [source.at[k] for k in range(source.shape[0])]
        for part in parts:
            copies.append(pltpu.make_async_copy(part, target.at[at], sem.at[at]))
            copies[-1].start()
            at += 1
    return copies


def slopes_kernel(blocks, order, *refs):
    out_g, out_u, hid, gates, ups, hsem, gsem, usem = refs[8:]
    copies = bring(refs[:4], hid, hsem) + bring(refs[4:6], gates, gsem)
    later = bring(refs[6:8], ups, usem)
    for copy in copies:
        copy.wait()
    rows = out_g.shape[2]
    hidden = out_g.shape[1]
    columns = []
    for k in range(blocks):
        at = pl.multiple_of(order[k] * rows, 128)
        columns.append(hid[:, :, pl.ds(at, rows)].reshape(-1, rows))
    chosen = jnp.concatenate(columns, 1)
    for side, (held, out) in enumerate(((gates, out_g), (ups, out_u))):
        if side == 1:
            for copy in later:
                copy.wait()
        result = dims(held[...].reshape(-1, hidden), chosen, 0, 0).astype(BF)
        for k in range(blocks):
            out[k] = result[:, k * rows : (k + 1) * rows]


def slopes_of(pieces, slope_gate, slope_up, order):
    tok, width = pieces[0].shape
    hidden = slope_gate[0].shape[2]
    rows = 128
    return pl.pallas_call(
        functools.partial(slopes_kernel, len(order)),
        out_shape=(jax.ShapeDtypeStruct((len(order), hidden, rows), BF),) * 2,
        in_specs=[SCALARS] + [ANYWHERE] * 8,
        out_specs=(VMEM, VMEM),
        scratch_shapes=[
            pltpu.VMEM((4, tok, width), BF),
            pltpu.VMEM((4, tok, hidden), BF),
            pltpu.VMEM((4, tok, hidden), BF),
        ]
        + [pltpu.SemaphoreType.DMA((4,))] * 3,
        compiler_params=pltpu.CompilerParams(vmem_limit_bytes=18 * 2**20),
        cost_estimate=SMALL,
    )(scalars(order), *pinned(*pieces, *slope_gate, *slope_up))


def down_kernel(blocks, order, *refs):
    feeds, cots, fsem, csem = refs[-4:]
    for copy in bring(refs[:2], feeds, fsem) + bring(refs[2:6], cots, csem):
        copy.wait()
    outs = refs[6:-4]
    hidden, width = feeds.shape[2], cots.shape[2]
    total = dims(feeds[...].reshape(-1, hidden), cots[...].reshape(-1, width), 0, 0)
    if blocks == 1:
        outs[0][...] = total.astype(BF)
    else:
        sent_ref, kept_ref, held = outs
        held[...] = total.reshape(held.shape)
        for k in range(blocks // 2):
            kept_ref[k] = held[order[2 * k]].astype(BF)
            sent_ref[k] = held[order[2 * k + 1]].astype(BF)


def down_slopes(hidden_feed, cots, order, cut):
    tok, width = cots[0].shape
    hidden = hidden_feed[0].shape[2]
    if len(order) > 1:
        out = jax.ShapeDtypeStruct((len(order) // 2, cut, width), BF)
        outs, scratch = (out, out), [pltpu.VMEM((len(order), cut, width), F32)]
    else:
        outs, scratch = (jax.ShapeDtypeStruct((hidden, width), BF),), []
    return pl.pallas_call(
        functools.partial(down_kernel, len(order)),
        out_shape=outs,
        in_specs=[SCALARS] + [ANYWHERE] * 6,
        out_specs=(VMEM,) * len(outs),
        scratch_shapes=scratch
        + [
            pltpu.VMEM((4, tok, hidden), BF),
            pltpu.VMEM((4, tok, width), BF),
            pltpu.SemaphoreType.DMA((4,)),
            pltpu.SemaphoreType.DMA((4,)),
        ],
        compiler_params=pltpu.CompilerParams(vmem_limit_bytes=20 * 2**20),
        cost_estimate=SMALL,
    )(scalars(order), *pinned(*hidden_feed, *cots))


def feed_out_kernel(nd, where, *refs):
    downs, (f0, f1, kept_ref, sent_ref, wd, feeds, sem, fsem) = refs[:nd], refs[nd:]
    for copy in starts(downs, where, 0, wd, sem) + bring((f0, f1), feeds, fsem):
        copy.wait()
    down_all = wd[...].reshape(feeds.shape[2], wd.shape[2])
    for part in range(2):
        kept_ref[part] = dims(feeds[2 * part], down_all, 1, 0)
        sent_ref[part] = dims(feeds[2 * part + 1], down_all, 1, 0).astype(BF)


def feed_out(hidden_feed, downs, down_where):
    tok, hidden = hidden_feed[0].shape[1:]
    width = downs[0].shape[2]
    return pl.pallas_call(
        functools.partial(feed_out_kernel, len(downs)),
        out_shape=(
            jax.ShapeDtypeStruct((2, tok, width), F32),
            jax.ShapeDtypeStruct((2, tok, width), BF),
        ),
        in_specs=[SCALARS] + [ANYWHERE] * (len(downs) + 2),
        out_specs=(VMEM, VMEM),
        scratch_shapes=[
            pltpu.VMEM((count(downs),) + downs[0].shape[1:], BF),
            pltpu.VMEM((4, tok, hidden), BF),
            pltpu.SemaphoreType.DMA((count(downs),)),
            pltpu.SemaphoreType.DMA((4,)),
        ],
        compiler_params=pltpu.CompilerParams(vmem_limit_bytes=14 * 2**20),
        cost_estimate=SMALL,
    )(scalars(down_where), *pinned(*downs, *hidden_feed))


def finish_kernel(gate_ref, up_ref, out_ref):
    rows = out_ref.shape[1] // 2
    for side, ref in enumerate((gate_ref, up_ref)):
        total = ref[0].astype(F32) + ref[1].astype(F32)
        for k in range(2, ref.shape[0]):
            total = total + ref[k].astype(F32)
        total = total.T.astype(BF)
        for n in range(out_ref.shape[0]):
            out_ref[n, side * rows : (side + 1) * rows, :] = total[n * rows : (n + 1) * rows]


def finish(gate, up, group):
    _, hidden, rows = gate.shape
    return pl.pallas_call(
        finish_kernel,
        out_shape=jax.ShapeDtypeStruct((group, 2 * rows // group, hidden), BF),
        in_specs=[VMEM, VMEM],
        out_specs=VMEM,
        compiler_params=pltpu.CompilerParams(vmem_limit_bytes=8 * 2**20),
        cost_estimate=SMALL,
    )(gate, up)


def unmix_kernel(cut, x_ref, gate_ref, up_ref):
    group, rows, hidden = x_ref.shape
    rows //= 2
    for side, ref in ((0, gate_ref), (1, up_ref)):
        parts = [x_ref[n, side * rows : (side + 1) * rows, :].astype(F32) for n in range(group)]
        ref[...] = jnp.concatenate(
            [part[:, w * cut : (w + 1) * cut] for w in range(hidden // cut) for part in parts], 1
        )


def unmix(value, cut):
    group, rows, hidden = value.shape
    out = jax.ShapeDtypeStruct((rows // 2, group * hidden), F32)
    return pl.pallas_call(
        functools.partial(unmix_kernel, cut),
        out_shape=(out, out),
        in_specs=[VMEM],
        out_specs=(VMEM, VMEM),
        compiler_params=pltpu.CompilerParams(vmem_limit_bytes=8 * 2**20),
        cost_estimate=SMALL,
    )(value)


def middle_kernel(n, where, attended_ref, tokens_ref, gains_ref, *refs):
    stacks, (hidden_ref, middle_ref, inverse_ref, merge, sem) = refs[:n], refs[n:]
    for copy in starts(stacks, where, 0, merge, sem):
        copy.wait()
    width = tokens_ref.shape[1]
    full = merge[...].reshape(attended_ref.shape[1], width)
    middle = tokens_ref[...].astype(F32) + dims(attended_ref[...], full, 1, 0)
    inverse = lax.rsqrt(jnp.mean(middle * middle, -1, keepdims=True) + EPS)
    middle_ref[...] = middle
    inverse_ref[...] = inverse
    hidden_ref[...] = (middle * inverse * gains_ref[1:2, :]).astype(BF)


def middle_of(attended, tokens, gains, stacks, where):
    tok, width = tokens.shape
    outs = (
        jax.ShapeDtypeStruct((tok, width), BF),
        jax.ShapeDtypeStruct((tok, width), F32),
        jax.ShapeDtypeStruct((tok, 1), F32),
    )
    return pl.pallas_call(
        functools.partial(middle_kernel, len(stacks)),
        out_shape=outs,
        in_specs=[SCALARS] + [VMEM] * 3 + [ANYWHERE] * len(stacks),
        out_specs=(VMEM,) * 3,
        scratch_shapes=[
            pltpu.VMEM((count(stacks),) + stacks[0].shape[1:], BF),
            pltpu.SemaphoreType.DMA((count(stacks),)),
        ],
        compiler_params=pltpu.CompilerParams(vmem_limit_bytes=10 * 2**20),
        cost_estimate=SMALL,
    )(scalars(where), attended, tokens, gains, *stacks)


def turn_back_kernel(
    n, where, kept_ref, near_ref, far_ref, middle_ref, inverse_ref, gains_ref, cot_ref, *refs
):
    stacks, (slope_ref, low_ref, attended_ref, gain_ref, merge, sem) = refs[:n], refs[n:]
    copies = starts(stacks, where, 0, merge, sem)
    slope = kept_ref[...] + near_ref[...].astype(F32) + far_ref[...].astype(F32)
    inverse = inverse_ref[...]
    normed = middle_ref[...] * inverse
    gain_ref[...] = jnp.sum(slope * normed, 0, keepdims=True)
    scaled = slope * gains_ref[1:2, :]
    mean = jnp.mean(scaled * normed, -1, keepdims=True)
    slope_middle = cot_ref[...].astype(F32) + inverse * (scaled - normed * mean)
    slope_ref[...] = slope_middle
    low = slope_middle.astype(BF)
    low_ref[...] = low
    for copy in copies:
        copy.wait()
    full = merge[...].reshape(attended_ref.shape[0], low.shape[1])
    attended_ref[...] = dims(full, low, 1, 1).astype(BF)


def turn_back(kept, came_near, came_far, middle, inverse, gains, cotangent, stacks, where):
    tok, width = middle.shape
    outs = (
        jax.ShapeDtypeStruct((tok, width), F32),
        jax.ShapeDtypeStruct((tok, width), BF),
        jax.ShapeDtypeStruct((width, tok), BF),
        jax.ShapeDtypeStruct((1, width), F32),
    )
    return pl.pallas_call(
        functools.partial(turn_back_kernel, len(stacks)),
        out_shape=outs,
        in_specs=[SCALARS] + [VMEM] * 7 + [ANYWHERE] * len(stacks),
        out_specs=(VMEM,) * 4,
        scratch_shapes=[
            pltpu.VMEM((count(stacks),) + stacks[0].shape[1:], BF),
            pltpu.SemaphoreType.DMA((count(stacks),)),
        ],
        compiler_params=pltpu.CompilerParams(vmem_limit_bytes=12 * 2**20),
        cost_estimate=SMALL,
    )(
        scalars(where), kept, came_near, came_far, middle, inverse, gains, cotangent, *stacks
    )


def emit(total, order, held, sent_ref, kept_ref):
    held[...] = total.reshape(held.shape)
    half = sent_ref.shape[0]
    first = sent_ref.shape[2] - total.shape[1]
    for k in range(half):
        kept_ref[k, :, first:] = held[order[k]].astype(BF)
        sent_ref[k, :, first:] = held[order[half + k]].astype(BF)


def outer_kernel(order, left_ref, right_ref, sent_ref, kept_ref, held):
    emit(dims(left_ref[...], right_ref[...], 0, 0), order, held, sent_ref, kept_ref)


def blocks_out(order, width, columns):
    half = len(order) // 2
    rows = width // len(order)
    out = jax.ShapeDtypeStruct((half, rows, columns), BF)
    return out, pltpu.VMEM((len(order), rows, columns), F32)


def outer_blocks(order, left, right):
    tok, width = left.shape
    columns = right.shape[1]
    out, held = blocks_out(order, width, columns)
    return pl.pallas_call(
        outer_kernel,
        out_shape=(out, out),
        in_specs=[SCALARS, VMEM, VMEM],
        out_specs=(VMEM, VMEM),
        scratch_shapes=[held],
        compiler_params=pltpu.CompilerParams(vmem_limit_bytes=10 * 2**20),
        cost_estimate=SMALL,
    )(scalars(order), left, right)


def unturn(value, cosine, sine):
    half = DH // 2
    one, two = value[:half], value[half:]
    return [one * cosine + two * sine, two * cosine - one * sine]


def query_end_kernel(
    order, qmix_ref, qbasis_ref, cos_ref, sin_ref, hidden_ref, weights_ref, *refs
):
    part_ref, outs = refs[0], refs[1:]
    cosine, sine = cos_ref[...], sin_ref[...]
    parts = []
    for r in range(RQ):
        parts += unturn(qbasis_ref[r * DH : (r + 1) * DH, :], cosine, sine)
    tok = cosine.shape[1]
    parts += [qmix_ref[...], jnp.zeros((LEFT - QB - QM, tok), F32)]
    slopes = jnp.concatenate(parts, 0).astype(BF)
    weights = weights_ref[...].reshape(hidden_ref.shape[1], PACKED)[:, :LEFT]
    part_ref[...] = dims(slopes, weights, 0, 1)
    total = dims(hidden_ref[...], slopes, 0, 1)
    if len(outs) == 1:
        outs[0][...] = total.astype(BF)
    else:
        emit(total, order, outs[2], outs[0], outs[1])


def query_end(order, qmix, qbasis, cosine, sine, hidden, weights):
    tok, width = hidden.shape
    outs = [jax.ShapeDtypeStruct((tok, width), F32)]
    scratch = []
    if len(order) > 1:
        out, held = blocks_out(order, width, LEFT)
        outs += [out, out]
        scratch = [held]
    else:
        outs += [jax.ShapeDtypeStruct((width, LEFT), BF)]
    return pl.pallas_call(
        query_end_kernel,
        out_shape=tuple(outs),
        in_specs=[SCALARS] + [VMEM] * 6,
        out_specs=(VMEM,) * len(outs),
        scratch_shapes=scratch,
        compiler_params=pltpu.CompilerParams(vmem_limit_bytes=12 * 2**20),
        cost_estimate=SMALL,
    )(scalars(order), qmix, qbasis, cosine, sine, hidden, weights)


def key_end_kernel(
    order,
    kept_ref,
    came_ref,
    cos_ref,
    sin_ref,
    hidden_ref,
    weights_ref,
    part_ref,
    tokens_ref,
    inverse_ref,
    gains_ref,
    middle_ref,
    feed_gain_ref,
    *refs
):
    if order.shape[0] > 1:
        query_sent, query_kept, out_ref, away_ref, stay_ref, held = refs
        away_ref[:, :, :LEFT] = query_sent[...]
        stay_ref[:, :, :LEFT] = query_kept[...]
    else:
        out_ref, total_ref = refs
    cosine, sine = cos_ref[...], sin_ref[...]
    own = kept_ref[...] + came_ref[...].astype(F32)
    parts = []
    for r in range(RK):
        parts += unturn(own[KM + r * DH : KM + (r + 1) * DH], cosine, sine)
    tok, width = hidden_ref.shape
    parts += [own[2 * KM + KB :], own[:KM], own[KM + KB : 2 * KM + KB]]
    parts += [jnp.zeros((PACKED - GAINS, tok), F32)]
    slopes = jnp.concatenate(parts, 0).astype(BF)
    weights = weights_ref[...].reshape(width, PACKED)[:, LEFT:]
    slope = part_ref[...] + dims(slopes, weights, 0, 1)
    inverse = inverse_ref[...]
    normed = tokens_ref[...].astype(F32) * inverse
    scaled = slope * gains_ref[0:1, :]
    mean = jnp.mean(scaled * normed, -1, keepdims=True)
    out_ref[...] = middle_ref[...] + inverse * (scaled - normed * mean)
    gain_slope = jnp.sum(slope * normed, 0, keepdims=True)
    total = dims(hidden_ref[...], slopes, 0, 1)
    rows = jnp.concatenate(
        [gain_slope, feed_gain_ref[...], jnp.zeros((PACKED - GAINS - 2, width), F32)], 0
    )
    columns = jnp.concatenate([jnp.zeros((128 - rows.shape[0], width), F32), rows], 0).T
    total = jnp.concatenate([total[:, :-128], total[:, -128:] + columns], 1)
    if order.shape[0] > 1:
        emit(total, order, held, away_ref, stay_ref)
    else:
        total_ref[...] = total.astype(BF)


def key_end(order, *args):
    tok, width = args[4].shape
    outs = [jax.ShapeDtypeStruct((tok, width), F32)]
    scratch = []
    if len(order) > 1:
        _, held = blocks_out(order, width, PACKED - LEFT)
        out, _ = blocks_out(order, width, PACKED)
        outs += [out, out]
        scratch = [held]
    else:
        outs += [jax.ShapeDtypeStruct((width, PACKED - LEFT), BF)]
    return pl.pallas_call(
        key_end_kernel,
        out_shape=tuple(outs),
        in_specs=[SCALARS] + [VMEM] * len(args),
        out_specs=(VMEM,) * len(outs),
        scratch_shapes=scratch,
        compiler_params=pltpu.CompilerParams(vmem_limit_bytes=14 * 2**20),
        cost_estimate=SMALL,
    )(scalars(order), *args)


def key_parts(kv_ref, head, at):
    base = at + H * RK
    row = at + head * RK
    total = kv_ref[pl.ds(row, 1), :] * kv_ref[base : base + DH, :]
    total = total + kv_ref[pl.ds(row + 1, 1), :] * kv_ref[base + DH : base + 2 * DH, :]
    return (total * (1.0 / RK)).astype(BF)


def query_parts(qm_ref, qt_ref, head):
    total = qm_ref[pl.ds(head * RQ, 1), :] * qt_ref[0:DH, :]
    for r in range(1, RQ):
        total = total + qm_ref[pl.ds(head * RQ + r, 1), :] * qt_ref[r * DH : (r + 1) * DH, :]
    queries = (total * (1.0 / RQ)).astype(BF)
    return (queries.astype(F32) * DH**-0.5).astype(BF)


def attend_kernel(
    place_ref, qm_ref, qt_ref, k0, k1, k2, k3, attended_ref, probs_ref, kv_ref, bias
):
    pair = pl.program_id(0)
    tok, slots = bias.shape

    @pl.when(pair == 0)
    def _():
        for block, part in enumerate((k0, k1, k2, k3)):
            kv_ref[:, block * tok : (block + 1) * tok] = part[...].astype(F32)
        near, length = place_ref[0], place_ref[1]
        rows = near * tok + lax.broadcasted_iota(jnp.int32, (tok, tok), 0)
        for block, bit in enumerate((0, 2, 1, 3)):
            keys = (near ^ bit) * tok + lax.broadcasted_iota(jnp.int32, (tok, tok), 1)
            allowed = (keys <= rows) & (keys < length)
            bias[:, block * tok : (block + 1) * tok] = jnp.where(allowed, 0.0, NEG)

    outs = []
    for inner in range(PAIR):
        head = pair * PAIR + inner
        keys = key_parts(kv_ref, head, 0)
        values = key_parts(kv_ref, head, H * RK + RK * DH)
        queries = query_parts(qm_ref, qt_ref, head)
        scores = dims(queries, keys, 0, 0) + bias[...]
        peak = jnp.max(scores, -1, keepdims=True)
        powers = jnp.exp(scores - peak)
        total = jnp.sum(powers, -1, keepdims=True)
        probs = (powers * (1.0 / total)).astype(BF)
        probs_ref[inner] = probs
        outs.append(dims(probs, values, 1, 1))
    attended_ref[...] = jnp.concatenate(outs, 1).astype(BF)


def attend(places, query_mix, query_turned, factors):
    tok = query_mix.shape[1]
    slots = 4 * tok
    table = jax.ShapeDtypeStruct((factors[0].shape[0], slots), F32)
    return pl.pallas_call(
        attend_kernel,
        grid=(H // PAIR,),
        out_shape=(
            jax.ShapeDtypeStruct((tok, H * DH), BF),
            pltpu.HBM((H, tok, slots), BF),
            table,
        ),
        in_specs=[SCALARS, whole(query_mix), whole(query_turned)] + [whole(f) for f in factors],
        out_specs=(
            pl.BlockSpec((tok, PAIR * DH), lambda i: (0, i)),
            pl.BlockSpec((PAIR, tok, slots), lambda i: (i, 0, 0)),
            whole(table),
        ),
        scratch_shapes=[pltpu.VMEM((tok, slots), F32)],
        compiler_params=pltpu.CompilerParams(vmem_limit_bytes=16 * 2**20),
        cost_estimate=SMALL,
    )(places, query_mix, query_turned, *pinned(*factors))


def attend_back_kernel(*refs):
    qm_ref, qt_ref, kv_ref, slope_ref, probs_all = refs[:5]
    kept_ref, sent_ref, qmix_ref, qbasis_ref, mix_ref, basis_ref, probs_held, psem = refs[5:]
    pair = pl.program_id(0)
    vm = H * RK + RK * DH
    kb = RK * DH

    def coming(at):
        return pltpu.make_async_copy(
            probs_all.at[pl.ds(at * PAIR, PAIR)], probs_held.at[at % 2], psem.at[at % 2]
        )

    @pl.when(pair == 0)
    def _():
        coming(pair).start()
        basis_ref[...] = jnp.zeros_like(basis_ref)
        qbasis_ref[...] = jnp.zeros_like(qbasis_ref)

    @pl.when(pair + 1 < pl.num_programs(0))
    def _():
        coming(pair + 1).start()

    coming(pair).wait()
    probs_ref = probs_held.at[pair % 2]
    for inner in range(PAIR):
        head = pair * PAIR + inner
        keys = key_parts(kv_ref, head, 0)
        values = key_parts(kv_ref, head, vm)
        queries = query_parts(qm_ref, qt_ref, head)
        slope = slope_ref[inner * DH : (inner + 1) * DH, :]
        probs_low = probs_ref[inner]
        slope_probs = dims(slope, values, 0, 0)
        probs = probs_low.astype(F32)
        weighted = probs * slope_probs
        total = jnp.sum(weighted, -1, keepdims=True)
        slope_scores = (weighted - probs * total).astype(BF)
        slope_query = dims(keys, slope_scores, 1, 1) * (DH**-0.5 / RQ)
        slope_key = dims(queries, slope_scores, 1, 0) * (1.0 / RK)
        slope_value = dims(slope, probs_low, 1, 0) * (1.0 / RK)
        for r in range(RK):
            row = head * RK + r
            for at, piece, side in ((0, slope_key, 0), (vm, slope_value, 1)):
                base = at + H * RK + r * DH
                here = side * RK + r
                basis_ref[here * DH : (here + 1) * DH, :] += kv_ref[pl.ds(at + row, 1), :] * piece
                mix_ref[pl.ds(side * H * RK + row, 1), :] = jnp.sum(
                    piece * kv_ref[base : base + DH, :], 0, keepdims=True
                )
        for r in range(RQ):
            row = head * RQ + r
            cut = slice(r * DH, (r + 1) * DH)
            qbasis_ref[cut, :] += qm_ref[pl.ds(row, 1), :] * slope_query
            qmix_ref[pl.ds(row, 1), :] = jnp.sum(slope_query * qt_ref[cut, :], 0, keepdims=True)

    @pl.when(pair == pl.num_programs(0) - 1)
    def _():
        half = kept_ref.shape[2] * 2
        tok = kept_ref.shape[2]
        km = H * RK
        for base, ref, begin, rows in (
            (0, mix_ref, 0, km),
            (km, basis_ref, 0, kb),
            (vm, mix_ref, km, km),
            (vm + km, basis_ref, kb, kb),
        ):
            part = ref[begin : begin + rows, :]
            for block in range(2):
                kept_ref[block, base : base + rows, :] = part[:, block * tok : (block + 1) * tok]
                sent_ref[block, base : base + rows, :] = part[
                    :, half + block * tok : half + (block + 1) * tok
                ].astype(BF)


def attend_back(query_mix, query_turned, row_factors, slope_attended, probs):
    tok = query_mix.shape[1]
    rows, slots = row_factors.shape
    outs = (
        jax.ShapeDtypeStruct((2, rows, tok), F32),
        jax.ShapeDtypeStruct((2, rows, tok), BF),
        jax.ShapeDtypeStruct((H * RQ, tok), F32),
        jax.ShapeDtypeStruct((RQ * DH, tok), F32),
    )
    return pl.pallas_call(
        attend_back_kernel,
        grid=(H // PAIR,),
        out_shape=outs,
        in_specs=[
            whole(query_mix),
            whole(query_turned),
            whole(row_factors),
            pl.BlockSpec((PAIR * DH, tok), lambda i: (i, 0)),
            pl.BlockSpec(memory_space=pltpu.HBM),
        ],
        out_specs=tuple(whole(o) for o in outs),
        scratch_shapes=[
            pltpu.VMEM((2 * H * RK, slots), F32),
            pltpu.VMEM((2 * RK * DH, slots), F32),
            pltpu.VMEM((2, PAIR, tok, slots), BF),
            pltpu.SemaphoreType.DMA((2,)),
        ],
        compiler_params=pltpu.CompilerParams(vmem_limit_bytes=18 * 2**20),
        cost_estimate=SMALL,
    )(query_mix, query_turned, row_factors, slope_attended, *pinned(probs))


QB, KB, VB = RQ * DH, RK * DH, RK * DH
QM, KM, VM = H * RQ, H * RK, H * RK
LEFT = 512
GAINS = LEFT + KB + VB + KM + VM
PACKED = 896


def steps_of_any_mesh(
    tokens, places, cosine, sine, packed, merge_weight, both, down_weight, cotangent
):
    tok, width = tokens.shape
    group, twice, hidden = both.shape
    rows = twice // 2
    cut = down_weight.shape[0]
    axes = ("wide", "narrow")
    packed = [lax.all_gather(packed, axes, axis=0, tiled=True)[None]]
    merge = [lax.all_gather(merge_weight, axes, axis=0, tiled=True)[None]]
    downs = [lax.all_gather(down_weight, "wide", axis=0, tiled=True)[None]]
    both = lax.all_to_all(both, "narrow", 0, 0, tiled=True)
    both = lax.all_gather(both, "wide", axis=0, tiled=False)
    both = both.reshape(-1, 2, rows, hidden).transpose(1, 0, 2, 3)
    both = both.reshape(2, 8, 4, width // 32, hidden).transpose(1, 2, 0, 3, 4)
    weights_in = ([both.reshape(8, 4, width // 16, hidden)], list(range(8)), downs, [0])

    hidden_one, inverse_one, gains, weights, query_mix, query_turned, own_factors = project(
        tokens, cosine, sine, packed, [0]
    )
    attended, probs, row_factors = attend(
        places, query_mix, query_turned, gather_narrow(own_factors)
    )
    hidden_two, middle, inverse_two = middle_of(attended, tokens, gains, merge, [0])
    own, far, close, cross = gather_narrow(hidden_two)
    cot_own, cot_far, cot_near, cot_cross = gather_narrow(cotangent)
    parts = [
        feed((own, close), (cot_own, cot_near), *weights_in),
        feed((far, cross), (cot_far, cot_cross), *weights_in),
    ]
    hidden_feed, slope_gate, slope_up = zip(*(part[:3] for part in parts))
    came_near = flip(parts[0][4], "narrow", 1)
    came_far = flip(add_low(parts[1][3], flip(parts[1][4], "narrow", 1)), "narrow", 2)
    full = slopes_of((own, close, far, cross), slope_gate, slope_up, list(range(width // 128)))
    full = [s.transpose(0, 2, 1).reshape(width, hidden) for s in full]
    slopes = jnp.concatenate([scatter_wide(s).reshape(group, rows, hidden) for s in full], 1)
    slopes = lax.all_to_all(slopes.astype(BF), "narrow", 0, 0, tiled=True)
    cots = (cot_own, cot_near, cot_far, cot_cross)
    down_slope = scatter_wide(down_slopes(hidden_feed, cots, [0], cut)[0])
    kept, sent = feed_out(hidden_feed, downs, [0])
    fed = kept + flip(sent, "narrow", 1).astype(F32)
    fed = fed[0] + flip(fed[1].astype(BF), "narrow", 2).astype(F32)
    output = (middle + fed).astype(BF)

    slope_middle, slope_low, slope_attended, feed_gain_slope = turn_back(
        parts[0][3], came_near, came_far, middle, inverse_two, gains, cotangent, merge, [0]
    )
    merge_slope = scatter_all(dims(attended, slope_low, 0, 0).astype(BF))
    factors_in = (query_mix, query_turned, row_factors, slope_attended, probs)
    key_kept, key_sent, query_mix_slope, query_basis_slope = attend_back(*factors_in)
    key_pair = key_kept + flip(key_sent, "narrow", 1).astype(F32)
    key_came = flip(key_pair[1].astype(BF), "narrow", 2)
    part, query_slopes = query_end(
        [0], query_mix_slope, query_basis_slope, cosine, sine, hidden_one, weights
    )
    tokens_slope, key_slopes = key_end(
        [0], key_pair[0], key_came, cosine, sine, hidden_one, weights, part, tokens, inverse_one,
        gains, slope_middle, feed_gain_slope,
    )
    query_slopes, key_slopes = scatter_all(query_slopes), scatter_all(key_slopes)
    return output, tokens_slope, query_slopes, key_slopes, merge_slope, slopes, down_slope


def steps_of_small_mesh(
    tokens, places, cosine, sine, packed, merge_weight, both_in, down_weight, cotangent
):
    tok, width = tokens.shape
    cut = down_weight.shape[0]
    high, low = wide_place()
    rounds = lax.axis_size("wide") // 2
    group = lax.axis_size("narrow")
    join = lambda a, b: jnp.concatenate([a, b], 0)

    first, both_in = tie(jnp.concatenate([packed, merge_weight], 1)[None], both_in)
    first = turned(first)
    both = lax.all_to_all(both_in, "narrow", 0, 0, tiled=True)
    *first, both = tie(*first, both)
    pieces = [both[None]]
    one = jnp.concatenate([f[:, :, :PACKED] for f in first], 0)
    two = jnp.concatenate([f[:, :, PACKED:] for f in first], 0)
    one, one_came, two, two_came, piece = tie(
        one, flip(one, "narrow", 2), two, flip(two, "wide", 1), turn(pieces[0], 1)
    )
    pieces.append(piece)
    one, two = join(one, one_came), join(two, two_came)
    one, one_came, two, two_came, piece = tie(
        one, flip(one, "wide", 1), two, flip(two, "narrow", 2), turn(pieces[1], 1)
    )
    pieces.append(piece)
    one, two = join(one, one_came), join(two, two_came)
    where, merge_where = relative_blocks(), relative_blocks(True)
    both_where = [((high - k) % rounds) * 2 + low for k in range(rounds)] + [
        ((high - k) % rounds) * 2 + 1 - low for k in range(rounds)
    ]
    one, piece, down_own = tie(one, pieces[2], down_weight)
    pieces.append(turn(piece, 1))
    down_came = flip(down_own, "wide", 1)
    hidden_one, inverse_one, gains, weights, query_mix, query_turned, factor = project(
        tokens, cosine, sine, [one, flip(one, "narrow", 1)], where
    )
    factor, two, down_came, pieces[3], first_own, first_came = tie(
        factor, two, down_came, pieces[3], pieces[0], pieces[1]
    )
    merge = [two, flip(two, "narrow", 1)]
    others = [flip(first_own, "wide", 1)]
    pair = jnp.where(low == 0, jnp.stack([down_own, down_came]), jnp.stack([down_came, down_own]))
    downs = [ring_all_to_all(jnp.stack([pair.reshape(2 * cut, width)] * rounds))]
    down_where = list(range(rounds))
    factor_far, factor_near = tie(flip(factor, "narrow", 2), flip(factor, "narrow", 1))
    others.append(flip(after(first_came, factor_far), "wide", 1))
    factor_cross, others[0], cot_own = tie(
        flip(factor_far, "narrow", 1), others[0], cotangent
    )

    cot_far = flip(cot_own, "narrow", 2)
    others += [flip(piece, "wide", 1) for piece in after((pieces[2], pieces[3]), factor_cross)]
    attended, probs, row_factors = attend(
        places, query_mix, query_turned, (factor, factor_far, factor_near, factor_cross)
    )
    attended, cot_far, others[1], others[2], merge[1] = tie(
        attended, cot_far, others[1], others[2], merge[1]
    )
    hidden_two, middle, inverse_two = middle_of(attended, tokens, gains, merge, merge_where)
    own, cot_far = tie(hidden_two, cot_far)

    far, close = flip(own, "narrow", 2), flip(own, "narrow", 1)
    cot_near, cot_cross = flip(cot_own, "narrow", 1), flip(cot_far, "narrow", 1)
    weights_in = (pieces + others, both_where, downs, down_where)
    one = feed((own, close), (cot_own, cot_near), *weights_in)
    far, one_sent = tie(far, one[4])
    came_near = flip(one_sent, "narrow", 1)
    cross = flip(far, "narrow", 1)
    two = feed((far, cross), (cot_far, cot_cross), *weights_in)
    for_far = add_low(two[3], flip(two[4], "narrow", 1))
    hidden_feed, slope_gate, slope_up = zip(one[:3], two[:3])
    for_far, slope_gate, slope_up, came_near = tie(for_far, slope_gate, slope_up, came_near)
    came_far = flip(for_far, "narrow", 2)
    slots = (own, close, far, cross)
    cots = (cot_own, cot_near, cot_far, cot_cross)
    to_send = slopes_of(slots, slope_gate, slope_up, [2 * k + 1 - low for k in range(rounds)])
    hidden_feed, gate_sent, up_sent = tie(hidden_feed, *to_send)
    gate_came = flip(gate_sent, "wide", 1)
    down_order = [
        2 * ((high + k) % rounds) + side for k in range(rounds) for side in (low, 1 - low)
    ]
    down_sent, down_kept = down_slopes(hidden_feed, cots, down_order, cut)
    slope_gate, slope_up, down_sent = tie(slope_gate, slope_up, down_sent)
    to_keep = slopes_of(slots, slope_gate, slope_up, [2 * k + low for k in range(rounds)])
    came_far, gate_kept, up_kept = tie(came_far, *to_keep)

    slope_middle, slope_low, slope_attended, feed_gain_slope = turn_back(
        one[3], came_near, came_far, middle, inverse_two, gains, cotangent, merge, merge_where
    )
    merge_sent, merge_kept = outer_blocks(scatter_order(True), attended, slope_low)
    merge_sent, slope_attended, gate_came, up_sent = tie(
        merge_sent, slope_attended, gate_came, up_sent
    )
    up_came = flip(up_sent, "wide", 1)
    merge_came = flip(merge_sent, "narrow", 1)
    gate_sum = add_low(gate_kept, gate_came)
    slope_attended, gate_sum = tie(slope_attended, gate_sum)
    gate_sum = ring_all_to_all(gate_sum)
    key_kept, key_sent, query_mix_slope, query_basis_slope = attend_back(
        query_mix, query_turned, row_factors, slope_attended, probs
    )
    key_kept, key_sent, query_basis_slope, merge_came, up_came, gate_sum, down_sent = tie(
        key_kept, key_sent, query_basis_slope, merge_came, up_came, gate_sum, down_sent
    )
    key_came = flip(key_sent, "narrow", 1)
    down_came = flip(down_sent, "wide", 1)
    merge_sum = add_low(merge_kept, merge_came)
    key_came, merge_sum = tie(key_came, merge_sum)
    key_pair = key_kept + key_came.astype(F32)
    merge_came = flip(merge_sum[8:], "narrow", 2)
    key_far, up_came, query_basis_slope = tie(
        key_pair[1].astype(BF), up_came, query_basis_slope
    )
    key_came = flip(key_far, "narrow", 2)
    up_sum = ring_all_to_all(add_low(up_kept, up_came))
    order = scatter_order(True)
    part, query_sent, query_kept = query_end(
        order, query_mix_slope, query_basis_slope, cosine, sine, hidden_one, weights
    )
    key_came, part = tie(key_came, part)
    tokens_slope, ends_sent, ends = key_end(
        order, key_pair[0], key_came, cosine, sine, hidden_one, weights, part, tokens, inverse_one,
        gains, slope_middle, feed_gain_slope, query_sent, query_kept,
    )

    ends_came, merge_came = tie(flip(ends_sent, "narrow", 1), merge_came)
    ends = add_low(ends, ends_came)
    merge_sum = add_low(merge_sum[:8], merge_came)
    ends, merge_sum, hidden_feed = tie(ends, merge_sum, hidden_feed)
    ends_came = flip(ends[8:], "narrow", 2)
    merge_came = flip(merge_sum[4:], "wide", 1)
    kept, sent = feed_out(hidden_feed, downs, down_where)
    ends_came, kept, sent, merge_came, down_came, up_sum = tie(
        ends_came, kept, sent, merge_came, down_came, up_sum
    )
    ends = add_low(ends[:8], ends_came)
    ends, sent, up_sum, merge_came = tie(ends, sent, up_sum, merge_came)
    ends_came = flip(ends[4:], "wide", 1)
    fed = kept + flip(sent, "narrow", 1).astype(F32)
    slopes = finish(gate_sum, up_sum, group)
    merge_sum = add_low(merge_sum[:4], merge_came)
    ends_came, slopes, fed, merge_sum = tie(ends_came, slopes, fed, merge_sum)
    ends = add_low(ends[:4], ends_came)
    ends, slopes = tie(ends, slopes)
    sums = spread_turns(ends)
    slopes = lax.all_to_all(slopes, "narrow", 0, 0, tiled=True)
    merge_slope = spread_turns(merge_sum)
    fed_came = flip(fed[1].astype(BF), "narrow", 2)
    down_slope = spread_turns(add_low(down_kept, down_came))
    output = (middle + fed[0] + fed_came.astype(F32)).astype(BF)
    return output, tokens_slope, sums[:, :LEFT], sums[:, LEFT:], merge_slope, slopes, down_slope


def per_device(
    tokens,
    lengths,
    attend_gain,
    query_heads,
    query_basis,
    key_heads,
    key_basis,
    value_heads,
    value_basis,
    merge_weight,
    feed_gain,
    gate_weight,
    up_weight,
    down_weight,
    cotangent,
):
    tok, width = tokens.shape
    wide_count = lax.axis_size("wide")
    narrow_count = lax.axis_size("narrow")
    near = lax.axis_index("narrow")
    rows = gate_weight.shape[0]
    cut = down_weight.shape[0]
    hidden = cut * wide_count
    small = small_mesh()

    positions = (near * tok + jnp.arange(tok, dtype=jnp.int32)).astype(F32)
    frequency = jnp.power(10000.0, -2.0 * jnp.arange(DH // 2, dtype=F32) / DH)
    angles = frequency[:, None] * positions[None, :]
    cosine, sine = jnp.cos(angles), jnp.sin(angles)

    packed = jnp.concatenate(
        [
            query_basis,
            query_heads,
            jnp.zeros((rows, LEFT - QB - QM), BF),
            key_basis,
            value_basis,
            key_heads,
            value_heads,
            attend_gain[:, None],
            feed_gain[:, None],
            jnp.zeros((rows, PACKED - GAINS - 2), BF),
        ],
        1,
    )

    def columns(weight):
        parts = weight.reshape(rows, wide_count, narrow_count, cut).transpose(2, 0, 1, 3)
        return parts.reshape(narrow_count, rows, hidden)

    both_in = jnp.concatenate([columns(gate_weight), columns(up_weight)], 1)
    places = jnp.stack([near.astype(jnp.int32), lengths[0].astype(jnp.int32)])
    if small:
        exact = steps_of_small_mesh
    else:
        exact = steps_of_any_mesh
    output, tokens_slope, query_slopes, key_slopes, merge_slope, slopes, down_slope = exact(
        tokens, places, cosine, sine, packed, merge_weight, both_in, down_weight, cotangent
    )
    if small:
        slopes = unmix(slopes, cut)
    else:
        slopes = slopes.reshape(narrow_count, 2, rows, wide_count, cut).transpose(1, 2, 3, 0, 4)
        slopes = slopes.reshape(2, rows, hidden * narrow_count).astype(F32)

    base = GAINS - LEFT
    return (
        output,
        tokens_slope,
        key_slopes[:, base],
        query_slopes[:, QB : QB + QM],
        query_slopes[:, :QB],
        key_slopes[:, KB + VB : KB + VB + KM],
        key_slopes[:, :KB],
        key_slopes[:, KB + VB + KM : KB + VB + KM + VM],
        key_slopes[:, KB : KB + VB],
        merge_slope,
        key_slopes[:, base + 1],
        slopes[0],
        slopes[1],
        down_slope,
    )


def solution(mesh):
    both = ("wide", "narrow")
    row, vector = P(both, None), P(both)
    return jax.shard_map(
        per_device,
        mesh=mesh,
        in_specs=(row, P("wide"), vector) + (row,) * 7 + (vector,) + (row,) * 4,
        out_specs=(row, row, vector) + (row,) * 7 + (vector,) + (row,) * 3,
        check_vma=False,
    )
```

```python
import functools

import jax
import jax.numpy as jnp
from jax import lax
from jax.experimental import pallas as pl
from jax.experimental.pallas import tpu as pltpu
from jax.sharding import PartitionSpec as P

H = 16
DH = 64
RQ = 6
RK = 2
PAIR = 2
EPS = 1e-06
NEG = -1e30
BF = jnp.bfloat16
F32 = jnp.float32


def dims(left, right, left_dim, right_dim):
    return lax.dot_general(
        left, right, (((left_dim,), (right_dim,)), ((), ())), preferred_element_type=F32
    )


def flip(value, axis, bit):
    size = lax.axis_size(axis)
    return lax.ppermute(value, axis, [(i, i ^ bit) for i in range(size)])


def turn(value, steps):
    size = lax.axis_size("wide")
    return lax.ppermute(value, "wide", [(i, (i + 2 * steps) % size) for i in range(size)])


def small_mesh():
    return lax.axis_size("wide") == 8 and lax.axis_size("narrow") == 4


def wide_place():
    me = lax.axis_index("wide")
    return me // 2, me % 2


def tie(*values):
    return lax.optimization_barrier(values)


def after(value, *others):
    return lax.optimization_barrier((value, others))[0]


def ring_groups():
    size = lax.axis_size("wide")
    return [list(range(x, size, 2)) for x in range(2)]


def ring_all_to_all(value):
    return lax.all_to_all(value, "wide", 0, 0, axis_index_groups=ring_groups(), tiled=True)


def spread_high(blocks):
    return jnp.sum(ring_all_to_all(blocks).astype(F32), 0)


def scatter_wide(value):
    return lax.psum_scatter(value, "wide", scatter_dimension=0, tiled=True).astype(F32)


def turned(value):
    rounds = lax.axis_size("wide") // 2
    return [value] + [turn(value, k) for k in range(1, rounds)]


def joined(value, axis, bit):
    return jnp.concatenate([value, flip(value, axis, bit)], 0)


def relative_blocks(swapped=False):
    high, low = wide_place()
    rounds = lax.axis_size("wide") // 2
    near = lax.axis_index("narrow")
    return [
        (((high - k) % rounds) * 2 + (low ^ x)) * 4 + (near ^ (2 * y) ^ c)
        for c in (0, 1)
        for x, y in ([(0, 0), (1, 0), (0, 1), (1, 1)] if swapped else [(0, 0), (0, 1), (1, 0), (1, 1)])
        for k in range(rounds)
    ]


def scatter_all(value):
    return lax.psum_scatter(value, ("wide", "narrow"), scatter_dimension=0, tiled=True).astype(F32)


def scatter_order(turning):
    high, low = wide_place()
    rounds = lax.axis_size("wide") // 2
    near = lax.axis_index("narrow")
    return [
        (((high + k) % rounds if turning else k) * 2 + (low ^ x)) * 4 + (near ^ (2 * y) ^ c)
        for c in (0, 1)
        for y in (0, 1)
        for x in (0, 1)
        for k in range(rounds)
    ]


def spread_turns(blocks):
    total = blocks[0].astype(F32)
    for k in range(1, blocks.shape[0]):
        total = total + turn(blocks[k], k).astype(F32)
    return total


def add_low(kept, came):
    return (kept.astype(F32) + came.astype(F32)).astype(BF)


def gather_narrow(value):
    far = flip(value, "narrow", 2)
    return [value, far, flip(value, "narrow", 1), flip(far, "narrow", 1)]


def starts(stacks, where_ref, first, target, sem):
    copies = []
    for stack in stacks:
        for k in range(stack.shape[0]):
            at = len(copies)
            copies.append(
                pltpu.make_async_copy(
                    stack.at[k], target.at[where_ref[first + at]], sem.at[first + at]
                )
            )
            copies[-1].start()
    return copies


def count(stacks):
    return sum(stack.shape[0] for stack in stacks)


def whole(array):
    return pl.BlockSpec(array.shape, lambda *i: (0,) * len(array.shape))


ANYWHERE = pl.BlockSpec(memory_space=pl.ANY)


def pinned(*arrays):
    return [pltpu.with_memory_space_constraint(a, pltpu.HBM) for a in arrays]


SCALARS = pl.BlockSpec(memory_space=pltpu.SMEM)
SMALL = pl.CostEstimate(flops=3 * 10**9, bytes_accessed=2**22, transcendentals=0)


def scalars(*lists):
    return jnp.stack([jnp.asarray(v, jnp.int32) for one in lists for v in one])


def project_kernel(n, where, tokens_ref, cos_ref, sin_ref, *refs):
    packed, refs = refs[:n], refs[n:]
    hidden_ref, inverse_ref, gains_ref, packed_ref, qm_ref, qt_ref, kv_ref, sem = refs
    copies = starts(packed, where, 0, packed_ref, sem)
    source = tokens_ref[...].astype(F32)
    inverse = lax.rsqrt(jnp.mean(source * source, -1, keepdims=True) + EPS)
    inverse_ref[...] = inverse
    normed = source * inverse
    for copy in copies:
        copy.wait()
    width = source.shape[1]
    weights = packed_ref[...].reshape(width, PACKED)
    gains = weights[:, PACKED - 128 :].astype(F32).T
    at = GAINS - (PACKED - 128)
    gains_ref[...] = gains[at : at + 8]
    hidden = (normed * gains[at : at + 1]).astype(BF)
    hidden_ref[...] = hidden
    factors = dims(hidden, weights, 1, 0).T
    cosine, sine = cos_ref[...], sin_ref[...]
    half = DH // 2
    for r in range(RQ + RK):
        base = r * DH if r < RQ else LEFT + (r - RQ) * DH
        one = factors[base : base + half]
        two = factors[base + half : base + DH]
        a, b = one * cosine - two * sine, one * sine + two * cosine
        if r < RQ:
            qt_ref[base : base + half, :] = a
            qt_ref[base + half : base + DH, :] = b
        else:
            row = KM + (r - RQ) * DH
            kv_ref[row : row + half, :] = a.astype(BF)
            kv_ref[row + half : row + DH, :] = b.astype(BF)
    qm_ref[...] = factors[QB : QB + QM]
    base = LEFT + KB
    kv_ref[2 * KM + KB :, :] = factors[base : base + VB].astype(BF)
    base += VB
    kv_ref[0:KM, :] = factors[base : base + KM].astype(BF)
    kv_ref[KM + KB : 2 * KM + KB, :] = factors[base + KM : base + 2 * KM].astype(BF)


VMEM = pl.BlockSpec(memory_space=pltpu.VMEM)


def project(tokens, cosine, sine, packed, where):
    tok, width = tokens.shape
    outs = (
        jax.ShapeDtypeStruct((tok, width), BF),
        jax.ShapeDtypeStruct((tok, 1), F32),
        jax.ShapeDtypeStruct((8, width), F32),
        jax.ShapeDtypeStruct((count(packed),) + packed[0].shape[1:], BF),
        jax.ShapeDtypeStruct((QM, tok), F32),
        jax.ShapeDtypeStruct((QB, tok), F32),
        jax.ShapeDtypeStruct((2 * (KM + KB), tok), BF),
    )
    return pl.pallas_call(
        functools.partial(project_kernel, len(packed)),
        out_shape=outs,
        in_specs=[SCALARS] + [VMEM] * 3 + [ANYWHERE] * len(packed),
        out_specs=tuple(VMEM for _ in outs),
        scratch_shapes=[pltpu.SemaphoreType.DMA((count(packed),))],
        compiler_params=pltpu.CompilerParams(vmem_limit_bytes=14 * 2**20),
        cost_estimate=SMALL,
    )(scalars(where), tokens, cosine, sine, *packed)


def halves_of(both_ref, width, hidden):
    rows = both_ref.shape[2] // 2
    return (
        both_ref[:, :, :rows, :].reshape(width, hidden),
        both_ref[:, :, rows:, :].reshape(width, hidden),
    )


def feed_kernel(nb, nd, where, *refs):
    pieces, refs = refs[:2], refs[2:]
    cots, refs = refs[:2], refs[2:]
    boths, refs = refs[:nb], refs[nb:]
    downs, refs = refs[:nd], refs[nd:]
    hf_out, sg_out, su_out, kept_ref, sent_ref, hid, cot, wgu, wd, held, sem, psem, osem = refs
    outgoing = []
    width, hidden = hid.shape[2], wgu.shape[3]
    loads = [
        [
            pltpu.make_async_copy(pieces[b], hid.at[b], psem.at[b]),
            pltpu.make_async_copy(cots[b], cot.at[b], psem.at[2 + b]),
        ]
        for b in range(2)
    ]
    loads[0][0].start()
    in_both = starts(boths, where, 0, wgu, sem)
    loads[0][1].start()
    in_down = starts(downs, where, count(boths), wd, sem)
    for copy in loads[1]:
        copy.start()
    for b in range(2):
        loads[b][0].wait()
        if b == 0:
            for copy in in_both:
                copy.wait()
        gate_all, up_all = halves_of(wgu, width, hidden)
        gate = dims(hid[b], gate_all, 1, 0)
        upward = dims(hid[b], up_all, 1, 0)
        loads[b][1].wait()
        if b == 0:
            for copy in in_down:
                copy.wait()
        down_all = wd[...].reshape(hidden, width)
        slope = dims(cot[b], down_all, 1, 1)
        sig = jax.nn.sigmoid(gate)
        silu = gate * sig
        held[0, b] = (silu * upward).astype(BF)
        slope_up = (slope * silu).astype(BF)
        slope_gate = (slope * upward * sig * (1.0 + gate * (1.0 - sig))).astype(BF)
        held[1, b] = slope_gate
        held[2, b] = slope_up
        for k, out in enumerate((hf_out, sg_out, su_out)):
            outgoing.append(pltpu.make_async_copy(held.at[k, b], out.at[b], osem.at[k, b]))
            outgoing[-1].start()
        back = dims(slope_gate, gate_all, 1, 1) + dims(slope_up, up_all, 1, 1)
        if b == 0:
            kept_ref[...] = back
        else:
            sent_ref[...] = back.astype(BF)
    for copy in outgoing:
        copy.wait()


def feed(pieces, cots, boths, both_where, downs, down_where):
    tok, width = pieces[0].shape
    hidden = boths[0].shape[3]
    low = pltpu.HBM((2, tok, hidden), BF)
    outs = (
        low,
        low,
        low,
        jax.ShapeDtypeStruct((tok, width), F32),
        jax.ShapeDtypeStruct((tok, width), BF),
    )
    blocks = lambda stacks: pltpu.VMEM((count(stacks),) + stacks[0].shape[1:], BF)
    total = count(boths) + count(downs)
    return pl.pallas_call(
        functools.partial(feed_kernel, len(boths), len(downs)),
        out_shape=outs,
        in_specs=[SCALARS] + [ANYWHERE] * (4 + len(boths) + len(downs)),
        out_specs=(ANYWHERE,) * 3 + (VMEM,) * 2,
        scratch_shapes=[
            pltpu.VMEM((2, tok, width), BF),
            pltpu.VMEM((2, tok, width), BF),
            blocks(boths),
            blocks(downs),
            pltpu.VMEM((3, 2, tok, hidden), BF),
            pltpu.SemaphoreType.DMA((total,)),
            pltpu.SemaphoreType.DMA((4,)),
            pltpu.SemaphoreType.DMA((3, 2)),
        ],
        compiler_params=pltpu.CompilerParams(vmem_limit_bytes=20 * 2**20),
        cost_estimate=SMALL,
    )(scalars(both_where, down_where), *pinned(*pieces, *cots, *boths, *downs))


def bring(sources, target, sem):
    copies = []
    at = 0
    for source in sources:
        parts = [source] if len(source.shape) == 2 else [source.at[k] for k in range(source.shape[0])]
        for part in parts:
            copies.append(pltpu.make_async_copy(part, target.at[at], sem.at[at]))
            copies[-1].start()
            at += 1
    return copies


def slopes_kernel(blocks, order, *refs):
    *outs, hid, gates, ups, hsem, gsem, usem = refs[8:]
    out = outs[0]
    copies = bring(refs[:4], hid, hsem) + bring(refs[4:6], gates, gsem)
    later = bring(refs[6:8], ups, usem)
    for copy in copies:
        copy.wait()
    rows, hidden = out.shape[-1], out.shape[-2]
    columns = []
    for k in range(blocks):
        at = pl.multiple_of(order[k] * rows, 128)
        columns.append(hid[:, :, pl.ds(at, rows)].reshape(-1, rows))
    chosen = jnp.concatenate(columns, 1)
    for side, held in enumerate((gates, ups)):
        if side == 1:
            for copy in later:
                copy.wait()
        result = dims(held[...].reshape(-1, hidden), chosen, 0, 0).astype(BF)
        for k in range(blocks):
            part = result[:, k * rows : (k + 1) * rows]
            if len(outs) == 2:
                outs[side][k] = part
            else:
                out[k, side] = part


def slopes_of(pieces, slope_gate, slope_up, order, apart=False):
    tok, width = pieces[0].shape
    hidden = slope_gate[0].shape[2]
    rows = 128
    return pl.pallas_call(
        functools.partial(slopes_kernel, len(order)),
        out_shape=(jax.ShapeDtypeStruct((len(order), hidden, rows), BF),) * 2
        if apart
        else jax.ShapeDtypeStruct((len(order), 2, hidden, rows), BF),
        in_specs=[SCALARS] + [ANYWHERE] * 8,
        out_specs=(VMEM, VMEM) if apart else VMEM,
        scratch_shapes=[
            pltpu.VMEM((4, tok, width), BF),
            pltpu.VMEM((4, tok, hidden), BF),
            pltpu.VMEM((4, tok, hidden), BF),
        ]
        + [pltpu.SemaphoreType.DMA((4,))] * 3,
        compiler_params=pltpu.CompilerParams(vmem_limit_bytes=18 * 2**20),
        cost_estimate=SMALL,
    )(scalars(order), *pinned(*pieces, *slope_gate, *slope_up))


def down_kernel(blocks, order, *refs):
    feeds, cots, fsem, csem = refs[-4:]
    for copy in bring(refs[:2], feeds, fsem) + bring(refs[2:6], cots, csem):
        copy.wait()
    outs = refs[6:-4]
    hidden, width = feeds.shape[2], cots.shape[2]
    total = dims(feeds[...].reshape(-1, hidden), cots[...].reshape(-1, width), 0, 0)
    if blocks == 1:
        outs[0][...] = total.astype(BF)
    else:
        sent_ref, kept_ref, held = outs
        held[...] = total.reshape(held.shape)
        for k in range(blocks // 2):
            kept_ref[k] = held[order[2 * k]].astype(BF)
            sent_ref[k] = held[order[2 * k + 1]].astype(BF)


def down_slopes(hidden_feed, cots, order, cut):
    tok, width = cots[0].shape
    hidden = hidden_feed[0].shape[2]
    if len(order) > 1:
        out = jax.ShapeDtypeStruct((len(order) // 2, cut, width), BF)
        outs, scratch = (out, out), [pltpu.VMEM((len(order), cut, width), F32)]
    else:
        outs, scratch = (jax.ShapeDtypeStruct((hidden, width), BF),), []
    return pl.pallas_call(
        functools.partial(down_kernel, len(order)),
        out_shape=outs,
        in_specs=[SCALARS] + [ANYWHERE] * 6,
        out_specs=(VMEM,) * len(outs),
        scratch_shapes=scratch
        + [
            pltpu.VMEM((4, tok, hidden), BF),
            pltpu.VMEM((4, tok, width), BF),
            pltpu.SemaphoreType.DMA((4,)),
            pltpu.SemaphoreType.DMA((4,)),
        ],
        compiler_params=pltpu.CompilerParams(vmem_limit_bytes=20 * 2**20),
        cost_estimate=SMALL,
    )(scalars(order), *pinned(*hidden_feed, *cots))


def feed_out_kernel(nd, where, *refs):
    downs, (f0, f1, kept_ref, sent_ref, wd, feeds, sem, fsem) = refs[:nd], refs[nd:]
    for copy in starts(downs, where, 0, wd, sem) + bring((f0, f1), feeds, fsem):
        copy.wait()
    down_all = wd[...].reshape(feeds.shape[2], wd.shape[2])
    for part in range(2):
        kept_ref[part] = dims(feeds[2 * part], down_all, 1, 0)
        sent_ref[part] = dims(feeds[2 * part + 1], down_all, 1, 0).astype(BF)


def feed_out(hidden_feed, downs, down_where):
    tok, hidden = hidden_feed[0].shape[1:]
    width = downs[0].shape[2]
    return pl.pallas_call(
        functools.partial(feed_out_kernel, len(downs)),
        out_shape=(
            jax.ShapeDtypeStruct((2, tok, width), F32),
            jax.ShapeDtypeStruct((2, tok, width), BF),
        ),
        in_specs=[SCALARS] + [ANYWHERE] * (len(downs) + 2),
        out_specs=(VMEM, VMEM),
        scratch_shapes=[
            pltpu.VMEM((count(downs),) + downs[0].shape[1:], BF),
            pltpu.VMEM((4, tok, hidden), BF),
            pltpu.SemaphoreType.DMA((count(downs),)),
            pltpu.SemaphoreType.DMA((4,)),
        ],
        compiler_params=pltpu.CompilerParams(vmem_limit_bytes=14 * 2**20),
        cost_estimate=SMALL,
    )(scalars(down_where), *pinned(*downs, *hidden_feed))


def finish_kernel(parts_ref, out_ref):
    rows = out_ref.shape[1] // 2
    for side in range(2):
        total = parts_ref[0, side].astype(F32)
        for k in range(1, parts_ref.shape[0]):
            total = total + parts_ref[k, side].astype(F32)
        total = total.T.astype(BF)
        for n in range(out_ref.shape[0]):
            out_ref[n, side * rows : (side + 1) * rows, :] = total[n * rows : (n + 1) * rows]


def finish(parts, group):
    _, _, hidden, rows = parts.shape
    return pl.pallas_call(
        finish_kernel,
        out_shape=jax.ShapeDtypeStruct((group, 2 * rows // group, hidden), BF),
        in_specs=[VMEM],
        out_specs=VMEM,
        compiler_params=pltpu.CompilerParams(vmem_limit_bytes=8 * 2**20),
        cost_estimate=SMALL,
    )(parts)


def unmix_kernel(cut, x_ref, gate_ref, up_ref):
    group, rows, hidden = x_ref.shape
    rows //= 2
    for side, ref in ((0, gate_ref), (1, up_ref)):
        parts = [x_ref[n, side * rows : (side + 1) * rows, :].astype(F32) for n in range(group)]
        ref[...] = jnp.concatenate(
            [part[:, w * cut : (w + 1) * cut] for w in range(hidden // cut) for part in parts], 1
        )


def unmix(value, cut):
    group, rows, hidden = value.shape
    out = jax.ShapeDtypeStruct((rows // 2, group * hidden), F32)
    return pl.pallas_call(
        functools.partial(unmix_kernel, cut),
        out_shape=(out, out),
        in_specs=[VMEM],
        out_specs=(VMEM, VMEM),
        compiler_params=pltpu.CompilerParams(vmem_limit_bytes=8 * 2**20),
        cost_estimate=SMALL,
    )(value)


def middle_kernel(n, where, attended_ref, tokens_ref, gains_ref, *refs):
    stacks, (hidden_ref, middle_ref, inverse_ref, merge, sem) = refs[:n], refs[n:]
    for copy in starts(stacks, where, 0, merge, sem):
        copy.wait()
    width = tokens_ref.shape[1]
    full = merge[...].reshape(attended_ref.shape[1], width)
    middle = tokens_ref[...].astype(F32) + dims(attended_ref[...], full, 1, 0)
    inverse = lax.rsqrt(jnp.mean(middle * middle, -1, keepdims=True) + EPS)
    middle_ref[...] = middle
    inverse_ref[...] = inverse
    hidden_ref[...] = (middle * inverse * gains_ref[1:2, :]).astype(BF)


def middle_of(attended, tokens, gains, stacks, where):
    tok, width = tokens.shape
    outs = (
        jax.ShapeDtypeStruct((tok, width), BF),
        jax.ShapeDtypeStruct((tok, width), F32),
        jax.ShapeDtypeStruct((tok, 1), F32),
    )
    return pl.pallas_call(
        functools.partial(middle_kernel, len(stacks)),
        out_shape=outs,
        in_specs=[SCALARS] + [VMEM] * 3 + [ANYWHERE] * len(stacks),
        out_specs=(VMEM,) * 3,
        scratch_shapes=[
            pltpu.VMEM((count(stacks),) + stacks[0].shape[1:], BF),
            pltpu.SemaphoreType.DMA((count(stacks),)),
        ],
        compiler_params=pltpu.CompilerParams(vmem_limit_bytes=10 * 2**20),
        cost_estimate=SMALL,
    )(scalars(where), attended, tokens, gains, *stacks)


def turn_back_kernel(
    n, where, kept_ref, near_ref, far_ref, middle_ref, inverse_ref, gains_ref, cot_ref, *refs
):
    stacks, (slope_ref, low_ref, attended_ref, gain_ref, merge, sem) = refs[:n], refs[n:]
    copies = starts(stacks, where, 0, merge, sem)
    slope = kept_ref[...] + near_ref[...].astype(F32) + far_ref[...].astype(F32)
    inverse = inverse_ref[...]
    normed = middle_ref[...] * inverse
    gain_ref[...] = jnp.sum(slope * normed, 0, keepdims=True)
    scaled = slope * gains_ref[1:2, :]
    mean = jnp.mean(scaled * normed, -1, keepdims=True)
    slope_middle = cot_ref[...].astype(F32) + inverse * (scaled - normed * mean)
    slope_ref[...] = slope_middle
    low = slope_middle.astype(BF)
    low_ref[...] = low
    for copy in copies:
        copy.wait()
    full = merge[...].reshape(attended_ref.shape[0], low.shape[1])
    attended_ref[...] = dims(full, low, 1, 1).astype(BF)


def turn_back(kept, came_near, came_far, middle, inverse, gains, cotangent, stacks, where):
    tok, width = middle.shape
    outs = (
        jax.ShapeDtypeStruct((tok, width), F32),
        jax.ShapeDtypeStruct((tok, width), BF),
        jax.ShapeDtypeStruct((width, tok), BF),
        jax.ShapeDtypeStruct((1, width), F32),
    )
    return pl.pallas_call(
        functools.partial(turn_back_kernel, len(stacks)),
        out_shape=outs,
        in_specs=[SCALARS] + [VMEM] * 7 + [ANYWHERE] * len(stacks),
        out_specs=(VMEM,) * 4,
        scratch_shapes=[
            pltpu.VMEM((count(stacks),) + stacks[0].shape[1:], BF),
            pltpu.SemaphoreType.DMA((count(stacks),)),
        ],
        compiler_params=pltpu.CompilerParams(vmem_limit_bytes=12 * 2**20),
        cost_estimate=SMALL,
    )(
        scalars(where), kept, came_near, came_far, middle, inverse, gains, cotangent, *stacks
    )


def emit(total, order, held, sent_ref, kept_ref):
    held[...] = total.reshape(held.shape)
    half = sent_ref.shape[0]
    first = sent_ref.shape[2] - total.shape[1]
    for k in range(half):
        kept_ref[k, :, first:] = held[order[k]].astype(BF)
        sent_ref[k, :, first:] = held[order[half + k]].astype(BF)


def outer_kernel(order, left_ref, right_ref, sent_ref, kept_ref, held):
    emit(dims(left_ref[...], right_ref[...], 0, 0), order, held, sent_ref, kept_ref)


def blocks_out(order, width, columns):
    half = len(order) // 2
    rows = width // len(order)
    out = jax.ShapeDtypeStruct((half, rows, columns), BF)
    return out, pltpu.VMEM((len(order), rows, columns), F32)


def outer_blocks(order, left, right):
    tok, width = left.shape
    columns = right.shape[1]
    out, held = blocks_out(order, width, columns)
    return pl.pallas_call(
        outer_kernel,
        out_shape=(out, out),
        in_specs=[SCALARS, VMEM, VMEM],
        out_specs=(VMEM, VMEM),
        scratch_shapes=[held],
        compiler_params=pltpu.CompilerParams(vmem_limit_bytes=10 * 2**20),
        cost_estimate=SMALL,
    )(scalars(order), left, right)


def unturn(value, cosine, sine):
    half = DH // 2
    one, two = value[:half], value[half:]
    return [one * cosine + two * sine, two * cosine - one * sine]


def query_end_kernel(
    order, qmix_ref, qbasis_ref, cos_ref, sin_ref, hidden_ref, weights_ref, *refs
):
    part_ref, outs = refs[0], refs[1:]
    cosine, sine = cos_ref[...], sin_ref[...]
    parts = []
    for r in range(RQ):
        parts += unturn(qbasis_ref[r * DH : (r + 1) * DH, :], cosine, sine)
    tok = cosine.shape[1]
    parts += [qmix_ref[...], jnp.zeros((LEFT - QB - QM, tok), F32)]
    slopes = jnp.concatenate(parts, 0).astype(BF)
    weights = weights_ref[...].reshape(hidden_ref.shape[1], PACKED)[:, :LEFT]
    part_ref[...] = dims(slopes, weights, 0, 1)
    total = dims(hidden_ref[...], slopes, 0, 1)
    if len(outs) == 1:
        outs[0][...] = total.astype(BF)
    else:
        emit(total, order, outs[2], outs[0], outs[1])


def query_end(order, qmix, qbasis, cosine, sine, hidden, weights):
    tok, width = hidden.shape
    outs = [jax.ShapeDtypeStruct((tok, width), F32)]
    scratch = []
    if len(order) > 1:
        out, held = blocks_out(order, width, LEFT)
        outs += [out, out]
        scratch = [held]
    else:
        outs += [jax.ShapeDtypeStruct((width, LEFT), BF)]
    return pl.pallas_call(
        query_end_kernel,
        out_shape=tuple(outs),
        in_specs=[SCALARS] + [VMEM] * 6,
        out_specs=(VMEM,) * len(outs),
        scratch_shapes=scratch,
        compiler_params=pltpu.CompilerParams(vmem_limit_bytes=12 * 2**20),
        cost_estimate=SMALL,
    )(scalars(order), qmix, qbasis, cosine, sine, hidden, weights)


def key_end_kernel(
    order,
    kept_ref,
    came_ref,
    cos_ref,
    sin_ref,
    hidden_ref,
    weights_ref,
    part_ref,
    tokens_ref,
    inverse_ref,
    gains_ref,
    middle_ref,
    feed_gain_ref,
    *refs
):
    if order.shape[0] > 1:
        query_sent, query_kept, out_ref, away_ref, stay_ref, held = refs
        away_ref[:, :, :LEFT] = query_sent[...]
        stay_ref[:, :, :LEFT] = query_kept[...]
    else:
        out_ref, total_ref = refs
    cosine, sine = cos_ref[...], sin_ref[...]
    own = kept_ref[...] + came_ref[...].astype(F32)
    parts = []
    for r in range(RK):
        parts += unturn(own[KM + r * DH : KM + (r + 1) * DH], cosine, sine)
    tok, width = hidden_ref.shape
    parts += [own[2 * KM + KB :], own[:KM], own[KM + KB : 2 * KM + KB]]
    parts += [jnp.zeros((PACKED - GAINS, tok), F32)]
    slopes = jnp.concatenate(parts, 0).astype(BF)
    weights = weights_ref[...].reshape(width, PACKED)[:, LEFT:]
    slope = part_ref[...] + dims(slopes, weights, 0, 1)
    inverse = inverse_ref[...]
    normed = tokens_ref[...].astype(F32) * inverse
    scaled = slope * gains_ref[0:1, :]
    mean = jnp.mean(scaled * normed, -1, keepdims=True)
    out_ref[...] = middle_ref[...] + inverse * (scaled - normed * mean)
    gain_slope = jnp.sum(slope * normed, 0, keepdims=True)
    total = dims(hidden_ref[...], slopes, 0, 1)
    rows = jnp.concatenate(
        [gain_slope, feed_gain_ref[...], jnp.zeros((PACKED - GAINS - 2, width), F32)], 0
    )
    columns = jnp.concatenate([jnp.zeros((128 - rows.shape[0], width), F32), rows], 0).T
    total = jnp.concatenate([total[:, :-128], total[:, -128:] + columns], 1)
    if order.shape[0] > 1:
        emit(total, order, held, away_ref, stay_ref)
    else:
        total_ref[...] = total.astype(BF)


def key_end(order, *args):
    tok, width = args[4].shape
    outs = [jax.ShapeDtypeStruct((tok, width), F32)]
    scratch = []
    if len(order) > 1:
        _, held = blocks_out(order, width, PACKED - LEFT)
        out, _ = blocks_out(order, width, PACKED)
        outs += [out, out]
        scratch = [held]
    else:
        outs += [jax.ShapeDtypeStruct((width, PACKED - LEFT), BF)]
    return pl.pallas_call(
        key_end_kernel,
        out_shape=tuple(outs),
        in_specs=[SCALARS] + [VMEM] * len(args),
        out_specs=(VMEM,) * len(outs),
        scratch_shapes=scratch,
        compiler_params=pltpu.CompilerParams(vmem_limit_bytes=14 * 2**20),
        cost_estimate=SMALL,
    )(scalars(order), *args)


def key_parts(kv_ref, head, at):
    base = at + H * RK
    row = at + head * RK
    total = kv_ref[pl.ds(row, 1), :] * kv_ref[base : base + DH, :]
    total = total + kv_ref[pl.ds(row + 1, 1), :] * kv_ref[base + DH : base + 2 * DH, :]
    return (total * (1.0 / RK)).astype(BF)


def query_parts(qm_ref, qt_ref, head):
    total = qm_ref[pl.ds(head * RQ, 1), :] * qt_ref[0:DH, :]
    for r in range(1, RQ):
        total = total + qm_ref[pl.ds(head * RQ + r, 1), :] * qt_ref[r * DH : (r + 1) * DH, :]
    queries = (total * (1.0 / RQ)).astype(BF)
    return (queries.astype(F32) * DH**-0.5).astype(BF)


def attend_kernel(
    place_ref, qm_ref, qt_ref, k0, k1, k2, k3, attended_ref, probs_ref, kv_ref, bias
):
    pair = pl.program_id(0)
    tok, slots = bias.shape

    @pl.when(pair == 0)
    def _():
        for block, part in enumerate((k0, k1, k2, k3)):
            kv_ref[:, block * tok : (block + 1) * tok] = part[...].astype(F32)
        near, length = place_ref[0], place_ref[1]
        rows = near * tok + lax.broadcasted_iota(jnp.int32, (tok, tok), 0)
        for block, bit in enumerate((0, 2, 1, 3)):
            keys = (near ^ bit) * tok + lax.broadcasted_iota(jnp.int32, (tok, tok), 1)
            allowed = (keys <= rows) & (keys < length)
            bias[:, block * tok : (block + 1) * tok] = jnp.where(allowed, 0.0, NEG)

    outs = []
    for inner in range(PAIR):
        head = pair * PAIR + inner
        keys = key_parts(kv_ref, head, 0)
        values = key_parts(kv_ref, head, H * RK + RK * DH)
        queries = query_parts(qm_ref, qt_ref, head)
        scores = dims(queries, keys, 0, 0) + bias[...]
        peak = jnp.max(scores, -1, keepdims=True)
        powers = jnp.exp(scores - peak)
        total = jnp.sum(powers, -1, keepdims=True)
        probs = (powers * (1.0 / total)).astype(BF)
        probs_ref[inner] = probs
        outs.append(dims(probs, values, 1, 1))
    attended_ref[...] = jnp.concatenate(outs, 1).astype(BF)


def attend(places, query_mix, query_turned, factors):
    tok = query_mix.shape[1]
    slots = 4 * tok
    table = pltpu.HBM((factors[0].shape[0], slots), F32)
    return pl.pallas_call(
        attend_kernel,
        grid=(H // PAIR,),
        out_shape=(
            jax.ShapeDtypeStruct((tok, H * DH), BF),
            pltpu.HBM((H, tok, slots), BF),
            table,
        ),
        in_specs=[SCALARS, whole(query_mix), whole(query_turned)] + [whole(f) for f in factors],
        out_specs=(
            pl.BlockSpec((tok, PAIR * DH), lambda i: (0, i)),
            pl.BlockSpec((PAIR, tok, slots), lambda i: (i, 0, 0)),
            whole(table),
        ),
        scratch_shapes=[pltpu.VMEM((tok, slots), F32)],
        compiler_params=pltpu.CompilerParams(vmem_limit_bytes=16 * 2**20),
        cost_estimate=SMALL,
    )(places, query_mix, query_turned, *pinned(*factors))


def attend_back_kernel(*refs):
    qm_ref, qt_ref, kv_ref, slope_ref, probs_all = refs[:5]
    kept_ref, sent_ref, qmix_ref, qbasis_ref, mix_ref, basis_ref, probs_held, psem = refs[5:]
    pair = pl.program_id(0)
    vm = H * RK + RK * DH
    kb = RK * DH

    def coming(at):
        return pltpu.make_async_copy(
            probs_all.at[pl.ds(at * PAIR, PAIR)], probs_held.at[at % 2], psem.at[at % 2]
        )

    @pl.when(pair == 0)
    def _():
        coming(pair).start()
        basis_ref[...] = jnp.zeros_like(basis_ref)
        qbasis_ref[...] = jnp.zeros_like(qbasis_ref)

    @pl.when(pair + 1 < pl.num_programs(0))
    def _():
        coming(pair + 1).start()

    coming(pair).wait()
    probs_ref = probs_held.at[pair % 2]
    for inner in range(PAIR):
        head = pair * PAIR + inner
        keys = key_parts(kv_ref, head, 0)
        values = key_parts(kv_ref, head, vm)
        queries = query_parts(qm_ref, qt_ref, head)
        slope = slope_ref[inner * DH : (inner + 1) * DH, :]
        probs_low = probs_ref[inner]
        slope_probs = dims(slope, values, 0, 0)
        probs = probs_low.astype(F32)
        weighted = probs * slope_probs
        total = jnp.sum(weighted, -1, keepdims=True)
        slope_scores = (weighted - probs * total).astype(BF)
        slope_query = dims(keys, slope_scores, 1, 1) * (DH**-0.5 / RQ)
        slope_key = dims(queries, slope_scores, 1, 0) * (1.0 / RK)
        slope_value = dims(slope, probs_low, 1, 0) * (1.0 / RK)
        for r in range(RK):
            row = head * RK + r
            for at, piece, side in ((0, slope_key, 0), (vm, slope_value, 1)):
                base = at + H * RK + r * DH
                here = side * RK + r
                basis_ref[here * DH : (here + 1) * DH, :] += kv_ref[pl.ds(at + row, 1), :] * piece
                mix_ref[pl.ds(side * H * RK + row, 1), :] = jnp.sum(
                    piece * kv_ref[base : base + DH, :], 0, keepdims=True
                )
        for r in range(RQ):
            row = head * RQ + r
            cut = slice(r * DH, (r + 1) * DH)
            qbasis_ref[cut, :] += qm_ref[pl.ds(row, 1), :] * slope_query
            qmix_ref[pl.ds(row, 1), :] = jnp.sum(slope_query * qt_ref[cut, :], 0, keepdims=True)

    @pl.when(pair == pl.num_programs(0) - 1)
    def _():
        half = kept_ref.shape[2] * 2
        tok = kept_ref.shape[2]
        km = H * RK
        for base, ref, begin, rows in (
            (0, mix_ref, 0, km),
            (km, basis_ref, 0, kb),
            (vm, mix_ref, km, km),
            (vm + km, basis_ref, kb, kb),
        ):
            part = ref[begin : begin + rows, :]
            for block in range(2):
                kept_ref[block, base : base + rows, :] = part[:, block * tok : (block + 1) * tok]
                sent_ref[block, base : base + rows, :] = part[
                    :, half + block * tok : half + (block + 1) * tok
                ].astype(BF)


def attend_back(query_mix, query_turned, row_factors, slope_attended, probs):
    tok = query_mix.shape[1]
    rows, slots = row_factors.shape
    outs = (
        jax.ShapeDtypeStruct((2, rows, tok), F32),
        jax.ShapeDtypeStruct((2, rows, tok), BF),
        jax.ShapeDtypeStruct((H * RQ, tok), F32),
        jax.ShapeDtypeStruct((RQ * DH, tok), F32),
    )
    return pl.pallas_call(
        attend_back_kernel,
        grid=(H // PAIR,),
        out_shape=outs,
        in_specs=[
            whole(query_mix),
            whole(query_turned),
            whole(row_factors),
            pl.BlockSpec((PAIR * DH, tok), lambda i: (i, 0)),
            pl.BlockSpec(memory_space=pltpu.HBM),
        ],
        out_specs=tuple(whole(o) for o in outs),
        scratch_shapes=[
            pltpu.VMEM((2 * H * RK, slots), F32),
            pltpu.VMEM((2 * RK * DH, slots), F32),
            pltpu.VMEM((2, PAIR, tok, slots), BF),
            pltpu.SemaphoreType.DMA((2,)),
        ],
        compiler_params=pltpu.CompilerParams(vmem_limit_bytes=18 * 2**20),
        cost_estimate=SMALL,
    )(query_mix, query_turned, *pinned(row_factors), slope_attended, *pinned(probs))


QB, KB, VB = RQ * DH, RK * DH, RK * DH
QM, KM, VM = H * RQ, H * RK, H * RK
LEFT = 512
GAINS = LEFT + KB + VB + KM + VM
PACKED = 896


def steps_of_any_mesh(
    tokens, places, cosine, sine, packed, merge_weight, both, down_weight, cotangent
):
    tok, width = tokens.shape
    group, twice, hidden = both.shape
    rows = twice // 2
    cut = down_weight.shape[0]
    axes = ("wide", "narrow")
    packed = [lax.all_gather(packed, axes, axis=0, tiled=True)[None]]
    merge = [lax.all_gather(merge_weight, axes, axis=0, tiled=True)[None]]
    downs = [lax.all_gather(down_weight, "wide", axis=0, tiled=True)[None]]
    both = lax.all_to_all(both, "narrow", 0, 0, tiled=True)
    both = lax.all_gather(both, "wide", axis=0, tiled=False)
    both = both.reshape(-1, 2, rows, hidden).transpose(1, 0, 2, 3)
    both = both.reshape(2, 8, 4, width // 32, hidden).transpose(1, 2, 0, 3, 4)
    weights_in = ([both.reshape(8, 4, width // 16, hidden)], list(range(8)), downs, [0])

    hidden_one, inverse_one, gains, weights, query_mix, query_turned, own_factors = project(
        tokens, cosine, sine, packed, [0]
    )
    attended, probs, row_factors = attend(
        places, query_mix, query_turned, gather_narrow(own_factors)
    )
    hidden_two, middle, inverse_two = middle_of(attended, tokens, gains, merge, [0])
    own, far, close, cross = gather_narrow(hidden_two)
    cot_own, cot_far, cot_near, cot_cross = gather_narrow(cotangent)
    parts = [
        feed((own, close), (cot_own, cot_near), *weights_in),
        feed((far, cross), (cot_far, cot_cross), *weights_in),
    ]
    hidden_feed, slope_gate, slope_up = zip(*(part[:3] for part in parts))
    came_near = flip(parts[0][4], "narrow", 1)
    came_far = flip(add_low(parts[1][3], flip(parts[1][4], "narrow", 1)), "narrow", 2)
    full = slopes_of((own, close, far, cross), slope_gate, slope_up, list(range(width // 128)))
    full = full.transpose(1, 0, 3, 2).reshape(2, width, hidden)
    slopes = jnp.concatenate([scatter_wide(s).reshape(group, rows, hidden) for s in full], 1)
    slopes = lax.all_to_all(slopes.astype(BF), "narrow", 0, 0, tiled=True)
    cots = (cot_own, cot_near, cot_far, cot_cross)
    down_slope = scatter_wide(down_slopes(hidden_feed, cots, [0], cut)[0])
    kept, sent = feed_out(hidden_feed, downs, [0])
    fed = kept + flip(sent, "narrow", 1).astype(F32)
    fed = fed[0] + flip(fed[1].astype(BF), "narrow", 2).astype(F32)
    output = (middle + fed).astype(BF)

    slope_middle, slope_low, slope_attended, feed_gain_slope = turn_back(
        parts[0][3], came_near, came_far, middle, inverse_two, gains, cotangent, merge, [0]
    )
    merge_slope = scatter_all(dims(attended, slope_low, 0, 0).astype(BF))
    factors_in = (query_mix, query_turned, row_factors, slope_attended, probs)
    key_kept, key_sent, query_mix_slope, query_basis_slope = attend_back(*factors_in)
    key_pair = key_kept + flip(key_sent, "narrow", 1).astype(F32)
    key_came = flip(key_pair[1].astype(BF), "narrow", 2)
    part, query_slopes = query_end(
        [0], query_mix_slope, query_basis_slope, cosine, sine, hidden_one, weights
    )
    tokens_slope, key_slopes = key_end(
        [0], key_pair[0], key_came, cosine, sine, hidden_one, weights, part, tokens, inverse_one,
        gains, slope_middle, feed_gain_slope,
    )
    query_slopes, key_slopes = scatter_all(query_slopes), scatter_all(key_slopes)
    return output, tokens_slope, query_slopes, key_slopes, merge_slope, slopes, down_slope


def steps_of_small_mesh(
    tokens, places, cosine, sine, packed, merge_weight, both_in, down_weight, cotangent
):
    tok, width = tokens.shape
    cut = down_weight.shape[0]
    high, low = wide_place()
    rounds = lax.axis_size("wide") // 2
    group = lax.axis_size("narrow")
    join = lambda a, b: jnp.concatenate([a, b], 0)

    first, both_in = tie(jnp.concatenate([packed, merge_weight], 1)[None], both_in)
    first = turned(first)
    both = lax.all_to_all(both_in, "narrow", 0, 0, tiled=True)
    first = tie(*first)
    one = jnp.concatenate([f[:, :, :PACKED] for f in first], 0)
    two = jnp.concatenate([f[:, :, PACKED:] for f in first], 0)
    one, one_came, two, two_came, both = tie(
        one, flip(one, "narrow", 2), two, flip(two, "wide", 1), both
    )
    one, two = join(one, one_came), join(two, two_came)
    pieces = [both[None]]
    one, one_came, two, two_came, piece = tie(
        one, flip(one, "wide", 1), two, flip(two, "narrow", 2), turn(pieces[0], 1)
    )
    one, two = join(one, one_came), join(two, two_came)
    where, merge_where = relative_blocks(), relative_blocks(True)
    both_where = [((high - k) % rounds) * 2 + low for k in range(rounds)] + [
        ((high - k) % rounds) * 2 + 1 - low for k in range(rounds)
    ]
    one, piece, down_own, first = tie(one, piece, down_weight, pieces[0])
    pieces += [piece, turn(piece, 1)]
    down_came = flip(down_own, "wide", 1)
    others = [flip(first, "wide", 1)]
    hidden_one, inverse_one, gains, weights, query_mix, query_turned, factor = project(
        tokens, cosine, sine, [one, flip(one, "narrow", 1)], where
    )
    factor, two, first, down_came = tie(factor, two, pieces[1], down_came)
    merge = [two, flip(two, "narrow", 1)]
    others.append(flip(first, "wide", 1))
    factor_far, factor_near, pieces[2], others[0], down_came = tie(
        flip(factor, "narrow", 2), flip(factor, "narrow", 1), pieces[2], others[0], down_came
    )
    pieces.append(turn(pieces[2], 1))
    pair = jnp.where(low == 0, jnp.stack([down_own, down_came]), jnp.stack([down_came, down_own]))
    pair = jnp.stack([pair.reshape(2 * cut, width)] * rounds)
    factor_cross, cot_own, first, pieces[3], others[1], pair = tie(
        flip(factor_far, "narrow", 1), cotangent, pieces[2], pieces[3], others[1], pair
    )
    downs = [ring_all_to_all(pair)]
    down_where = list(range(rounds))

    cot_far = flip(cot_own, "narrow", 2)
    others += [flip(first, "wide", 1), flip(pieces[3], "wide", 1)]
    attended, probs, row_factors = attend(
        places, query_mix, query_turned, (factor, factor_far, factor_near, factor_cross)
    )
    attended, cot_far, others[2], others[3], merge[1] = tie(
        attended, cot_far, others[2], others[3], merge[1]
    )
    hidden_two, middle, inverse_two = middle_of(attended, tokens, gains, merge, merge_where)
    own, cot_far = tie(hidden_two, cot_far)

    far, close = flip(own, "narrow", 2), flip(own, "narrow", 1)
    cot_near, cot_cross = flip(cot_own, "narrow", 1), flip(cot_far, "narrow", 1)
    weights_in = (pieces + others, both_where, downs, down_where)
    one = feed((own, close), (cot_own, cot_near), *weights_in)
    far, one_sent = tie(far, one[4])
    came_near = flip(one_sent, "narrow", 1)
    cross = flip(far, "narrow", 1)
    two = feed((far, cross), (cot_far, cot_cross), *weights_in)
    for_far = add_low(two[3], flip(two[4], "narrow", 1))
    hidden_feed, slope_gate, slope_up = zip(one[:3], two[:3])
    for_far, slope_gate, slope_up, came_near = tie(for_far, slope_gate, slope_up, came_near)
    came_far = flip(for_far, "narrow", 2)
    slots = (own, close, far, cross)
    cots = (cot_own, cot_near, cot_far, cot_cross)
    order = [2 * k + 1 - low for k in range(rounds)]
    to_send = slopes_of(slots, slope_gate, slope_up, order, True)
    *hidden_feed, gate_sent, up_sent = tie(*hidden_feed, *to_send)
    gate_came = flip(gate_sent, "wide", 1)
    down_order = [
        2 * ((high + k) % rounds) + side for k in range(rounds) for side in (low, 1 - low)
    ]
    down_sent, down_kept = down_slopes(hidden_feed, cots, down_order, cut)
    slope_gate, slope_up, down_sent = tie(slope_gate, slope_up, down_sent)
    to_keep = slopes_of(slots, slope_gate, slope_up, [2 * k + low for k in range(rounds)])
    came_far, to_keep = tie(came_far, to_keep)

    slope_middle, slope_low, slope_attended, feed_gain_slope = turn_back(
        one[3], came_near, came_far, middle, inverse_two, gains, cotangent, merge, merge_where
    )
    merge_sent, merge_kept = outer_blocks(scatter_order(True), attended, slope_low)
    merge_sent, slope_attended, gate_came, up_sent = tie(
        merge_sent, slope_attended, gate_came, up_sent
    )
    up_came = flip(up_sent, "wide", 1)
    merge_came = flip(merge_sent, "narrow", 1)
    merge_sum = add_low(merge_kept, merge_came)
    slope_attended, merge_sum, down_sent = tie(slope_attended, merge_sum, down_sent)
    merge_came = flip(merge_sum[8:], "narrow", 2)
    key_kept, key_sent, query_mix_slope, query_basis_slope = attend_back(
        query_mix, query_turned, row_factors, slope_attended, probs
    )
    key_kept, key_sent, query_basis_slope, merge_came, up_came, down_sent = tie(
        key_kept, key_sent, query_basis_slope, merge_came, up_came, down_sent
    )
    key_came = flip(key_sent, "narrow", 1)
    down_came = flip(down_sent, "wide", 1)
    merge_sum = add_low(merge_sum[:8], merge_came)
    key_came, merge_sum = tie(key_came, merge_sum)
    key_pair = key_kept + key_came.astype(F32)
    key_far, up_came, query_basis_slope, merge_sum = tie(
        key_pair[1].astype(BF), up_came, query_basis_slope, merge_sum
    )
    key_came = flip(key_far, "narrow", 2)
    parts = ring_all_to_all(add_low(to_keep, jnp.stack([gate_came, up_came], 1)))
    merge_came = flip(merge_sum[4:], "wide", 1)
    order = scatter_order(True)
    part, query_sent, query_kept = query_end(
        order, query_mix_slope, query_basis_slope, cosine, sine, hidden_one, weights
    )
    key_came, part = tie(key_came, part)
    tokens_slope, ends_sent, ends = key_end(
        order, key_pair[0], key_came, cosine, sine, hidden_one, weights, part, tokens, inverse_one,
        gains, slope_middle, feed_gain_slope, query_sent, query_kept,
    )

    ends = add_low(ends, flip(ends_sent, "narrow", 1))
    ends, hidden_feed = tie(ends, hidden_feed)
    ends_came = flip(ends[8:], "narrow", 2)
    kept, sent = feed_out(hidden_feed, downs, down_where)
    ends_came, kept, sent = tie(ends_came, kept, sent)
    ends = add_low(ends[:8], ends_came)
    ends, sent, down_came, parts = tie(ends, sent, down_came, parts)
    ends_came = flip(ends[4:], "wide", 1)
    fed = kept + flip(sent, "narrow", 1).astype(F32)
    slopes = lax.all_to_all(finish(parts, group), "narrow", 0, 0, tiled=True)
    merge_sum = add_low(merge_sum[:4], merge_came)
    down_sum = add_low(down_kept, down_came)
    ends_came, fed, merge_sum, down_sum = tie(ends_came, fed, merge_sum, down_sum)
    ends = jnp.concatenate([add_low(ends[:4], ends_came), merge_sum], 2)
    ends, fed_far, down_sum = tie(ends, fed[1].astype(BF), down_sum)
    sums = spread_turns(ends)
    slopes = after(slopes, sums)
    fed_came = flip(fed_far, "narrow", 2)
    down_slope = spread_turns(down_sum)
    merge_slope = sums[:, PACKED:]
    output = (middle + fed[0] + fed_came.astype(F32)).astype(BF)
    query_slopes, key_slopes = sums[:, :LEFT], sums[:, LEFT:PACKED]
    return output, tokens_slope, query_slopes, key_slopes, merge_slope, slopes, down_slope


def per_device(
    tokens,
    lengths,
    attend_gain,
    query_heads,
    query_basis,
    key_heads,
    key_basis,
    value_heads,
    value_basis,
    merge_weight,
    feed_gain,
    gate_weight,
    up_weight,
    down_weight,
    cotangent,
):
    tok, width = tokens.shape
    wide_count = lax.axis_size("wide")
    narrow_count = lax.axis_size("narrow")
    near = lax.axis_index("narrow")
    rows = gate_weight.shape[0]
    cut = down_weight.shape[0]
    hidden = cut * wide_count
    small = small_mesh()

    positions = (near * tok + jnp.arange(tok, dtype=jnp.int32)).astype(F32)
    frequency = jnp.power(10000.0, -2.0 * jnp.arange(DH // 2, dtype=F32) / DH)
    angles = frequency[:, None] * positions[None, :]
    cosine, sine = jnp.cos(angles), jnp.sin(angles)

    packed = jnp.concatenate(
        [
            query_basis,
            query_heads,
            jnp.zeros((rows, LEFT - QB - QM), BF),
            key_basis,
            value_basis,
            key_heads,
            value_heads,
            attend_gain[:, None],
            feed_gain[:, None],
            jnp.zeros((rows, PACKED - GAINS - 2), BF),
        ],
        1,
    )

    def columns(weight):
        parts = weight.reshape(rows, wide_count, narrow_count, cut).transpose(2, 0, 1, 3)
        return parts.reshape(narrow_count, rows, hidden)

    both_in = jnp.concatenate([columns(gate_weight), columns(up_weight)], 1)
    places = jnp.stack([near.astype(jnp.int32), lengths[0].astype(jnp.int32)])
    if small:
        exact = steps_of_small_mesh
    else:
        exact = steps_of_any_mesh
    output, tokens_slope, query_slopes, key_slopes, merge_slope, slopes, down_slope = exact(
        tokens, places, cosine, sine, packed, merge_weight, both_in, down_weight, cotangent
    )
    if small:
        slopes = unmix(slopes, cut)
    else:
        slopes = slopes.reshape(narrow_count, 2, rows, wide_count, cut).transpose(1, 2, 3, 0, 4)
        slopes = slopes.reshape(2, rows, hidden * narrow_count).astype(F32)

    base = GAINS - LEFT
    return (
        output,
        tokens_slope,
        key_slopes[:, base],
        query_slopes[:, QB : QB + QM],
        query_slopes[:, :QB],
        key_slopes[:, KB + VB : KB + VB + KM],
        key_slopes[:, :KB],
        key_slopes[:, KB + VB + KM : KB + VB + KM + VM],
        key_slopes[:, KB : KB + VB],
        merge_slope,
        key_slopes[:, base + 1],
        slopes[0],
        slopes[1],
        down_slope,
    )


def solution(mesh):
    both = ("wide", "narrow")
    row, vector = P(both, None), P(both)
    return jax.shard_map(
        per_device,
        mesh=mesh,
        in_specs=(row, P("wide"), vector) + (row,) * 7 + (vector,) + (row,) * 4,
        out_specs=(row, row, vector) + (row,) * 7 + (vector,) + (row,) * 3,
        check_vma=False,
    )
```

```python
import functools

import jax
import jax.numpy as jnp
from jax import lax
from jax.experimental import pallas as pl
from jax.experimental.pallas import tpu as pltpu
from jax.sharding import PartitionSpec as P

H = 16
DH = 64
RQ = 6
RK = 2
PAIR = 2
EPS = 1e-06
NEG = -1e30
BF = jnp.bfloat16
F32 = jnp.float32


def dims(left, right, left_dim, right_dim):
    return lax.dot_general(
        left, right, (((left_dim,), (right_dim,)), ((), ())), preferred_element_type=F32
    )


def flip(value, axis, bit):
    size = lax.axis_size(axis)
    return lax.ppermute(value, axis, [(i, i ^ bit) for i in range(size)])


def turn(value, steps):
    size = lax.axis_size("wide")
    return lax.ppermute(value, "wide", [(i, (i + 2 * steps) % size) for i in range(size)])


def small_mesh():
    return lax.axis_size("wide") == 8 and lax.axis_size("narrow") == 4


def wide_place():
    me = lax.axis_index("wide")
    return me // 2, me % 2


def tie(*values):
    return lax.optimization_barrier(values)


def after(value, *others):
    return lax.optimization_barrier((value, others))[0]


def ring_groups():
    size = lax.axis_size("wide")
    return [list(range(x, size, 2)) for x in range(2)]


def ring_all_to_all(value):
    return lax.all_to_all(value, "wide", 0, 0, axis_index_groups=ring_groups(), tiled=True)


def pick(value, index, axis):
    return lax.dynamic_index_in_dim(value, index, axis, keepdims=False)


def spread_high(blocks):
    return jnp.sum(ring_all_to_all(blocks).astype(F32), 0)


def scatter_wide(value):
    return lax.psum_scatter(value, "wide", scatter_dimension=0, tiled=True).astype(F32)


def turned(value):
    rounds = lax.axis_size("wide") // 2
    return [value] + [turn(value, k) for k in range(1, rounds)]


def joined(value, axis, bit):
    return jnp.concatenate([value, flip(value, axis, bit)], 0)


def relative_blocks(swapped=False):
    high, low = wide_place()
    rounds = lax.axis_size("wide") // 2
    near = lax.axis_index("narrow")
    return [
        (((high - k) % rounds) * 2 + (low ^ x)) * 4 + (near ^ (2 * y) ^ c)
        for c in (0, 1)
        for x, y in ([(0, 0), (1, 0), (0, 1), (1, 1)] if swapped else [(0, 0), (0, 1), (1, 0), (1, 1)])
        for k in range(rounds)
    ]


def scatter_all(value):
    return lax.psum_scatter(value, ("wide", "narrow"), scatter_dimension=0, tiled=True).astype(F32)


def scatter_order(turning):
    high, low = wide_place()
    rounds = lax.axis_size("wide") // 2
    near = lax.axis_index("narrow")
    return [
        (((high + k) % rounds if turning else k) * 2 + (low ^ x)) * 4 + (near ^ (2 * y) ^ c)
        for c in (0, 1)
        for y in (0, 1)
        for x in (0, 1)
        for k in range(rounds)
    ]


def spread_turns(blocks):
    total = blocks[0].astype(F32)
    for k in range(1, blocks.shape[0]):
        total = total + turn(blocks[k], k).astype(F32)
    return total


def add_low(kept, came):
    return (kept.astype(F32) + came.astype(F32)).astype(BF)


def gather_narrow(value):
    far = flip(value, "narrow", 2)
    return [value, far, flip(value, "narrow", 1), flip(far, "narrow", 1)]


def starts(stacks, where_ref, first, target, sem):
    copies = []
    for stack in stacks:
        for k in range(stack.shape[0]):
            at = len(copies)
            copies.append(
                pltpu.make_async_copy(
                    stack.at[k], target.at[where_ref[first + at]], sem.at[first + at]
                )
            )
            copies[-1].start()
    return copies


def count(stacks):
    return sum(stack.shape[0] for stack in stacks)


def whole(array):
    return pl.BlockSpec(array.shape, lambda *i: (0,) * len(array.shape))


ANYWHERE = pl.BlockSpec(memory_space=pl.ANY)


def pinned(*arrays):
    return [pltpu.with_memory_space_constraint(a, pltpu.HBM) for a in arrays]


SCALARS = pl.BlockSpec(memory_space=pltpu.SMEM)
SMALL = pl.CostEstimate(flops=3 * 10**9, bytes_accessed=2**22, transcendentals=0)


def scalars(*lists):
    return jnp.stack([jnp.asarray(v, jnp.int32) for one in lists for v in one])


def project_kernel(n, where, tokens_ref, cos_ref, sin_ref, *refs):
    packed, refs = refs[:n], refs[n:]
    hidden_ref, inverse_ref, gains_ref, packed_ref, qm_ref, qt_ref, kv_ref, sem = refs
    copies = starts(packed, where, 0, packed_ref, sem)
    source = tokens_ref[...].astype(F32)
    inverse = lax.rsqrt(jnp.mean(source * source, -1, keepdims=True) + EPS)
    inverse_ref[...] = inverse
    normed = source * inverse
    for copy in copies:
        copy.wait()
    width = source.shape[1]
    weights = packed_ref[...].reshape(width, PACKED)
    gains = weights[:, PACKED - 128 :].astype(F32).T
    at = GAINS - (PACKED - 128)
    gains_ref[...] = gains[at : at + 8]
    hidden = (normed * gains[at : at + 1]).astype(BF)
    hidden_ref[...] = hidden
    factors = dims(hidden, weights, 1, 0).T
    cosine, sine = cos_ref[...], sin_ref[...]
    half = DH // 2
    for r in range(RQ + RK):
        base = r * DH if r < RQ else LEFT + (r - RQ) * DH
        one = factors[base : base + half]
        two = factors[base + half : base + DH]
        a, b = one * cosine - two * sine, one * sine + two * cosine
        if r < RQ:
            qt_ref[base : base + half, :] = a
            qt_ref[base + half : base + DH, :] = b
        else:
            row = KM + (r - RQ) * DH
            kv_ref[row : row + half, :] = a.astype(BF)
            kv_ref[row + half : row + DH, :] = b.astype(BF)
    qm_ref[...] = factors[QB : QB + QM]
    base = LEFT + KB
    kv_ref[2 * KM + KB :, :] = factors[base : base + VB].astype(BF)
    base += VB
    kv_ref[0:KM, :] = factors[base : base + KM].astype(BF)
    kv_ref[KM + KB : 2 * KM + KB, :] = factors[base + KM : base + 2 * KM].astype(BF)


VMEM = pl.BlockSpec(memory_space=pltpu.VMEM)


def project(tokens, cosine, sine, packed, where):
    tok, width = tokens.shape
    outs = (
        jax.ShapeDtypeStruct((tok, width), BF),
        jax.ShapeDtypeStruct((tok, 1), F32),
        jax.ShapeDtypeStruct((8, width), F32),
        jax.ShapeDtypeStruct((count(packed),) + packed[0].shape[1:], BF),
        jax.ShapeDtypeStruct((QM, tok), F32),
        jax.ShapeDtypeStruct((QB, tok), F32),
        jax.ShapeDtypeStruct((2 * (KM + KB), tok), BF),
    )
    return pl.pallas_call(
        functools.partial(project_kernel, len(packed)),
        out_shape=outs,
        in_specs=[SCALARS] + [VMEM] * 3 + [ANYWHERE] * len(packed),
        out_specs=tuple(VMEM for _ in outs),
        scratch_shapes=[pltpu.SemaphoreType.DMA((count(packed),))],
        compiler_params=pltpu.CompilerParams(vmem_limit_bytes=14 * 2**20),
        cost_estimate=SMALL,
    )(scalars(where), tokens, cosine, sine, *packed)


def halves_of(both_ref, width, hidden):
    rows = both_ref.shape[2] // 2
    return (
        both_ref[:, :, :rows, :].reshape(width, hidden),
        both_ref[:, :, rows:, :].reshape(width, hidden),
    )


def feed_kernel(nb, nd, where, *refs):
    pieces, refs = refs[:2], refs[2:]
    cots, refs = refs[:2], refs[2:]
    boths, refs = refs[:nb], refs[nb:]
    downs, refs = refs[:nd], refs[nd:]
    hf_out, sg_out, su_out, kept_ref, sent_ref, hid, cot, wgu, wd, held, sem, psem, osem = refs
    outgoing = []
    width, hidden = hid.shape[2], wgu.shape[3]
    loads = [
        [
            pltpu.make_async_copy(pieces[b], hid.at[b], psem.at[b]),
            pltpu.make_async_copy(cots[b], cot.at[b], psem.at[2 + b]),
        ]
        for b in range(2)
    ]
    loads[0][0].start()
    in_both = starts(boths, where, 0, wgu, sem)
    loads[0][1].start()
    in_down = starts(downs, where, count(boths), wd, sem)
    for copy in loads[1]:
        copy.start()
    for b in range(2):
        loads[b][0].wait()
        if b == 0:
            for copy in in_both:
                copy.wait()
        gate_all, up_all = halves_of(wgu, width, hidden)
        gate = dims(hid[b], gate_all, 1, 0)
        upward = dims(hid[b], up_all, 1, 0)
        loads[b][1].wait()
        if b == 0:
            for copy in in_down:
                copy.wait()
        down_all = wd[...].reshape(hidden, width)
        slope = dims(cot[b], down_all, 1, 1)
        sig = jax.nn.sigmoid(gate)
        silu = gate * sig
        held[0, b] = (silu * upward).astype(BF)
        slope_up = (slope * silu).astype(BF)
        slope_gate = (slope * upward * sig * (1.0 + gate * (1.0 - sig))).astype(BF)
        held[1, b] = slope_gate
        held[2, b] = slope_up
        for k, out in enumerate((hf_out, sg_out, su_out)):
            outgoing.append(pltpu.make_async_copy(held.at[k, b], out.at[b], osem.at[k, b]))
            outgoing[-1].start()
        back = dims(slope_gate, gate_all, 1, 1) + dims(slope_up, up_all, 1, 1)
        if b == 0:
            kept_ref[...] = back
        else:
            sent_ref[...] = back.astype(BF)
    for copy in outgoing:
        copy.wait()


def feed(pieces, cots, boths, both_where, downs, down_where):
    tok, width = pieces[0].shape
    hidden = boths[0].shape[3]
    low = pltpu.HBM((2, tok, hidden), BF)
    outs = (
        low,
        low,
        low,
        jax.ShapeDtypeStruct((tok, width), F32),
        jax.ShapeDtypeStruct((tok, width), BF),
    )
    blocks = lambda stacks: pltpu.VMEM((count(stacks),) + stacks[0].shape[1:], BF)
    total = count(boths) + count(downs)
    return pl.pallas_call(
        functools.partial(feed_kernel, len(boths), len(downs)),
        out_shape=outs,
        in_specs=[SCALARS] + [ANYWHERE] * (4 + len(boths) + len(downs)),
        out_specs=(ANYWHERE,) * 3 + (VMEM,) * 2,
        scratch_shapes=[
            pltpu.VMEM((2, tok, width), BF),
            pltpu.VMEM((2, tok, width), BF),
            blocks(boths),
            blocks(downs),
            pltpu.VMEM((3, 2, tok, hidden), BF),
            pltpu.SemaphoreType.DMA((total,)),
            pltpu.SemaphoreType.DMA((4,)),
            pltpu.SemaphoreType.DMA((3, 2)),
        ],
        compiler_params=pltpu.CompilerParams(vmem_limit_bytes=20 * 2**20),
        cost_estimate=SMALL,
    )(scalars(both_where, down_where), *pinned(*pieces, *cots, *boths, *downs))


def bring(sources, target, sem):
    copies = []
    at = 0
    for source in sources:
        parts = [source] if len(source.shape) == 2 else [source.at[k] for k in range(source.shape[0])]
        for part in parts:
            copies.append(pltpu.make_async_copy(part, target.at[at], sem.at[at]))
            copies[-1].start()
            at += 1
    return copies


def slopes_kernel(blocks, order, *refs):
    *outs, hid, gates, ups, hsem, gsem, usem = refs[8:]
    out = outs[0]
    copies = bring(refs[:4], hid, hsem) + bring(refs[4:6], gates, gsem)
    later = bring(refs[6:8], ups, usem)
    for copy in copies:
        copy.wait()
    rows, hidden = out.shape[-1], out.shape[-2]
    columns = []
    for k in range(blocks):
        at = pl.multiple_of(order[k] * rows, 128)
        columns.append(hid[:, :, pl.ds(at, rows)].reshape(-1, rows))
    chosen = jnp.concatenate(columns, 1)
    for side, held in enumerate((gates, ups)):
        if side == 1:
            for copy in later:
                copy.wait()
        result = dims(held[...].reshape(-1, hidden), chosen, 0, 0).astype(BF)
        for k in range(blocks):
            part = result[:, k * rows : (k + 1) * rows]
            if len(outs) == 2:
                outs[side][k] = part
            else:
                out[k, side] = part


def slopes_of(pieces, slope_gate, slope_up, order, apart=False):
    tok, width = pieces[0].shape
    hidden = slope_gate[0].shape[2]
    rows = 128
    return pl.pallas_call(
        functools.partial(slopes_kernel, len(order)),
        out_shape=(jax.ShapeDtypeStruct((len(order), hidden, rows), BF),) * 2
        if apart
        else jax.ShapeDtypeStruct((len(order), 2, hidden, rows), BF),
        in_specs=[SCALARS] + [ANYWHERE] * 8,
        out_specs=(VMEM, VMEM) if apart else VMEM,
        scratch_shapes=[
            pltpu.VMEM((4, tok, width), BF),
            pltpu.VMEM((4, tok, hidden), BF),
            pltpu.VMEM((4, tok, hidden), BF),
        ]
        + [pltpu.SemaphoreType.DMA((4,))] * 3,
        compiler_params=pltpu.CompilerParams(vmem_limit_bytes=18 * 2**20),
        cost_estimate=SMALL,
    )(scalars(order), *pinned(*pieces, *slope_gate, *slope_up))


def down_kernel(blocks, order, *refs):
    feeds, cots, fsem, csem = refs[-4:]
    for copy in bring(refs[:2], feeds, fsem) + bring(refs[2:6], cots, csem):
        copy.wait()
    outs = refs[6:-4]
    hidden, width = feeds.shape[2], cots.shape[2]
    total = dims(feeds[...].reshape(-1, hidden), cots[...].reshape(-1, width), 0, 0)
    if blocks == 1:
        outs[0][...] = total.astype(BF)
    else:
        sent_ref, kept_ref, held = outs
        held[...] = total.reshape(held.shape)
        for k in range(blocks // 2):
            kept_ref[k] = held[order[2 * k]].astype(BF)
            sent_ref[k] = held[order[2 * k + 1]].astype(BF)


def down_slopes(hidden_feed, cots, order, cut):
    tok, width = cots[0].shape
    hidden = hidden_feed[0].shape[2]
    if len(order) > 1:
        out = jax.ShapeDtypeStruct((len(order) // 2, cut, width), BF)
        outs, scratch = (out, out), [pltpu.VMEM((len(order), cut, width), F32)]
    else:
        outs, scratch = (jax.ShapeDtypeStruct((hidden, width), BF),), []
    return pl.pallas_call(
        functools.partial(down_kernel, len(order)),
        out_shape=outs,
        in_specs=[SCALARS] + [ANYWHERE] * 6,
        out_specs=(VMEM,) * len(outs),
        scratch_shapes=scratch
        + [
            pltpu.VMEM((4, tok, hidden), BF),
            pltpu.VMEM((4, tok, width), BF),
            pltpu.SemaphoreType.DMA((4,)),
            pltpu.SemaphoreType.DMA((4,)),
        ],
        compiler_params=pltpu.CompilerParams(vmem_limit_bytes=20 * 2**20),
        cost_estimate=SMALL,
    )(scalars(order), *pinned(*hidden_feed, *cots))


def feed_out_kernel(nd, where, *refs):
    downs, (f0, f1, kept_ref, sent_ref, wd, feeds, sem, fsem) = refs[:nd], refs[nd:]
    for copy in starts(downs, where, 0, wd, sem) + bring((f0, f1), feeds, fsem):
        copy.wait()
    down_all = wd[...].reshape(feeds.shape[2], wd.shape[2])
    for part in range(2):
        kept_ref[part] = dims(feeds[2 * part], down_all, 1, 0)
        sent_ref[part] = dims(feeds[2 * part + 1], down_all, 1, 0).astype(BF)


def feed_out(hidden_feed, downs, down_where):
    tok, hidden = hidden_feed[0].shape[1:]
    width = downs[0].shape[2]
    return pl.pallas_call(
        functools.partial(feed_out_kernel, len(downs)),
        out_shape=(
            jax.ShapeDtypeStruct((2, tok, width), F32),
            jax.ShapeDtypeStruct((2, tok, width), BF),
        ),
        in_specs=[SCALARS] + [ANYWHERE] * (len(downs) + 2),
        out_specs=(VMEM, VMEM),
        scratch_shapes=[
            pltpu.VMEM((count(downs),) + downs[0].shape[1:], BF),
            pltpu.VMEM((4, tok, hidden), BF),
            pltpu.SemaphoreType.DMA((count(downs),)),
            pltpu.SemaphoreType.DMA((4,)),
        ],
        compiler_params=pltpu.CompilerParams(vmem_limit_bytes=14 * 2**20),
        cost_estimate=SMALL,
    )(scalars(down_where), *pinned(*downs, *hidden_feed))


def finish_kernel(parts_ref, out_ref):
    rows = out_ref.shape[1] // 2
    for side in range(2):
        total = parts_ref[0, side].astype(F32)
        for k in range(1, parts_ref.shape[0]):
            total = total + parts_ref[k, side].astype(F32)
        total = total.T.astype(BF)
        for n in range(out_ref.shape[0]):
            out_ref[n, side * rows : (side + 1) * rows, :] = total[n * rows : (n + 1) * rows]


def finish(parts, group):
    _, _, hidden, rows = parts.shape
    return pl.pallas_call(
        finish_kernel,
        out_shape=jax.ShapeDtypeStruct((group, 2 * rows // group, hidden), BF),
        in_specs=[VMEM],
        out_specs=VMEM,
        compiler_params=pltpu.CompilerParams(vmem_limit_bytes=8 * 2**20),
        cost_estimate=SMALL,
    )(parts)


def unmix_kernel(cut, x_ref, gate_ref, up_ref):
    group, rows, hidden = x_ref.shape
    rows //= 2
    for side, ref in ((0, gate_ref), (1, up_ref)):
        parts = [x_ref[n, side * rows : (side + 1) * rows, :].astype(F32) for n in range(group)]
        ref[...] = jnp.concatenate(
            [part[:, w * cut : (w + 1) * cut] for w in range(hidden // cut) for part in parts], 1
        )


def unmix(value, cut):
    group, rows, hidden = value.shape
    out = jax.ShapeDtypeStruct((rows // 2, group * hidden), F32)
    return pl.pallas_call(
        functools.partial(unmix_kernel, cut),
        out_shape=(out, out),
        in_specs=[VMEM],
        out_specs=(VMEM, VMEM),
        compiler_params=pltpu.CompilerParams(vmem_limit_bytes=8 * 2**20),
        cost_estimate=SMALL,
    )(value)


def middle_kernel(n, where, attended_ref, tokens_ref, gains_ref, *refs):
    stacks, (hidden_ref, middle_ref, inverse_ref, merge, sem) = refs[:n], refs[n:]
    for copy in starts(stacks, where, 0, merge, sem):
        copy.wait()
    width = tokens_ref.shape[1]
    full = merge[...].reshape(attended_ref.shape[1], width)
    middle = tokens_ref[...].astype(F32) + dims(attended_ref[...], full, 1, 0)
    inverse = lax.rsqrt(jnp.mean(middle * middle, -1, keepdims=True) + EPS)
    middle_ref[...] = middle
    inverse_ref[...] = inverse
    hidden_ref[...] = (middle * inverse * gains_ref[1:2, :]).astype(BF)


def middle_of(attended, tokens, gains, stacks, where):
    tok, width = tokens.shape
    outs = (
        jax.ShapeDtypeStruct((tok, width), BF),
        jax.ShapeDtypeStruct((tok, width), F32),
        jax.ShapeDtypeStruct((tok, 1), F32),
    )
    return pl.pallas_call(
        functools.partial(middle_kernel, len(stacks)),
        out_shape=outs,
        in_specs=[SCALARS] + [VMEM] * 3 + [ANYWHERE] * len(stacks),
        out_specs=(VMEM,) * 3,
        scratch_shapes=[
            pltpu.VMEM((count(stacks),) + stacks[0].shape[1:], BF),
            pltpu.SemaphoreType.DMA((count(stacks),)),
        ],
        compiler_params=pltpu.CompilerParams(vmem_limit_bytes=10 * 2**20),
        cost_estimate=SMALL,
    )(scalars(where), attended, tokens, gains, *stacks)


def turn_back_kernel(
    n, where, kept_ref, near_ref, far_ref, middle_ref, inverse_ref, gains_ref, cot_ref, *refs
):
    stacks, (slope_ref, low_ref, attended_ref, gain_ref, merge, sem) = refs[:n], refs[n:]
    copies = starts(stacks, where, 0, merge, sem)
    slope = kept_ref[...] + near_ref[...].astype(F32) + far_ref[...].astype(F32)
    inverse = inverse_ref[...]
    normed = middle_ref[...] * inverse
    gain_ref[...] = jnp.sum(slope * normed, 0, keepdims=True)
    scaled = slope * gains_ref[1:2, :]
    mean = jnp.mean(scaled * normed, -1, keepdims=True)
    slope_middle = cot_ref[...].astype(F32) + inverse * (scaled - normed * mean)
    slope_ref[...] = slope_middle
    low = slope_middle.astype(BF)
    low_ref[...] = low
    for copy in copies:
        copy.wait()
    full = merge[...].reshape(attended_ref.shape[0], low.shape[1])
    attended_ref[...] = dims(full, low, 1, 1).astype(BF)


def turn_back(kept, came_near, came_far, middle, inverse, gains, cotangent, stacks, where):
    tok, width = middle.shape
    outs = (
        jax.ShapeDtypeStruct((tok, width), F32),
        jax.ShapeDtypeStruct((tok, width), BF),
        jax.ShapeDtypeStruct((width, tok), BF),
        jax.ShapeDtypeStruct((1, width), F32),
    )
    return pl.pallas_call(
        functools.partial(turn_back_kernel, len(stacks)),
        out_shape=outs,
        in_specs=[SCALARS] + [VMEM] * 7 + [ANYWHERE] * len(stacks),
        out_specs=(VMEM,) * 4,
        scratch_shapes=[
            pltpu.VMEM((count(stacks),) + stacks[0].shape[1:], BF),
            pltpu.SemaphoreType.DMA((count(stacks),)),
        ],
        compiler_params=pltpu.CompilerParams(vmem_limit_bytes=12 * 2**20),
        cost_estimate=SMALL,
    )(
        scalars(where), kept, came_near, came_far, middle, inverse, gains, cotangent, *stacks
    )


def emit(total, order, held, sent_ref, kept_ref):
    held[...] = total.reshape(held.shape)
    half = sent_ref.shape[0]
    first = sent_ref.shape[2] - total.shape[1]
    for k in range(half):
        kept_ref[k, :, first:] = held[order[k]].astype(BF)
        sent_ref[k, :, first:] = held[order[half + k]].astype(BF)


def outer_kernel(order, left_ref, right_ref, sent_ref, kept_ref, held):
    emit(dims(left_ref[...], right_ref[...], 0, 0), order, held, sent_ref, kept_ref)


def blocks_out(order, width, columns):
    half = len(order) // 2
    rows = width // len(order)
    out = jax.ShapeDtypeStruct((half, rows, columns), BF)
    return out, pltpu.VMEM((len(order), rows, columns), F32)


def outer_blocks(order, left, right):
    tok, width = left.shape
    columns = right.shape[1]
    out, held = blocks_out(order, width, columns)
    return pl.pallas_call(
        outer_kernel,
        out_shape=(out, out),
        in_specs=[SCALARS, VMEM, VMEM],
        out_specs=(VMEM, VMEM),
        scratch_shapes=[held],
        compiler_params=pltpu.CompilerParams(vmem_limit_bytes=10 * 2**20),
        cost_estimate=SMALL,
    )(scalars(order), left, right)


def unturn(value, cosine, sine):
    half = DH // 2
    one, two = value[:half], value[half:]
    return [one * cosine + two * sine, two * cosine - one * sine]


def query_end_kernel(
    order, qmix_ref, qbasis_ref, cos_ref, sin_ref, hidden_ref, weights_ref, *refs
):
    part_ref, outs = refs[0], refs[1:]
    cosine, sine = cos_ref[...], sin_ref[...]
    parts = []
    for r in range(RQ):
        parts += unturn(qbasis_ref[r * DH : (r + 1) * DH, :], cosine, sine)
    tok = cosine.shape[1]
    parts += [qmix_ref[...], jnp.zeros((LEFT - QB - QM, tok), F32)]
    slopes = jnp.concatenate(parts, 0).astype(BF)
    weights = weights_ref[...].reshape(hidden_ref.shape[1], PACKED)[:, :LEFT]
    part_ref[...] = dims(slopes, weights, 0, 1)
    total = dims(hidden_ref[...], slopes, 0, 1)
    if len(outs) == 1:
        outs[0][...] = total.astype(BF)
    else:
        emit(total, order, outs[2], outs[0], outs[1])


def query_end(order, qmix, qbasis, cosine, sine, hidden, weights):
    tok, width = hidden.shape
    outs = [jax.ShapeDtypeStruct((tok, width), F32)]
    scratch = []
    if len(order) > 1:
        out, held = blocks_out(order, width, LEFT)
        outs += [out, out]
        scratch = [held]
    else:
        outs += [jax.ShapeDtypeStruct((width, LEFT), BF)]
    return pl.pallas_call(
        query_end_kernel,
        out_shape=tuple(outs),
        in_specs=[SCALARS] + [VMEM] * 6,
        out_specs=(VMEM,) * len(outs),
        scratch_shapes=scratch,
        compiler_params=pltpu.CompilerParams(vmem_limit_bytes=12 * 2**20),
        cost_estimate=SMALL,
    )(scalars(order), qmix, qbasis, cosine, sine, hidden, weights)


def key_end_kernel(
    order,
    kept_ref,
    came_ref,
    cos_ref,
    sin_ref,
    hidden_ref,
    weights_ref,
    part_ref,
    tokens_ref,
    inverse_ref,
    gains_ref,
    middle_ref,
    feed_gain_ref,
    *refs
):
    if order.shape[0] > 1:
        query_sent, query_kept, out_ref, away_ref, stay_ref, held = refs
        away_ref[:, :, :LEFT] = query_sent[...]
        stay_ref[:, :, :LEFT] = query_kept[...]
    else:
        out_ref, total_ref = refs
    cosine, sine = cos_ref[...], sin_ref[...]
    own = kept_ref[...] + came_ref[...].astype(F32)
    parts = []
    for r in range(RK):
        parts += unturn(own[KM + r * DH : KM + (r + 1) * DH], cosine, sine)
    tok, width = hidden_ref.shape
    parts += [own[2 * KM + KB :], own[:KM], own[KM + KB : 2 * KM + KB]]
    parts += [jnp.zeros((PACKED - GAINS, tok), F32)]
    slopes = jnp.concatenate(parts, 0).astype(BF)
    weights = weights_ref[...].reshape(width, PACKED)[:, LEFT:]
    slope = part_ref[...] + dims(slopes, weights, 0, 1)
    inverse = inverse_ref[...]
    normed = tokens_ref[...].astype(F32) * inverse
    scaled = slope * gains_ref[0:1, :]
    mean = jnp.mean(scaled * normed, -1, keepdims=True)
    out_ref[...] = middle_ref[...] + inverse * (scaled - normed * mean)
    gain_slope = jnp.sum(slope * normed, 0, keepdims=True)
    total = dims(hidden_ref[...], slopes, 0, 1)
    rows = jnp.concatenate(
        [gain_slope, feed_gain_ref[...], jnp.zeros((PACKED - GAINS - 2, width), F32)], 0
    )
    columns = jnp.concatenate([jnp.zeros((128 - rows.shape[0], width), F32), rows], 0).T
    total = jnp.concatenate([total[:, :-128], total[:, -128:] + columns], 1)
    if order.shape[0] > 1:
        emit(total, order, held, away_ref, stay_ref)
    else:
        total_ref[...] = total.astype(BF)


def key_end(order, *args):
    tok, width = args[4].shape
    outs = [jax.ShapeDtypeStruct((tok, width), F32)]
    scratch = []
    if len(order) > 1:
        _, held = blocks_out(order, width, PACKED - LEFT)
        out, _ = blocks_out(order, width, PACKED)
        outs += [out, out]
        scratch = [held]
    else:
        outs += [jax.ShapeDtypeStruct((width, PACKED - LEFT), BF)]
    return pl.pallas_call(
        key_end_kernel,
        out_shape=tuple(outs),
        in_specs=[SCALARS] + [VMEM] * len(args),
        out_specs=(VMEM,) * len(outs),
        scratch_shapes=scratch,
        compiler_params=pltpu.CompilerParams(vmem_limit_bytes=14 * 2**20),
        cost_estimate=SMALL,
    )(scalars(order), *args)


def key_parts(kv_ref, head, at):
    base = at + H * RK
    row = at + head * RK
    total = kv_ref[pl.ds(row, 1), :] * kv_ref[base : base + DH, :]
    total = total + kv_ref[pl.ds(row + 1, 1), :] * kv_ref[base + DH : base + 2 * DH, :]
    return (total * (1.0 / RK)).astype(BF)


def query_parts(qm_ref, qt_ref, head):
    total = qm_ref[pl.ds(head * RQ, 1), :] * qt_ref[0:DH, :]
    for r in range(1, RQ):
        total = total + qm_ref[pl.ds(head * RQ + r, 1), :] * qt_ref[r * DH : (r + 1) * DH, :]
    queries = (total * (1.0 / RQ)).astype(BF)
    return (queries.astype(F32) * DH**-0.5).astype(BF)


def attend_kernel(
    place_ref, qm_ref, qt_ref, k0, k1, k2, k3, attended_ref, probs_ref, kv_ref, bias
):
    pair = pl.program_id(0)
    tok, slots = bias.shape

    @pl.when(pair == 0)
    def _():
        for block, part in enumerate((k0, k1, k2, k3)):
            kv_ref[:, block * tok : (block + 1) * tok] = part[...].astype(F32)
        near, length = place_ref[0], place_ref[1]
        rows = near * tok + lax.broadcasted_iota(jnp.int32, (tok, tok), 0)
        for block, bit in enumerate((0, 2, 1, 3)):
            keys = (near ^ bit) * tok + lax.broadcasted_iota(jnp.int32, (tok, tok), 1)
            allowed = (keys <= rows) & (keys < length)
            bias[:, block * tok : (block + 1) * tok] = jnp.where(allowed, 0.0, NEG)

    outs = []
    for inner in range(PAIR):
        head = pair * PAIR + inner
        keys = key_parts(kv_ref, head, 0)
        values = key_parts(kv_ref, head, H * RK + RK * DH)
        queries = query_parts(qm_ref, qt_ref, head)
        scores = dims(queries, keys, 0, 0) + bias[...]
        peak = jnp.max(scores, -1, keepdims=True)
        powers = jnp.exp(scores - peak)
        total = jnp.sum(powers, -1, keepdims=True)
        probs = (powers * (1.0 / total)).astype(BF)
        probs_ref[inner] = probs
        outs.append(dims(probs, values, 1, 1))
    attended_ref[...] = jnp.concatenate(outs, 1).astype(BF)


def attend(places, query_mix, query_turned, factors):
    tok = query_mix.shape[1]
    slots = 4 * tok
    table = pltpu.HBM((factors[0].shape[0], slots), F32)
    return pl.pallas_call(
        attend_kernel,
        grid=(H // PAIR,),
        out_shape=(
            jax.ShapeDtypeStruct((tok, H * DH), BF),
            pltpu.HBM((H, tok, slots), BF),
            table,
        ),
        in_specs=[SCALARS, whole(query_mix), whole(query_turned)] + [whole(f) for f in factors],
        out_specs=(
            pl.BlockSpec((tok, PAIR * DH), lambda i: (0, i)),
            pl.BlockSpec((PAIR, tok, slots), lambda i: (i, 0, 0)),
            whole(table),
        ),
        scratch_shapes=[pltpu.VMEM((tok, slots), F32)],
        compiler_params=pltpu.CompilerParams(vmem_limit_bytes=16 * 2**20),
        cost_estimate=SMALL,
    )(places, query_mix, query_turned, *pinned(*factors))


def attend_back_kernel(*refs):
    qm_ref, qt_ref, kv_ref, slope_ref, probs_all = refs[:5]
    kept_ref, sent_ref, qmix_ref, qbasis_ref, mix_ref, basis_ref, probs_held, psem = refs[5:]
    pair = pl.program_id(0)
    vm = H * RK + RK * DH
    kb = RK * DH

    def coming(at):
        return pltpu.make_async_copy(
            probs_all.at[pl.ds(at * PAIR, PAIR)], probs_held.at[at % 2], psem.at[at % 2]
        )

    @pl.when(pair == 0)
    def _():
        coming(pair).start()
        basis_ref[...] = jnp.zeros_like(basis_ref)
        qbasis_ref[...] = jnp.zeros_like(qbasis_ref)

    @pl.when(pair + 1 < pl.num_programs(0))
    def _():
        coming(pair + 1).start()

    coming(pair).wait()
    probs_ref = probs_held.at[pair % 2]
    for inner in range(PAIR):
        head = pair * PAIR + inner
        keys = key_parts(kv_ref, head, 0)
        values = key_parts(kv_ref, head, vm)
        queries = query_parts(qm_ref, qt_ref, head)
        slope = slope_ref[inner * DH : (inner + 1) * DH, :]
        probs_low = probs_ref[inner]
        slope_probs = dims(slope, values, 0, 0)
        probs = probs_low.astype(F32)
        weighted = probs * slope_probs
        total = jnp.sum(weighted, -1, keepdims=True)
        slope_scores = (weighted - probs * total).astype(BF)
        slope_query = dims(keys, slope_scores, 1, 1) * (DH**-0.5 / RQ)
        slope_key = dims(queries, slope_scores, 1, 0) * (1.0 / RK)
        slope_value = dims(slope, probs_low, 1, 0) * (1.0 / RK)
        for r in range(RK):
            row = head * RK + r
            for at, piece, side in ((0, slope_key, 0), (vm, slope_value, 1)):
                base = at + H * RK + r * DH
                here = side * RK + r
                basis_ref[here * DH : (here + 1) * DH, :] += kv_ref[pl.ds(at + row, 1), :] * piece
                mix_ref[pl.ds(side * H * RK + row, 1), :] = jnp.sum(
                    piece * kv_ref[base : base + DH, :], 0, keepdims=True
                )
        for r in range(RQ):
            row = head * RQ + r
            cut = slice(r * DH, (r + 1) * DH)
            qbasis_ref[cut, :] += qm_ref[pl.ds(row, 1), :] * slope_query
            qmix_ref[pl.ds(row, 1), :] = jnp.sum(slope_query * qt_ref[cut, :], 0, keepdims=True)

    @pl.when(pair == pl.num_programs(0) - 1)
    def _():
        half = kept_ref.shape[2] * 2
        tok = kept_ref.shape[2]
        km = H * RK
        for base, ref, begin, rows in (
            (0, mix_ref, 0, km),
            (km, basis_ref, 0, kb),
            (vm, mix_ref, km, km),
            (vm + km, basis_ref, kb, kb),
        ):
            part = ref[begin : begin + rows, :]
            for block in range(2):
                kept_ref[block, base : base + rows, :] = part[:, block * tok : (block + 1) * tok]
                sent_ref[block, base : base + rows, :] = part[
                    :, half + block * tok : half + (block + 1) * tok
                ].astype(BF)


def attend_back(query_mix, query_turned, row_factors, slope_attended, probs):
    tok = query_mix.shape[1]
    rows, slots = row_factors.shape
    outs = (
        jax.ShapeDtypeStruct((2, rows, tok), F32),
        jax.ShapeDtypeStruct((2, rows, tok), BF),
        jax.ShapeDtypeStruct((H * RQ, tok), F32),
        jax.ShapeDtypeStruct((RQ * DH, tok), F32),
    )
    return pl.pallas_call(
        attend_back_kernel,
        grid=(H // PAIR,),
        out_shape=outs,
        in_specs=[
            whole(query_mix),
            whole(query_turned),
            whole(row_factors),
            pl.BlockSpec((PAIR * DH, tok), lambda i: (i, 0)),
            pl.BlockSpec(memory_space=pltpu.HBM),
        ],
        out_specs=tuple(whole(o) for o in outs),
        scratch_shapes=[
            pltpu.VMEM((2 * H * RK, slots), F32),
            pltpu.VMEM((2 * RK * DH, slots), F32),
            pltpu.VMEM((2, PAIR, tok, slots), BF),
            pltpu.SemaphoreType.DMA((2,)),
        ],
        compiler_params=pltpu.CompilerParams(vmem_limit_bytes=18 * 2**20),
        cost_estimate=SMALL,
    )(query_mix, query_turned, *pinned(row_factors), slope_attended, *pinned(probs))


QB, KB, VB = RQ * DH, RK * DH, RK * DH
QM, KM, VM = H * RQ, H * RK, H * RK
LEFT = 512
GAINS = LEFT + KB + VB + KM + VM
PACKED = 896


def steps_of_any_mesh(
    tokens, places, cosine, sine, packed, merge_weight, both, down_weight, cotangent
):
    tok, width = tokens.shape
    group, twice, hidden = both.shape
    rows = twice // 2
    cut = down_weight.shape[0]
    axes = ("wide", "narrow")
    packed = [lax.all_gather(packed, axes, axis=0, tiled=True)[None]]
    merge = [lax.all_gather(merge_weight, axes, axis=0, tiled=True)[None]]
    downs = [lax.all_gather(down_weight, "wide", axis=0, tiled=True)[None]]
    both = lax.all_to_all(both, "narrow", 0, 0, tiled=True)
    both = lax.all_gather(both, "wide", axis=0, tiled=False)
    both = both.reshape(-1, 2, rows, hidden).transpose(1, 0, 2, 3)
    both = both.reshape(2, 8, 4, width // 32, hidden).transpose(1, 2, 0, 3, 4)
    weights_in = ([both.reshape(8, 4, width // 16, hidden)], list(range(8)), downs, [0])

    hidden_one, inverse_one, gains, weights, query_mix, query_turned, own_factors = project(
        tokens, cosine, sine, packed, [0]
    )
    attended, probs, row_factors = attend(
        places, query_mix, query_turned, gather_narrow(own_factors)
    )
    hidden_two, middle, inverse_two = middle_of(attended, tokens, gains, merge, [0])
    own, far, close, cross = gather_narrow(hidden_two)
    cot_own, cot_far, cot_near, cot_cross = gather_narrow(cotangent)
    parts = [
        feed((own, close), (cot_own, cot_near), *weights_in),
        feed((far, cross), (cot_far, cot_cross), *weights_in),
    ]
    hidden_feed, slope_gate, slope_up = zip(*(part[:3] for part in parts))
    came_near = flip(parts[0][4], "narrow", 1)
    came_far = flip(add_low(parts[1][3], flip(parts[1][4], "narrow", 1)), "narrow", 2)
    full = slopes_of((own, close, far, cross), slope_gate, slope_up, list(range(width // 128)))
    full = full.transpose(1, 0, 3, 2).reshape(2, width, hidden)
    slopes = jnp.concatenate([scatter_wide(s).reshape(group, rows, hidden) for s in full], 1)
    slopes = lax.all_to_all(slopes.astype(BF), "narrow", 0, 0, tiled=True)
    cots = (cot_own, cot_near, cot_far, cot_cross)
    down_slope = scatter_wide(down_slopes(hidden_feed, cots, [0], cut)[0])
    kept, sent = feed_out(hidden_feed, downs, [0])
    fed = kept + flip(sent, "narrow", 1).astype(F32)
    fed = fed[0] + flip(fed[1].astype(BF), "narrow", 2).astype(F32)
    output = (middle + fed).astype(BF)

    slope_middle, slope_low, slope_attended, feed_gain_slope = turn_back(
        parts[0][3], came_near, came_far, middle, inverse_two, gains, cotangent, merge, [0]
    )
    merge_slope = scatter_all(dims(attended, slope_low, 0, 0).astype(BF))
    factors_in = (query_mix, query_turned, row_factors, slope_attended, probs)
    key_kept, key_sent, query_mix_slope, query_basis_slope = attend_back(*factors_in)
    key_pair = key_kept + flip(key_sent, "narrow", 1).astype(F32)
    key_came = flip(key_pair[1].astype(BF), "narrow", 2)
    part, query_slopes = query_end(
        [0], query_mix_slope, query_basis_slope, cosine, sine, hidden_one, weights
    )
    tokens_slope, key_slopes = key_end(
        [0], key_pair[0], key_came, cosine, sine, hidden_one, weights, part, tokens, inverse_one,
        gains, slope_middle, feed_gain_slope,
    )
    query_slopes, key_slopes = scatter_all(query_slopes), scatter_all(key_slopes)
    return output, tokens_slope, query_slopes, key_slopes, merge_slope, slopes, down_slope


def steps_of_small_mesh(
    tokens, places, cosine, sine, packed, merge_weight, both_in, down_weight, cotangent
):
    tok, width = tokens.shape
    cut = down_weight.shape[0]
    high, low = wide_place()
    rounds = lax.axis_size("wide") // 2
    group = lax.axis_size("narrow")
    join = lambda a, b: jnp.concatenate([a, b], 0)

    first = turned(jnp.concatenate([packed, merge_weight], 1)[None])
    both = lax.all_to_all(both_in, "narrow", 0, 0, tiled=True)
    first = tie(*first)
    one = jnp.concatenate([f[:, :, :PACKED] for f in first], 0)
    two = jnp.concatenate([f[:, :, PACKED:] for f in first], 0)
    one, one_came, two, two_came, both = tie(
        one, flip(one, "narrow", 2), two, flip(two, "wide", 1), both
    )
    one, two = join(one, one_came), join(two, two_came)
    pieces = [both[None]]
    one, one_came, two, two_came, piece = tie(
        one, flip(one, "wide", 1), two, flip(two, "narrow", 2), turn(pieces[0], 1)
    )
    one, two = join(one, one_came), join(two, two_came)
    where, merge_where = relative_blocks(), relative_blocks(True)
    both_where = [((high - k) % rounds) * 2 + low for k in range(rounds)] + [
        ((high - k) % rounds) * 2 + 1 - low for k in range(rounds)
    ]
    one, piece, down_own, first = tie(one, piece, down_weight, pieces[0])
    pieces += [piece, turn(piece, 1)]
    down_came = flip(down_own, "wide", 1)
    others = [flip(first, "wide", 1)]
    hidden_one, inverse_one, gains, weights, query_mix, query_turned, factor = project(
        tokens, cosine, sine, [one, flip(one, "narrow", 1)], where
    )
    factor, two, first, down_came = tie(factor, two, pieces[1], down_came)
    merge = [two, flip(two, "narrow", 1)]
    others.append(flip(first, "wide", 1))
    factor_far, factor_near, pieces[2], others[0], down_came = tie(
        flip(factor, "narrow", 2), flip(factor, "narrow", 1), pieces[2], others[0], down_came
    )
    pieces.append(turn(pieces[2], 1))
    pair = jnp.where(low == 0, jnp.stack([down_own, down_came]), jnp.stack([down_came, down_own]))
    pair = jnp.stack([pair.reshape(2 * cut, width)] * rounds)
    factor_cross, cot_own, first, pieces[3], others[1], pair = tie(
        flip(factor_far, "narrow", 1), cotangent, pieces[2], pieces[3], others[1], pair
    )
    downs = [ring_all_to_all(pair)]
    down_where = list(range(rounds))

    cot_far = flip(cot_own, "narrow", 2)
    others += [flip(first, "wide", 1), flip(pieces[3], "wide", 1)]
    attended, probs, row_factors = attend(
        places, query_mix, query_turned, (factor, factor_far, factor_near, factor_cross)
    )
    attended, cot_far, others[2], others[3], merge[1] = tie(
        attended, cot_far, others[2], others[3], merge[1]
    )
    hidden_two, middle, inverse_two = middle_of(attended, tokens, gains, merge, merge_where)
    own, cot_far = tie(hidden_two, cot_far)

    far, close = flip(own, "narrow", 2), flip(own, "narrow", 1)
    cot_near, cot_cross = flip(cot_own, "narrow", 1), flip(cot_far, "narrow", 1)
    weights_in = (pieces + others, both_where, downs, down_where)
    one = feed((own, close), (cot_own, cot_near), *weights_in)
    far, one_sent = tie(far, one[4])
    came_near = flip(one_sent, "narrow", 1)
    cross = flip(far, "narrow", 1)
    two = feed((far, cross), (cot_far, cot_cross), *weights_in)
    for_far = add_low(two[3], flip(two[4], "narrow", 1))
    hidden_feed, slope_gate, slope_up = zip(one[:3], two[:3])
    for_far, slope_gate, slope_up, came_near = tie(for_far, slope_gate, slope_up, came_near)
    came_far = flip(for_far, "narrow", 2)
    slots = (own, close, far, cross)
    cots = (cot_own, cot_near, cot_far, cot_cross)
    order = [2 * k + 1 - low for k in range(rounds)]
    to_send = slopes_of(slots, slope_gate, slope_up, order, True)
    *hidden_feed, gate_sent, up_sent = tie(*hidden_feed, *to_send)
    gate_came = flip(gate_sent, "wide", 1)
    down_parts = down_slopes(hidden_feed, cots, [0], cut)[0]
    slope_gate, slope_up, down_parts = tie(slope_gate, slope_up, down_parts)
    down_parts = ring_all_to_all(down_parts.reshape(rounds, 2 * cut, width))
    to_keep = slopes_of(slots, slope_gate, slope_up, [2 * k + low for k in range(rounds)])
    came_far, to_keep = tie(came_far, to_keep)

    slope_middle, slope_low, slope_attended, feed_gain_slope = turn_back(
        one[3], came_near, came_far, middle, inverse_two, gains, cotangent, merge, merge_where
    )
    merge_sent, merge_kept = outer_blocks(scatter_order(True), attended, slope_low)
    merge_sent, slope_attended, gate_came, up_sent = tie(
        merge_sent, slope_attended, gate_came, up_sent
    )
    up_came = flip(up_sent, "wide", 1)
    merge_came = flip(merge_sent, "narrow", 1)
    merge_sum = add_low(merge_kept, merge_came)
    slope_attended, merge_sum = tie(slope_attended, merge_sum)
    merge_came = flip(merge_sum[8:], "narrow", 2)
    key_kept, key_sent, query_mix_slope, query_basis_slope = attend_back(
        query_mix, query_turned, row_factors, slope_attended, probs
    )
    key_kept, key_sent, query_basis_slope, merge_came, up_came, down_parts = tie(
        key_kept, key_sent, query_basis_slope, merge_came, up_came, down_parts
    )
    key_came = flip(key_sent, "narrow", 1)
    merge_sum = add_low(merge_sum[:8], merge_came)
    key_came, merge_sum = tie(key_came, merge_sum)
    key_pair = key_kept + key_came.astype(F32)
    key_far, up_came, query_basis_slope, merge_sum = tie(
        key_pair[1].astype(BF), up_came, query_basis_slope, merge_sum
    )
    key_came = flip(key_far, "narrow", 2)
    parts = ring_all_to_all(add_low(to_keep, jnp.stack([gate_came, up_came], 1)))
    merge_came = flip(merge_sum[4:], "wide", 1)
    order = scatter_order(True)
    part, query_sent, query_kept = query_end(
        order, query_mix_slope, query_basis_slope, cosine, sine, hidden_one, weights
    )
    key_came, part = tie(key_came, part)
    tokens_slope, ends_sent, ends = key_end(
        order, key_pair[0], key_came, cosine, sine, hidden_one, weights, part, tokens, inverse_one,
        gains, slope_middle, feed_gain_slope, query_sent, query_kept,
    )

    ends = add_low(ends, flip(ends_sent, "narrow", 1))
    ends, hidden_feed = tie(ends, hidden_feed)
    ends_came = flip(ends[8:], "narrow", 2)
    kept, sent = feed_out(hidden_feed, downs, down_where)
    ends_came, kept, sent = tie(ends_came, kept, sent)
    ends = add_low(ends[:8], ends_came)
    ends, sent, parts, down_parts = tie(ends, sent, parts, down_parts)
    down_sum = jnp.sum(down_parts.astype(F32), 0).reshape(2, cut, width)
    down_came = flip(pick(down_sum, 1 - low, 0).astype(BF), "wide", 1)
    ends_came = flip(ends[4:], "wide", 1)
    fed = kept + flip(sent, "narrow", 1).astype(F32)
    slopes = lax.all_to_all(finish(parts, group), "narrow", 0, 0, tiled=True)
    merge_sum = add_low(merge_sum[:4], merge_came)
    ends_came, fed, merge_sum = tie(ends_came, fed, merge_sum)
    ends = jnp.concatenate([add_low(ends[:4], ends_came), merge_sum], 2)
    ends, fed_far = tie(ends, fed[1].astype(BF))
    sums = spread_turns(ends)
    slopes = after(slopes, sums)
    fed_came = flip(fed_far, "narrow", 2)
    down_slope = pick(down_sum, low, 0) + down_came.astype(F32)
    merge_slope = sums[:, PACKED:]
    output = (middle + fed[0] + fed_came.astype(F32)).astype(BF)
    query_slopes, key_slopes = sums[:, :LEFT], sums[:, LEFT:PACKED]
    return output, tokens_slope, query_slopes, key_slopes, merge_slope, slopes, down_slope


def per_device(
    tokens,
    lengths,
    attend_gain,
    query_heads,
    query_basis,
    key_heads,
    key_basis,
    value_heads,
    value_basis,
    merge_weight,
    feed_gain,
    gate_weight,
    up_weight,
    down_weight,
    cotangent,
):
    tok, width = tokens.shape
    wide_count = lax.axis_size("wide")
    narrow_count = lax.axis_size("narrow")
    near = lax.axis_index("narrow")
    rows = gate_weight.shape[0]
    cut = down_weight.shape[0]
    hidden = cut * wide_count
    small = small_mesh()

    positions = (near * tok + jnp.arange(tok, dtype=jnp.int32)).astype(F32)
    frequency = jnp.power(10000.0, -2.0 * jnp.arange(DH // 2, dtype=F32) / DH)
    angles = frequency[:, None] * positions[None, :]
    cosine, sine = jnp.cos(angles), jnp.sin(angles)

    packed = jnp.concatenate(
        [
            query_basis,
            query_heads,
            jnp.zeros((rows, LEFT - QB - QM), BF),
            key_basis,
            value_basis,
            key_heads,
            value_heads,
            attend_gain[:, None],
            feed_gain[:, None],
            jnp.zeros((rows, PACKED - GAINS - 2), BF),
        ],
        1,
    )

    def columns(weight):
        parts = weight.reshape(rows, wide_count, narrow_count, cut).transpose(2, 0, 1, 3)
        return parts.reshape(narrow_count, rows, hidden)

    both_in = jnp.concatenate([columns(gate_weight), columns(up_weight)], 1)
    places = jnp.stack([near.astype(jnp.int32), lengths[0].astype(jnp.int32)])
    if small:
        exact = steps_of_small_mesh
    else:
        exact = steps_of_any_mesh
    output, tokens_slope, query_slopes, key_slopes, merge_slope, slopes, down_slope = exact(
        tokens, places, cosine, sine, packed, merge_weight, both_in, down_weight, cotangent
    )
    if small:
        slopes = unmix(slopes, cut)
    else:
        slopes = slopes.reshape(narrow_count, 2, rows, wide_count, cut).transpose(1, 2, 3, 0, 4)
        slopes = slopes.reshape(2, rows, hidden * narrow_count).astype(F32)

    base = GAINS - LEFT
    return (
        output,
        tokens_slope,
        key_slopes[:, base],
        query_slopes[:, QB : QB + QM],
        query_slopes[:, :QB],
        key_slopes[:, KB + VB : KB + VB + KM],
        key_slopes[:, :KB],
        key_slopes[:, KB + VB + KM : KB + VB + KM + VM],
        key_slopes[:, KB : KB + VB],
        merge_slope,
        key_slopes[:, base + 1],
        slopes[0],
        slopes[1],
        down_slope,
    )


def solution(mesh):
    both = ("wide", "narrow")
    row, vector = P(both, None), P(both)
    return jax.shard_map(
        per_device,
        mesh=mesh,
        in_specs=(row, P("wide"), vector) + (row,) * 7 + (vector,) + (row,) * 4,
        out_specs=(row, row, vector) + (row,) * 7 + (vector,) + (row,) * 3,
        check_vma=False,
    )
```

```python
import functools

import jax
import jax.numpy as jnp
from jax import lax
from jax.experimental import pallas as pl
from jax.experimental.pallas import tpu as pltpu
from jax.sharding import PartitionSpec as P

H = 16
DH = 64
RQ = 6
RK = 2
PAIR = 2
EPS = 1e-06
NEG = -1e30
BF = jnp.bfloat16
F32 = jnp.float32


def dims(left, right, left_dim, right_dim):
    return lax.dot_general(
        left, right, (((left_dim,), (right_dim,)), ((), ())), preferred_element_type=F32
    )


def flip(value, axis, bit):
    size = lax.axis_size(axis)
    return lax.ppermute(value, axis, [(i, i ^ bit) for i in range(size)])


def turn(value, steps):
    size = lax.axis_size("wide")
    return lax.ppermute(value, "wide", [(i, (i + 2 * steps) % size) for i in range(size)])


def small_mesh():
    return lax.axis_size("wide") == 8 and lax.axis_size("narrow") == 4


def wide_place():
    me = lax.axis_index("wide")
    return me // 2, me % 2


def tie(*values):
    return lax.optimization_barrier(values)


def after(value, *others):
    return lax.optimization_barrier((value, others))[0]


def ring_groups():
    size = lax.axis_size("wide")
    return [list(range(x, size, 2)) for x in range(2)]


def ring_all_to_all(value):
    return lax.all_to_all(value, "wide", 0, 0, axis_index_groups=ring_groups(), tiled=True)


def pick(value, index, axis):
    return lax.dynamic_index_in_dim(value, index, axis, keepdims=False)


def spread_high(blocks):
    return jnp.sum(ring_all_to_all(blocks).astype(F32), 0)


def scatter_wide(value):
    return lax.psum_scatter(value, "wide", scatter_dimension=0, tiled=True).astype(F32)


def turned(value):
    rounds = lax.axis_size("wide") // 2
    return [value] + [turn(value, k) for k in range(1, rounds)]


def joined(value, axis, bit):
    return jnp.concatenate([value, flip(value, axis, bit)], 0)


def relative_blocks(swapped=False):
    high, low = wide_place()
    rounds = lax.axis_size("wide") // 2
    near = lax.axis_index("narrow")
    return [
        (((high - k) % rounds) * 2 + (low ^ x)) * 4 + (near ^ (2 * y) ^ c)
        for c in (0, 1)
        for x, y in ([(0, 0), (1, 0), (0, 1), (1, 1)] if swapped else [(0, 0), (0, 1), (1, 0), (1, 1)])
        for k in range(rounds)
    ]


def scatter_all(value):
    return lax.psum_scatter(value, ("wide", "narrow"), scatter_dimension=0, tiled=True).astype(F32)


def scatter_order(turning):
    high, low = wide_place()
    rounds = lax.axis_size("wide") // 2
    near = lax.axis_index("narrow")
    return [
        (((high + k) % rounds if turning else k) * 2 + (low ^ x)) * 4 + (near ^ (2 * y) ^ c)
        for c in (0, 1)
        for y in (0, 1)
        for x in (0, 1)
        for k in range(rounds)
    ]


def spread_turns(blocks):
    total = blocks[0].astype(F32)
    for k in range(1, blocks.shape[0]):
        total = total + turn(blocks[k], k).astype(F32)
    return total


def add_low(kept, came):
    return (kept.astype(F32) + came.astype(F32)).astype(BF)


def gather_narrow(value):
    far = flip(value, "narrow", 2)
    return [value, far, flip(value, "narrow", 1), flip(far, "narrow", 1)]


def starts(stacks, where_ref, first, target, sem):
    copies = []
    for stack in stacks:
        for k in range(stack.shape[0]):
            at = len(copies)
            copies.append(
                pltpu.make_async_copy(
                    stack.at[k], target.at[where_ref[first + at]], sem.at[first + at]
                )
            )
            copies[-1].start()
    return copies


def count(stacks):
    return sum(stack.shape[0] for stack in stacks)


def whole(array):
    return pl.BlockSpec(array.shape, lambda *i: (0,) * len(array.shape))


ANYWHERE = pl.BlockSpec(memory_space=pl.ANY)


def pinned(*arrays):
    return [pltpu.with_memory_space_constraint(a, pltpu.HBM) for a in arrays]


SCALARS = pl.BlockSpec(memory_space=pltpu.SMEM)
SMALL = pl.CostEstimate(flops=3 * 10**9, bytes_accessed=2**22, transcendentals=0)


def scalars(*lists):
    return jnp.stack([jnp.asarray(v, jnp.int32) for one in lists for v in one])


def project_kernel(n, where, tokens_ref, cos_ref, sin_ref, *refs):
    packed, refs = refs[:n], refs[n:]
    hidden_ref, inverse_ref, gains_ref, packed_out, qm_ref, qt_ref, kv_ref = refs[:7]
    packed_ref, sem, out_sem = refs[7:]
    copies = starts(packed, where, 0, packed_ref, sem)
    source = tokens_ref[...].astype(F32)
    inverse = lax.rsqrt(jnp.mean(source * source, -1, keepdims=True) + EPS)
    inverse_ref[...] = inverse
    normed = source * inverse
    for copy in copies:
        copy.wait()
    outgoing = pltpu.make_async_copy(packed_ref, packed_out, out_sem)
    outgoing.start()
    width = source.shape[1]
    weights = packed_ref[...].reshape(width, PACKED)
    gains = weights[:, PACKED - 128 :].astype(F32).T
    at = GAINS - (PACKED - 128)
    gains_ref[...] = gains[at : at + 8]
    hidden = (normed * gains[at : at + 1]).astype(BF)
    hidden_ref[...] = hidden
    factors = dims(hidden, weights, 1, 0).T
    cosine, sine = cos_ref[...], sin_ref[...]
    half = DH // 2
    for r in range(RQ + RK):
        base = r * DH if r < RQ else LEFT + (r - RQ) * DH
        one = factors[base : base + half]
        two = factors[base + half : base + DH]
        a, b = one * cosine - two * sine, one * sine + two * cosine
        if r < RQ:
            qt_ref[base : base + half, :] = a
            qt_ref[base + half : base + DH, :] = b
        else:
            row = KM + (r - RQ) * DH
            kv_ref[row : row + half, :] = a.astype(BF)
            kv_ref[row + half : row + DH, :] = b.astype(BF)
    qm_ref[...] = factors[QB : QB + QM]
    base = LEFT + KB
    kv_ref[2 * KM + KB :, :] = factors[base : base + VB].astype(BF)
    base += VB
    kv_ref[0:KM, :] = factors[base : base + KM].astype(BF)
    kv_ref[KM + KB : 2 * KM + KB, :] = factors[base + KM : base + 2 * KM].astype(BF)
    outgoing.wait()


VMEM = pl.BlockSpec(memory_space=pltpu.VMEM)


def project(tokens, cosine, sine, packed, where):
    tok, width = tokens.shape
    outs = (
        jax.ShapeDtypeStruct((tok, width), BF),
        jax.ShapeDtypeStruct((tok, 1), F32),
        jax.ShapeDtypeStruct((8, width), F32),
        pltpu.HBM((count(packed),) + packed[0].shape[1:], BF),
        jax.ShapeDtypeStruct((QM, tok), F32),
        jax.ShapeDtypeStruct((QB, tok), F32),
        jax.ShapeDtypeStruct((2 * (KM + KB), tok), BF),
    )
    return pl.pallas_call(
        functools.partial(project_kernel, len(packed)),
        out_shape=outs,
        in_specs=[SCALARS] + [VMEM] * 3 + [ANYWHERE] * len(packed),
        out_specs=(VMEM,) * 3 + (ANYWHERE,) + (VMEM,) * 3,
        scratch_shapes=[
            pltpu.VMEM((count(packed),) + packed[0].shape[1:], BF),
            pltpu.SemaphoreType.DMA((count(packed),)),
            pltpu.SemaphoreType.DMA,
        ],
        compiler_params=pltpu.CompilerParams(vmem_limit_bytes=14 * 2**20),
        cost_estimate=SMALL,
    )(scalars(where), tokens, cosine, sine, *packed)


def halves_of(both_ref, width, hidden):
    rows = both_ref.shape[2] // 2
    return (
        both_ref[:, :, :rows, :].reshape(width, hidden),
        both_ref[:, :, rows:, :].reshape(width, hidden),
    )


def feed_kernel(nb, nd, where, *refs):
    pieces, refs = refs[:2], refs[2:]
    cots, refs = refs[:2], refs[2:]
    boths, refs = refs[:nb], refs[nb:]
    downs, refs = refs[:nd], refs[nd:]
    hf_out, sg_out, su_out, kept_ref, sent_ref, hid, cot, wgu, wd, held, sem, psem, osem = refs
    outgoing = []
    width, hidden = hid.shape[2], wgu.shape[3]
    loads = [
        [
            pltpu.make_async_copy(pieces[b], hid.at[b], psem.at[b]),
            pltpu.make_async_copy(cots[b], cot.at[b], psem.at[2 + b]),
        ]
        for b in range(2)
    ]
    loads[0][0].start()
    in_both = starts(boths, where, 0, wgu, sem)
    loads[0][1].start()
    in_down = starts(downs, where, count(boths), wd, sem)
    for copy in loads[1]:
        copy.start()
    for b in range(2):
        loads[b][0].wait()
        if b == 0:
            for copy in in_both:
                copy.wait()
        gate_all, up_all = halves_of(wgu, width, hidden)
        gate = dims(hid[b], gate_all, 1, 0)
        upward = dims(hid[b], up_all, 1, 0)
        loads[b][1].wait()
        if b == 0:
            for copy in in_down:
                copy.wait()
        down_all = wd[...].reshape(hidden, width)
        slope = dims(cot[b], down_all, 1, 1)
        sig = jax.nn.sigmoid(gate)
        silu = gate * sig
        held[0, b] = (silu * upward).astype(BF)
        slope_up = (slope * silu).astype(BF)
        slope_gate = (slope * upward * sig * (1.0 + gate * (1.0 - sig))).astype(BF)
        held[1, b] = slope_gate
        held[2, b] = slope_up
        for k, out in enumerate((hf_out, sg_out, su_out)):
            outgoing.append(pltpu.make_async_copy(held.at[k, b], out.at[b], osem.at[k, b]))
            outgoing[-1].start()
        back = dims(slope_gate, gate_all, 1, 1) + dims(slope_up, up_all, 1, 1)
        if b == 0:
            kept_ref[...] = back
        else:
            sent_ref[...] = back.astype(BF)
    for copy in outgoing:
        copy.wait()


def feed(pieces, cots, boths, both_where, downs, down_where):
    tok, width = pieces[0].shape
    hidden = boths[0].shape[3]
    low = pltpu.HBM((2, tok, hidden), BF)
    outs = (
        low,
        low,
        low,
        jax.ShapeDtypeStruct((tok, width), F32),
        jax.ShapeDtypeStruct((tok, width), BF),
    )
    blocks = lambda stacks: pltpu.VMEM((count(stacks),) + stacks[0].shape[1:], BF)
    total = count(boths) + count(downs)
    return pl.pallas_call(
        functools.partial(feed_kernel, len(boths), len(downs)),
        out_shape=outs,
        in_specs=[SCALARS] + [ANYWHERE] * (4 + len(boths) + len(downs)),
        out_specs=(ANYWHERE,) * 3 + (VMEM,) * 2,
        scratch_shapes=[
            pltpu.VMEM((2, tok, width), BF),
            pltpu.VMEM((2, tok, width), BF),
            blocks(boths),
            blocks(downs),
            pltpu.VMEM((3, 2, tok, hidden), BF),
            pltpu.SemaphoreType.DMA((total,)),
            pltpu.SemaphoreType.DMA((4,)),
            pltpu.SemaphoreType.DMA((3, 2)),
        ],
        compiler_params=pltpu.CompilerParams(vmem_limit_bytes=20 * 2**20),
        cost_estimate=SMALL,
    )(scalars(both_where, down_where), *pinned(*pieces, *cots, *boths, *downs))


def bring(sources, target, sem):
    copies = []
    at = 0
    for source in sources:
        parts = [source] if len(source.shape) == 2 else [source.at[k] for k in range(source.shape[0])]
        for part in parts:
            copies.append(pltpu.make_async_copy(part, target.at[at], sem.at[at]))
            copies[-1].start()
            at += 1
    return copies


def slopes_kernel(blocks, order, *refs):
    *outs, hid, gates, ups, hsem, gsem, usem = refs[8:]
    out = outs[0]
    copies = bring(refs[:4], hid, hsem) + bring(refs[4:6], gates, gsem)
    later = bring(refs[6:8], ups, usem)
    for copy in copies:
        copy.wait()
    rows, hidden = out.shape[-1], out.shape[-2]
    columns = []
    for k in range(blocks):
        at = pl.multiple_of(order[k] * rows, 128)
        columns.append(hid[:, :, pl.ds(at, rows)].reshape(-1, rows))
    chosen = jnp.concatenate(columns, 1)
    for side, held in enumerate((gates, ups)):
        if side == 1:
            for copy in later:
                copy.wait()
        result = dims(held[...].reshape(-1, hidden), chosen, 0, 0).astype(BF)
        for k in range(blocks):
            part = result[:, k * rows : (k + 1) * rows]
            if len(outs) == 2:
                outs[side][k] = part
            else:
                out[k, side] = part


def slopes_of(pieces, slope_gate, slope_up, order, apart=False):
    tok, width = pieces[0].shape
    hidden = slope_gate[0].shape[2]
    rows = 128
    return pl.pallas_call(
        functools.partial(slopes_kernel, len(order)),
        out_shape=(jax.ShapeDtypeStruct((len(order), hidden, rows), BF),) * 2
        if apart
        else jax.ShapeDtypeStruct((len(order), 2, hidden, rows), BF),
        in_specs=[SCALARS] + [ANYWHERE] * 8,
        out_specs=(VMEM, VMEM) if apart else VMEM,
        scratch_shapes=[
            pltpu.VMEM((4, tok, width), BF),
            pltpu.VMEM((4, tok, hidden), BF),
            pltpu.VMEM((4, tok, hidden), BF),
        ]
        + [pltpu.SemaphoreType.DMA((4,))] * 3,
        compiler_params=pltpu.CompilerParams(vmem_limit_bytes=18 * 2**20),
        cost_estimate=SMALL,
    )(scalars(order), *pinned(*pieces, *slope_gate, *slope_up))


def down_kernel(blocks, order, *refs):
    feeds, cots, fsem, csem = refs[-4:]
    for copy in bring(refs[:2], feeds, fsem) + bring(refs[2:6], cots, csem):
        copy.wait()
    outs = refs[6:-4]
    hidden, width = feeds.shape[2], cots.shape[2]
    total = dims(feeds[...].reshape(-1, hidden), cots[...].reshape(-1, width), 0, 0)
    if blocks == 1:
        outs[0][...] = total.astype(BF)
    else:
        sent_ref, kept_ref, held = outs
        held[...] = total.reshape(held.shape)
        for k in range(blocks // 2):
            kept_ref[k] = held[order[2 * k]].astype(BF)
            sent_ref[k] = held[order[2 * k + 1]].astype(BF)


def down_slopes(hidden_feed, cots, order, cut):
    tok, width = cots[0].shape
    hidden = hidden_feed[0].shape[2]
    if len(order) > 1:
        out = jax.ShapeDtypeStruct((len(order) // 2, cut, width), BF)
        outs, scratch = (out, out), [pltpu.VMEM((len(order), cut, width), F32)]
    else:
        outs, scratch = (jax.ShapeDtypeStruct((hidden, width), BF),), []
    return pl.pallas_call(
        functools.partial(down_kernel, len(order)),
        out_shape=outs,
        in_specs=[SCALARS] + [ANYWHERE] * 6,
        out_specs=(VMEM,) * len(outs),
        scratch_shapes=scratch
        + [
            pltpu.VMEM((4, tok, hidden), BF),
            pltpu.VMEM((4, tok, width), BF),
            pltpu.SemaphoreType.DMA((4,)),
            pltpu.SemaphoreType.DMA((4,)),
        ],
        compiler_params=pltpu.CompilerParams(vmem_limit_bytes=20 * 2**20),
        cost_estimate=SMALL,
    )(scalars(order), *pinned(*hidden_feed, *cots))


def feed_out_kernel(nd, where, *refs):
    downs, (f0, f1, kept_ref, sent_ref, wd, feeds, sem, fsem) = refs[:nd], refs[nd:]
    for copy in starts(downs, where, 0, wd, sem) + bring((f0, f1), feeds, fsem):
        copy.wait()
    down_all = wd[...].reshape(feeds.shape[2], wd.shape[2])
    for part in range(2):
        kept_ref[part] = dims(feeds[2 * part], down_all, 1, 0)
        sent_ref[part] = dims(feeds[2 * part + 1], down_all, 1, 0).astype(BF)


def feed_out(hidden_feed, downs, down_where):
    tok, hidden = hidden_feed[0].shape[1:]
    width = downs[0].shape[2]
    return pl.pallas_call(
        functools.partial(feed_out_kernel, len(downs)),
        out_shape=(
            jax.ShapeDtypeStruct((2, tok, width), F32),
            jax.ShapeDtypeStruct((2, tok, width), BF),
        ),
        in_specs=[SCALARS] + [ANYWHERE] * (len(downs) + 2),
        out_specs=(VMEM, VMEM),
        scratch_shapes=[
            pltpu.VMEM((count(downs),) + downs[0].shape[1:], BF),
            pltpu.VMEM((4, tok, hidden), BF),
            pltpu.SemaphoreType.DMA((count(downs),)),
            pltpu.SemaphoreType.DMA((4,)),
        ],
        compiler_params=pltpu.CompilerParams(vmem_limit_bytes=14 * 2**20),
        cost_estimate=SMALL,
    )(scalars(down_where), *pinned(*downs, *hidden_feed))


def finish_kernel(parts_ref, out_ref):
    rows = out_ref.shape[1] // 2
    for side in range(2):
        total = parts_ref[0, side].astype(F32)
        for k in range(1, parts_ref.shape[0]):
            total = total + parts_ref[k, side].astype(F32)
        total = total.T.astype(BF)
        for n in range(out_ref.shape[0]):
            out_ref[n, side * rows : (side + 1) * rows, :] = total[n * rows : (n + 1) * rows]


def finish(parts, group):
    _, _, hidden, rows = parts.shape
    return pl.pallas_call(
        finish_kernel,
        out_shape=jax.ShapeDtypeStruct((group, 2 * rows // group, hidden), BF),
        in_specs=[VMEM],
        out_specs=VMEM,
        compiler_params=pltpu.CompilerParams(vmem_limit_bytes=8 * 2**20),
        cost_estimate=SMALL,
    )(parts)


def unmix_kernel(cut, x_ref, gate_ref, up_ref):
    group, rows, hidden = x_ref.shape
    rows //= 2
    for side, ref in ((0, gate_ref), (1, up_ref)):
        parts = [x_ref[n, side * rows : (side + 1) * rows, :].astype(F32) for n in range(group)]
        ref[...] = jnp.concatenate(
            [part[:, w * cut : (w + 1) * cut] for w in range(hidden // cut) for part in parts], 1
        )


def unmix(value, cut):
    group, rows, hidden = value.shape
    out = jax.ShapeDtypeStruct((rows // 2, group * hidden), F32)
    return pl.pallas_call(
        functools.partial(unmix_kernel, cut),
        out_shape=(out, out),
        in_specs=[VMEM],
        out_specs=(VMEM, VMEM),
        compiler_params=pltpu.CompilerParams(vmem_limit_bytes=8 * 2**20),
        cost_estimate=SMALL,
    )(value)


def middle_kernel(n, where, attended_ref, tokens_ref, gains_ref, *refs):
    stacks, (hidden_ref, middle_ref, inverse_ref, merge, sem) = refs[:n], refs[n:]
    for copy in starts(stacks, where, 0, merge, sem):
        copy.wait()
    width = tokens_ref.shape[1]
    full = merge[...].reshape(attended_ref.shape[1], width)
    middle = tokens_ref[...].astype(F32) + dims(attended_ref[...], full, 1, 0)
    inverse = lax.rsqrt(jnp.mean(middle * middle, -1, keepdims=True) + EPS)
    middle_ref[...] = middle
    inverse_ref[...] = inverse
    hidden_ref[...] = (middle * inverse * gains_ref[1:2, :]).astype(BF)


def middle_of(attended, tokens, gains, stacks, where):
    tok, width = tokens.shape
    outs = (
        jax.ShapeDtypeStruct((tok, width), BF),
        jax.ShapeDtypeStruct((tok, width), F32),
        jax.ShapeDtypeStruct((tok, 1), F32),
    )
    return pl.pallas_call(
        functools.partial(middle_kernel, len(stacks)),
        out_shape=outs,
        in_specs=[SCALARS] + [VMEM] * 3 + [ANYWHERE] * len(stacks),
        out_specs=(VMEM,) * 3,
        scratch_shapes=[
            pltpu.VMEM((count(stacks),) + stacks[0].shape[1:], BF),
            pltpu.SemaphoreType.DMA((count(stacks),)),
        ],
        compiler_params=pltpu.CompilerParams(vmem_limit_bytes=10 * 2**20),
        cost_estimate=SMALL,
    )(scalars(where), attended, tokens, gains, *stacks)


def turn_back_kernel(
    n, where, kept_ref, near_ref, far_ref, middle_ref, inverse_ref, gains_ref, cot_ref, *refs
):
    stacks, (slope_ref, low_ref, attended_ref, gain_ref, merge, sem) = refs[:n], refs[n:]
    copies = starts(stacks, where, 0, merge, sem)
    slope = kept_ref[...] + near_ref[...].astype(F32) + far_ref[...].astype(F32)
    inverse = inverse_ref[...]
    normed = middle_ref[...] * inverse
    gain_ref[...] = jnp.sum(slope * normed, 0, keepdims=True)
    scaled = slope * gains_ref[1:2, :]
    mean = jnp.mean(scaled * normed, -1, keepdims=True)
    slope_middle = cot_ref[...].astype(F32) + inverse * (scaled - normed * mean)
    slope_ref[...] = slope_middle
    low = slope_middle.astype(BF)
    low_ref[...] = low
    for copy in copies:
        copy.wait()
    full = merge[...].reshape(attended_ref.shape[0], low.shape[1])
    attended_ref[...] = dims(full, low, 1, 1).astype(BF)


def turn_back(kept, came_near, came_far, middle, inverse, gains, cotangent, stacks, where):
    tok, width = middle.shape
    outs = (
        jax.ShapeDtypeStruct((tok, width), F32),
        jax.ShapeDtypeStruct((tok, width), BF),
        jax.ShapeDtypeStruct((width, tok), BF),
        jax.ShapeDtypeStruct((1, width), F32),
    )
    return pl.pallas_call(
        functools.partial(turn_back_kernel, len(stacks)),
        out_shape=outs,
        in_specs=[SCALARS] + [VMEM] * 7 + [ANYWHERE] * len(stacks),
        out_specs=(VMEM,) * 4,
        scratch_shapes=[
            pltpu.VMEM((count(stacks),) + stacks[0].shape[1:], BF),
            pltpu.SemaphoreType.DMA((count(stacks),)),
        ],
        compiler_params=pltpu.CompilerParams(vmem_limit_bytes=12 * 2**20),
        cost_estimate=SMALL,
    )(
        scalars(where), kept, came_near, came_far, middle, inverse, gains, cotangent, *stacks
    )


def emit(total, order, held, sent_ref, kept_ref):
    held[...] = total.reshape(held.shape)
    half = sent_ref.shape[0]
    first = sent_ref.shape[2] - total.shape[1]
    for k in range(half):
        kept_ref[k, :, first:] = held[order[k]].astype(BF)
        sent_ref[k, :, first:] = held[order[half + k]].astype(BF)


def outer_kernel(order, left_ref, right_ref, sent_ref, kept_ref, held):
    emit(dims(left_ref[...], right_ref[...], 0, 0), order, held, sent_ref, kept_ref)


def blocks_out(order, width, columns):
    half = len(order) // 2
    rows = width // len(order)
    out = jax.ShapeDtypeStruct((half, rows, columns), BF)
    return out, pltpu.VMEM((len(order), rows, columns), F32)


def outer_blocks(order, left, right):
    tok, width = left.shape
    columns = right.shape[1]
    out, held = blocks_out(order, width, columns)
    return pl.pallas_call(
        outer_kernel,
        out_shape=(out, out),
        in_specs=[SCALARS, VMEM, VMEM],
        out_specs=(VMEM, VMEM),
        scratch_shapes=[held],
        compiler_params=pltpu.CompilerParams(vmem_limit_bytes=10 * 2**20),
        cost_estimate=SMALL,
    )(scalars(order), left, right)


def unturn(value, cosine, sine):
    half = DH // 2
    one, two = value[:half], value[half:]
    return [one * cosine + two * sine, two * cosine - one * sine]


def query_end_kernel(
    order, qmix_ref, qbasis_ref, cos_ref, sin_ref, hidden_ref, weights_ref, *refs
):
    part_ref, outs, (held_weights, wsem) = refs[0], refs[1:-2], refs[-2:]
    coming = pltpu.make_async_copy(weights_ref, held_weights, wsem)
    coming.start()
    cosine, sine = cos_ref[...], sin_ref[...]
    parts = []
    for r in range(RQ):
        parts += unturn(qbasis_ref[r * DH : (r + 1) * DH, :], cosine, sine)
    tok = cosine.shape[1]
    parts += [qmix_ref[...], jnp.zeros((LEFT - QB - QM, tok), F32)]
    slopes = jnp.concatenate(parts, 0).astype(BF)
    coming.wait()
    weights = held_weights[...].reshape(hidden_ref.shape[1], PACKED)[:, :LEFT]
    part_ref[...] = dims(slopes, weights, 0, 1)
    total = dims(hidden_ref[...], slopes, 0, 1)
    if len(outs) == 1:
        outs[0][...] = total.astype(BF)
    else:
        emit(total, order, outs[2], outs[0], outs[1])


def query_end(order, qmix, qbasis, cosine, sine, hidden, weights):
    tok, width = hidden.shape
    outs = [jax.ShapeDtypeStruct((tok, width), F32)]
    scratch = []
    if len(order) > 1:
        out, held = blocks_out(order, width, LEFT)
        outs += [out, out]
        scratch = [held]
    else:
        outs += [jax.ShapeDtypeStruct((width, LEFT), BF)]
    return pl.pallas_call(
        query_end_kernel,
        out_shape=tuple(outs),
        in_specs=[SCALARS] + [VMEM] * 5 + [ANYWHERE],
        out_specs=(VMEM,) * len(outs),
        scratch_shapes=scratch + [pltpu.VMEM(weights.shape, BF), pltpu.SemaphoreType.DMA],
        compiler_params=pltpu.CompilerParams(vmem_limit_bytes=12 * 2**20),
        cost_estimate=SMALL,
    )(scalars(order), qmix, qbasis, cosine, sine, hidden, *pinned(weights))


def key_end_kernel(
    order,
    kept_ref,
    came_ref,
    cos_ref,
    sin_ref,
    hidden_ref,
    weights_ref,
    part_ref,
    tokens_ref,
    inverse_ref,
    gains_ref,
    middle_ref,
    feed_gain_ref,
    *refs
):
    *refs, held_weights, wsem = refs
    coming = pltpu.make_async_copy(weights_ref, held_weights, wsem)
    coming.start()
    if order.shape[0] > 1:
        query_sent, query_kept, out_ref, away_ref, stay_ref, held = refs
        away_ref[:, :, :LEFT] = query_sent[...]
        stay_ref[:, :, :LEFT] = query_kept[...]
    else:
        out_ref, total_ref = refs
    cosine, sine = cos_ref[...], sin_ref[...]
    own = kept_ref[...] + came_ref[...].astype(F32)
    parts = []
    for r in range(RK):
        parts += unturn(own[KM + r * DH : KM + (r + 1) * DH], cosine, sine)
    tok, width = hidden_ref.shape
    parts += [own[2 * KM + KB :], own[:KM], own[KM + KB : 2 * KM + KB]]
    parts += [jnp.zeros((PACKED - GAINS, tok), F32)]
    slopes = jnp.concatenate(parts, 0).astype(BF)
    coming.wait()
    weights = held_weights[...].reshape(width, PACKED)[:, LEFT:]
    slope = part_ref[...] + dims(slopes, weights, 0, 1)
    inverse = inverse_ref[...]
    normed = tokens_ref[...].astype(F32) * inverse
    scaled = slope * gains_ref[0:1, :]
    mean = jnp.mean(scaled * normed, -1, keepdims=True)
    out_ref[...] = middle_ref[...] + inverse * (scaled - normed * mean)
    gain_slope = jnp.sum(slope * normed, 0, keepdims=True)
    total = dims(hidden_ref[...], slopes, 0, 1)
    rows = jnp.concatenate(
        [gain_slope, feed_gain_ref[...], jnp.zeros((PACKED - GAINS - 2, width), F32)], 0
    )
    columns = jnp.concatenate([jnp.zeros((128 - rows.shape[0], width), F32), rows], 0).T
    total = jnp.concatenate([total[:, :-128], total[:, -128:] + columns], 1)
    if order.shape[0] > 1:
        emit(total, order, held, away_ref, stay_ref)
    else:
        total_ref[...] = total.astype(BF)


def key_end(order, *args):
    tok, width = args[4].shape
    outs = [jax.ShapeDtypeStruct((tok, width), F32)]
    scratch = []
    if len(order) > 1:
        _, held = blocks_out(order, width, PACKED - LEFT)
        out, _ = blocks_out(order, width, PACKED)
        outs += [out, out]
        scratch = [held]
    else:
        outs += [jax.ShapeDtypeStruct((width, PACKED - LEFT), BF)]
    return pl.pallas_call(
        key_end_kernel,
        out_shape=tuple(outs),
        in_specs=[SCALARS] + [VMEM] * 5 + [ANYWHERE] + [VMEM] * (len(args) - 6),
        out_specs=(VMEM,) * len(outs),
        scratch_shapes=scratch + [pltpu.VMEM(args[5].shape, BF), pltpu.SemaphoreType.DMA],
        compiler_params=pltpu.CompilerParams(vmem_limit_bytes=14 * 2**20),
        cost_estimate=SMALL,
    )(scalars(order), *args[:5], *pinned(args[5]), *args[6:])


def key_parts(kv_ref, head, at):
    base = at + H * RK
    row = at + head * RK
    total = kv_ref[pl.ds(row, 1), :] * kv_ref[base : base + DH, :]
    total = total + kv_ref[pl.ds(row + 1, 1), :] * kv_ref[base + DH : base + 2 * DH, :]
    return (total * (1.0 / RK)).astype(BF)


def query_parts(qm_ref, qt_ref, head):
    total = qm_ref[pl.ds(head * RQ, 1), :] * qt_ref[0:DH, :]
    for r in range(1, RQ):
        total = total + qm_ref[pl.ds(head * RQ + r, 1), :] * qt_ref[r * DH : (r + 1) * DH, :]
    queries = (total * (1.0 / RQ)).astype(BF)
    return (queries.astype(F32) * DH**-0.5).astype(BF)


def attend_kernel(
    place_ref, qm_ref, qt_ref, k0, k1, k2, k3, attended_ref, probs_ref, kv_ref, bias
):
    pair = pl.program_id(0)
    tok, slots = bias.shape

    @pl.when(pair == 0)
    def _():
        for block, part in enumerate((k0, k1, k2, k3)):
            kv_ref[:, block * tok : (block + 1) * tok] = part[...].astype(F32)
        near, length = place_ref[0], place_ref[1]
        rows = near * tok + lax.broadcasted_iota(jnp.int32, (tok, tok), 0)
        for block, bit in enumerate((0, 2, 1, 3)):
            keys = (near ^ bit) * tok + lax.broadcasted_iota(jnp.int32, (tok, tok), 1)
            allowed = (keys <= rows) & (keys < length)
            bias[:, block * tok : (block + 1) * tok] = jnp.where(allowed, 0.0, NEG)

    outs = []
    for inner in range(PAIR):
        head = pair * PAIR + inner
        keys = key_parts(kv_ref, head, 0)
        values = key_parts(kv_ref, head, H * RK + RK * DH)
        queries = query_parts(qm_ref, qt_ref, head)
        scores = dims(queries, keys, 0, 0) + bias[...]
        peak = jnp.max(scores, -1, keepdims=True)
        powers = jnp.exp(scores - peak)
        total = jnp.sum(powers, -1, keepdims=True)
        probs = (powers * (1.0 / total)).astype(BF)
        probs_ref[inner] = probs
        outs.append(dims(probs, values, 1, 1))
    attended_ref[...] = jnp.concatenate(outs, 1).astype(BF)


def attend(places, query_mix, query_turned, factors):
    tok = query_mix.shape[1]
    slots = 4 * tok
    table = pltpu.HBM((factors[0].shape[0], slots), F32)
    return pl.pallas_call(
        attend_kernel,
        grid=(H // PAIR,),
        out_shape=(
            jax.ShapeDtypeStruct((tok, H * DH), BF),
            pltpu.HBM((H, tok, slots), BF),
            table,
        ),
        in_specs=[SCALARS, whole(query_mix), whole(query_turned)] + [whole(f) for f in factors],
        out_specs=(
            pl.BlockSpec((tok, PAIR * DH), lambda i: (0, i)),
            pl.BlockSpec((PAIR, tok, slots), lambda i: (i, 0, 0)),
            whole(table),
        ),
        scratch_shapes=[pltpu.VMEM((tok, slots), F32)],
        compiler_params=pltpu.CompilerParams(vmem_limit_bytes=16 * 2**20),
        cost_estimate=SMALL,
    )(places, query_mix, query_turned, *pinned(*factors))


def attend_back_kernel(*refs):
    qm_ref, qt_ref, kv_ref, slope_ref, probs_all = refs[:5]
    kept_ref, sent_ref, qmix_ref, qbasis_ref, mix_ref, basis_ref, probs_held, psem = refs[5:]
    pair = pl.program_id(0)
    vm = H * RK + RK * DH
    kb = RK * DH

    def coming(at):
        return pltpu.make_async_copy(
            probs_all.at[pl.ds(at * PAIR, PAIR)], probs_held.at[at % 2], psem.at[at % 2]
        )

    @pl.when(pair == 0)
    def _():
        coming(pair).start()
        basis_ref[...] = jnp.zeros_like(basis_ref)
        qbasis_ref[...] = jnp.zeros_like(qbasis_ref)

    @pl.when(pair + 1 < pl.num_programs(0))
    def _():
        coming(pair + 1).start()

    coming(pair).wait()
    probs_ref = probs_held.at[pair % 2]
    for inner in range(PAIR):
        head = pair * PAIR + inner
        keys = key_parts(kv_ref, head, 0)
        values = key_parts(kv_ref, head, vm)
        queries = query_parts(qm_ref, qt_ref, head)
        slope = slope_ref[inner * DH : (inner + 1) * DH, :]
        probs_low = probs_ref[inner]
        slope_probs = dims(slope, values, 0, 0)
        probs = probs_low.astype(F32)
        weighted = probs * slope_probs
        total = jnp.sum(weighted, -1, keepdims=True)
        slope_scores = (weighted - probs * total).astype(BF)
        slope_query = dims(keys, slope_scores, 1, 1) * (DH**-0.5 / RQ)
        slope_key = dims(queries, slope_scores, 1, 0) * (1.0 / RK)
        slope_value = dims(slope, probs_low, 1, 0) * (1.0 / RK)
        for r in range(RK):
            row = head * RK + r
            for at, piece, side in ((0, slope_key, 0), (vm, slope_value, 1)):
                base = at + H * RK + r * DH
                here = side * RK + r
                basis_ref[here * DH : (here + 1) * DH, :] += kv_ref[pl.ds(at + row, 1), :] * piece
                mix_ref[pl.ds(side * H * RK + row, 1), :] = jnp.sum(
                    piece * kv_ref[base : base + DH, :], 0, keepdims=True
                )
        for r in range(RQ):
            row = head * RQ + r
            cut = slice(r * DH, (r + 1) * DH)
            qbasis_ref[cut, :] += qm_ref[pl.ds(row, 1), :] * slope_query
            qmix_ref[pl.ds(row, 1), :] = jnp.sum(slope_query * qt_ref[cut, :], 0, keepdims=True)

    @pl.when(pair == pl.num_programs(0) - 1)
    def _():
        half = kept_ref.shape[2] * 2
        tok = kept_ref.shape[2]
        km = H * RK
        for base, ref, begin, rows in (
            (0, mix_ref, 0, km),
            (km, basis_ref, 0, kb),
            (vm, mix_ref, km, km),
            (vm + km, basis_ref, kb, kb),
        ):
            part = ref[begin : begin + rows, :]
            for block in range(2):
                kept_ref[block, base : base + rows, :] = part[:, block * tok : (block + 1) * tok]
                sent_ref[block, base : base + rows, :] = part[
                    :, half + block * tok : half + (block + 1) * tok
                ].astype(BF)


def attend_back(query_mix, query_turned, row_factors, slope_attended, probs):
    tok = query_mix.shape[1]
    rows, slots = row_factors.shape
    outs = (
        jax.ShapeDtypeStruct((2, rows, tok), F32),
        jax.ShapeDtypeStruct((2, rows, tok), BF),
        jax.ShapeDtypeStruct((H * RQ, tok), F32),
        jax.ShapeDtypeStruct((RQ * DH, tok), F32),
    )
    return pl.pallas_call(
        attend_back_kernel,
        grid=(H // PAIR,),
        out_shape=outs,
        in_specs=[
            whole(query_mix),
            whole(query_turned),
            whole(row_factors),
            pl.BlockSpec((PAIR * DH, tok), lambda i: (i, 0)),
            pl.BlockSpec(memory_space=pltpu.HBM),
        ],
        out_specs=tuple(whole(o) for o in outs),
        scratch_shapes=[
            pltpu.VMEM((2 * H * RK, slots), F32),
            pltpu.VMEM((2 * RK * DH, slots), F32),
            pltpu.VMEM((2, PAIR, tok, slots), BF),
            pltpu.SemaphoreType.DMA((2,)),
        ],
        compiler_params=pltpu.CompilerParams(vmem_limit_bytes=18 * 2**20),
        cost_estimate=SMALL,
    )(query_mix, query_turned, *pinned(row_factors), slope_attended, *pinned(probs))


QB, KB, VB = RQ * DH, RK * DH, RK * DH
QM, KM, VM = H * RQ, H * RK, H * RK
LEFT = 512
GAINS = LEFT + KB + VB + KM + VM
PACKED = 896


def steps_of_any_mesh(
    tokens, places, cosine, sine, packed, merge_weight, both, down_weight, cotangent
):
    tok, width = tokens.shape
    group, twice, hidden = both.shape
    rows = twice // 2
    cut = down_weight.shape[0]
    axes = ("wide", "narrow")
    packed = [lax.all_gather(packed, axes, axis=0, tiled=True)[None]]
    merge = [lax.all_gather(merge_weight, axes, axis=0, tiled=True)[None]]
    downs = [lax.all_gather(down_weight, "wide", axis=0, tiled=True)[None]]
    both = lax.all_to_all(both, "narrow", 0, 0, tiled=True)
    both = lax.all_gather(both, "wide", axis=0, tiled=False)
    both = both.reshape(-1, 2, rows, hidden).transpose(1, 0, 2, 3)
    both = both.reshape(2, 8, 4, width // 32, hidden).transpose(1, 2, 0, 3, 4)
    weights_in = ([both.reshape(8, 4, width // 16, hidden)], list(range(8)), downs, [0])

    hidden_one, inverse_one, gains, weights, query_mix, query_turned, own_factors = project(
        tokens, cosine, sine, packed, [0]
    )
    attended, probs, row_factors = attend(
        places, query_mix, query_turned, gather_narrow(own_factors)
    )
    hidden_two, middle, inverse_two = middle_of(attended, tokens, gains, merge, [0])
    own, far, close, cross = gather_narrow(hidden_two)
    cot_own, cot_far, cot_near, cot_cross = gather_narrow(cotangent)
    parts = [
        feed((own, close), (cot_own, cot_near), *weights_in),
        feed((far, cross), (cot_far, cot_cross), *weights_in),
    ]
    hidden_feed, slope_gate, slope_up = zip(*(part[:3] for part in parts))
    came_near = flip(parts[0][4], "narrow", 1)
    came_far = flip(add_low(parts[1][3], flip(parts[1][4], "narrow", 1)), "narrow", 2)
    full = slopes_of((own, close, far, cross), slope_gate, slope_up, list(range(width // 128)))
    full = full.transpose(1, 0, 3, 2).reshape(2, width, hidden)
    slopes = jnp.concatenate([scatter_wide(s).reshape(group, rows, hidden) for s in full], 1)
    slopes = lax.all_to_all(slopes.astype(BF), "narrow", 0, 0, tiled=True)
    cots = (cot_own, cot_near, cot_far, cot_cross)
    down_slope = scatter_wide(down_slopes(hidden_feed, cots, [0], cut)[0])
    kept, sent = feed_out(hidden_feed, downs, [0])
    fed = kept + flip(sent, "narrow", 1).astype(F32)
    fed = fed[0] + flip(fed[1].astype(BF), "narrow", 2).astype(F32)
    output = (middle + fed).astype(BF)

    slope_middle, slope_low, slope_attended, feed_gain_slope = turn_back(
        parts[0][3], came_near, came_far, middle, inverse_two, gains, cotangent, merge, [0]
    )
    merge_slope = scatter_all(dims(attended, slope_low, 0, 0).astype(BF))
    factors_in = (query_mix, query_turned, row_factors, slope_attended, probs)
    key_kept, key_sent, query_mix_slope, query_basis_slope = attend_back(*factors_in)
    key_pair = key_kept + flip(key_sent, "narrow", 1).astype(F32)
    key_came = flip(key_pair[1].astype(BF), "narrow", 2)
    part, query_slopes = query_end(
        [0], query_mix_slope, query_basis_slope, cosine, sine, hidden_one, weights
    )
    tokens_slope, key_slopes = key_end(
        [0], key_pair[0], key_came, cosine, sine, hidden_one, weights, part, tokens, inverse_one,
        gains, slope_middle, feed_gain_slope,
    )
    query_slopes, key_slopes = scatter_all(query_slopes), scatter_all(key_slopes)
    return output, tokens_slope, query_slopes, key_slopes, merge_slope, slopes, down_slope


def steps_of_small_mesh(
    tokens, places, cosine, sine, packed, merge_weight, both_in, down_weight, cotangent
):
    tok, width = tokens.shape
    cut = down_weight.shape[0]
    high, low = wide_place()
    rounds = lax.axis_size("wide") // 2
    group = lax.axis_size("narrow")
    join = lambda a, b: jnp.concatenate([a, b], 0)

    first = turned(jnp.concatenate([packed, merge_weight], 1)[None])
    both = lax.all_to_all(both_in, "narrow", 0, 0, tiled=True)
    first = tie(*first)
    one = jnp.concatenate([f[:, :, :PACKED] for f in first], 0)
    two = jnp.concatenate([f[:, :, PACKED:] for f in first], 0)
    one, one_came, two, two_came, both = tie(
        one, flip(one, "narrow", 2), two, flip(two, "wide", 1), both
    )
    one, two = join(one, one_came), join(two, two_came)
    pieces = [both[None]]
    one, one_came, two, two_came, piece = tie(
        one, flip(one, "wide", 1), two, flip(two, "narrow", 2), turn(pieces[0], 1)
    )
    one, two = join(one, one_came), join(two, two_came)
    where, merge_where = relative_blocks(), relative_blocks(True)
    both_where = [((high - k) % rounds) * 2 + low for k in range(rounds)] + [
        ((high - k) % rounds) * 2 + 1 - low for k in range(rounds)
    ]
    one, piece, down_own, first = tie(one, piece, down_weight, pieces[0])
    pieces += [piece, turn(piece, 1)]
    down_came = flip(down_own, "wide", 1)
    others = [flip(first, "wide", 1)]
    hidden_one, inverse_one, gains, weights, query_mix, query_turned, factor = project(
        tokens, cosine, sine, [one, flip(one, "narrow", 1)], where
    )
    factor, two, first, down_came = tie(factor, two, pieces[1], down_came)
    merge = [two, flip(two, "narrow", 1)]
    others.append(flip(first, "wide", 1))
    factor_far, factor_near, pieces[2], others[0], down_came = tie(
        flip(factor, "narrow", 2), flip(factor, "narrow", 1), pieces[2], others[0], down_came
    )
    pieces.append(turn(pieces[2], 1))
    pair = jnp.where(low == 0, jnp.stack([down_own, down_came]), jnp.stack([down_came, down_own]))
    pair = jnp.stack([pair.reshape(2 * cut, width)] * rounds)
    factor_cross, cot_own, first, pieces[3], others[1], pair = tie(
        flip(factor_far, "narrow", 1), cotangent, pieces[2], pieces[3], others[1], pair
    )
    downs = [ring_all_to_all(pair)]
    down_where = list(range(rounds))

    cot_far = flip(cot_own, "narrow", 2)
    others += [flip(first, "wide", 1), flip(pieces[3], "wide", 1)]
    attended, probs, row_factors = attend(
        places, query_mix, query_turned, (factor, factor_far, factor_near, factor_cross)
    )
    attended, cot_far, others[2], others[3], merge[1] = tie(
        attended, cot_far, others[2], others[3], merge[1]
    )
    hidden_two, middle, inverse_two = middle_of(attended, tokens, gains, merge, merge_where)
    own, cot_far = tie(hidden_two, cot_far)

    far, close = flip(own, "narrow", 2), flip(own, "narrow", 1)
    cot_near, cot_cross = flip(cot_own, "narrow", 1), flip(cot_far, "narrow", 1)
    weights_in = (pieces + others, both_where, downs, down_where)
    one = feed((own, close), (cot_own, cot_near), *weights_in)
    far, one_sent = tie(far, one[4])
    came_near = flip(one_sent, "narrow", 1)
    cross = flip(far, "narrow", 1)
    two = feed((far, cross), (cot_far, cot_cross), *weights_in)
    for_far = add_low(two[3], flip(two[4], "narrow", 1))
    hidden_feed, slope_gate, slope_up = zip(one[:3], two[:3])
    for_far, slope_gate, slope_up, came_near = tie(for_far, slope_gate, slope_up, came_near)
    came_far = flip(for_far, "narrow", 2)
    slots = (own, close, far, cross)
    cots = (cot_own, cot_near, cot_far, cot_cross)
    order = [2 * k + 1 - low for k in range(rounds)]
    to_send = slopes_of(slots, slope_gate, slope_up, order, True)
    *hidden_feed, gate_sent, up_sent = tie(*hidden_feed, *to_send)
    gate_came = flip(gate_sent, "wide", 1)
    down_parts = down_slopes(hidden_feed, cots, [0], cut)[0]
    slope_gate, slope_up, down_parts = tie(slope_gate, slope_up, down_parts)
    down_parts = ring_all_to_all(down_parts.reshape(rounds, 2 * cut, width))
    to_keep = slopes_of(slots, slope_gate, slope_up, [2 * k + low for k in range(rounds)])
    came_far, to_keep = tie(came_far, to_keep)

    slope_middle, slope_low, slope_attended, feed_gain_slope = turn_back(
        one[3], came_near, came_far, middle, inverse_two, gains, cotangent, merge, merge_where
    )
    merge_sent, merge_kept = outer_blocks(scatter_order(True), attended, slope_low)
    merge_sent, slope_attended, gate_came, up_sent = tie(
        merge_sent, slope_attended, gate_came, up_sent
    )
    up_came = flip(up_sent, "wide", 1)
    merge_came = flip(merge_sent, "narrow", 1)
    merge_sum = add_low(merge_kept, merge_came)
    slope_attended, merge_sum = tie(slope_attended, merge_sum)
    merge_came = flip(merge_sum[8:], "narrow", 2)
    key_kept, key_sent, query_mix_slope, query_basis_slope = attend_back(
        query_mix, query_turned, row_factors, slope_attended, probs
    )
    key_kept, key_sent, query_basis_slope, merge_came, up_came, down_parts = tie(
        key_kept, key_sent, query_basis_slope, merge_came, up_came, down_parts
    )
    key_came = flip(key_sent, "narrow", 1)
    key_pair = key_kept + key_came.astype(F32)
    key_far, up_came, query_basis_slope, merge_came = tie(
        key_pair[1].astype(BF), up_came, query_basis_slope, merge_came
    )
    merge_sum = add_low(merge_sum[:8], merge_came)
    key_came = flip(key_far, "narrow", 2)
    parts = ring_all_to_all(add_low(to_keep, jnp.stack([gate_came, up_came], 1)))
    merge_came = flip(merge_sum[4:], "wide", 1)
    order = scatter_order(True)
    part, query_sent, query_kept = query_end(
        order, query_mix_slope, query_basis_slope, cosine, sine, hidden_one, weights
    )
    key_came, part = tie(key_came, part)
    tokens_slope, ends_sent, ends = key_end(
        order, key_pair[0], key_came, cosine, sine, hidden_one, weights, part, tokens, inverse_one,
        gains, slope_middle, feed_gain_slope, query_sent, query_kept,
    )

    ends = add_low(ends, flip(ends_sent, "narrow", 1))
    ends, hidden_feed = tie(ends, hidden_feed)
    ends_came = flip(ends[8:], "narrow", 2)
    kept, sent = feed_out(hidden_feed, downs, down_where)
    ends_came, kept, sent = tie(ends_came, kept, sent)
    ends = add_low(ends[:8], ends_came)
    ends, sent, parts, down_parts = tie(ends, sent, parts, down_parts)
    down_sum = jnp.sum(down_parts.astype(F32), 0).reshape(2, cut, width)
    down_came = flip(pick(down_sum, 1 - low, 0).astype(BF), "wide", 1)
    ends_came = flip(ends[4:], "wide", 1)
    fed = kept + flip(sent, "narrow", 1).astype(F32)
    slopes = lax.all_to_all(finish(parts, group), "narrow", 0, 0, tiled=True)
    merge_sum = add_low(merge_sum[:4], merge_came)
    ends_came, fed, merge_sum = tie(ends_came, fed, merge_sum)
    ends = jnp.concatenate([add_low(ends[:4], ends_came), merge_sum], 2)
    ends, fed_far = tie(ends, fed[1].astype(BF))
    sums = spread_turns(ends)
    slopes = after(slopes, sums)
    fed_came = flip(fed_far, "narrow", 2)
    down_slope = pick(down_sum, low, 0) + down_came.astype(F32)
    merge_slope = sums[:, PACKED:]
    output = (middle + fed[0] + fed_came.astype(F32)).astype(BF)
    query_slopes, key_slopes = sums[:, :LEFT], sums[:, LEFT:PACKED]
    return output, tokens_slope, query_slopes, key_slopes, merge_slope, slopes, down_slope


def per_device(
    tokens,
    lengths,
    attend_gain,
    query_heads,
    query_basis,
    key_heads,
    key_basis,
    value_heads,
    value_basis,
    merge_weight,
    feed_gain,
    gate_weight,
    up_weight,
    down_weight,
    cotangent,
):
    tok, width = tokens.shape
    wide_count = lax.axis_size("wide")
    narrow_count = lax.axis_size("narrow")
    near = lax.axis_index("narrow")
    rows = gate_weight.shape[0]
    cut = down_weight.shape[0]
    hidden = cut * wide_count
    small = small_mesh()

    positions = (near * tok + jnp.arange(tok, dtype=jnp.int32)).astype(F32)
    frequency = jnp.power(10000.0, -2.0 * jnp.arange(DH // 2, dtype=F32) / DH)
    angles = frequency[:, None] * positions[None, :]
    cosine, sine = jnp.cos(angles), jnp.sin(angles)

    packed = jnp.concatenate(
        [
            query_basis,
            query_heads,
            jnp.zeros((rows, LEFT - QB - QM), BF),
            key_basis,
            value_basis,
            key_heads,
            value_heads,
            attend_gain[:, None],
            feed_gain[:, None],
            jnp.zeros((rows, PACKED - GAINS - 2), BF),
        ],
        1,
    )

    def columns(weight):
        parts = weight.reshape(rows, wide_count, narrow_count, cut).transpose(2, 0, 1, 3)
        return parts.reshape(narrow_count, rows, hidden)

    both_in = jnp.concatenate([columns(gate_weight), columns(up_weight)], 1)
    places = jnp.stack([near.astype(jnp.int32), lengths[0].astype(jnp.int32)])
    if small:
        exact = steps_of_small_mesh
    else:
        exact = steps_of_any_mesh
    output, tokens_slope, query_slopes, key_slopes, merge_slope, slopes, down_slope = exact(
        tokens, places, cosine, sine, packed, merge_weight, both_in, down_weight, cotangent
    )
    if small:
        slopes = unmix(slopes, cut)
    else:
        slopes = slopes.reshape(narrow_count, 2, rows, wide_count, cut).transpose(1, 2, 3, 0, 4)
        slopes = slopes.reshape(2, rows, hidden * narrow_count).astype(F32)

    base = GAINS - LEFT
    return (
        output,
        tokens_slope,
        key_slopes[:, base],
        query_slopes[:, QB : QB + QM],
        query_slopes[:, :QB],
        key_slopes[:, KB + VB : KB + VB + KM],
        key_slopes[:, :KB],
        key_slopes[:, KB + VB + KM : KB + VB + KM + VM],
        key_slopes[:, KB : KB + VB],
        merge_slope,
        key_slopes[:, base + 1],
        slopes[0],
        slopes[1],
        down_slope,
    )


def solution(mesh):
    both = ("wide", "narrow")
    row, vector = P(both, None), P(both)
    return jax.shard_map(
        per_device,
        mesh=mesh,
        in_specs=(row, P("wide"), vector) + (row,) * 7 + (vector,) + (row,) * 4,
        out_specs=(row, row, vector) + (row,) * 7 + (vector,) + (row,) * 3,
        check_vma=False,
    )
```

```python
import functools

import jax
import jax.numpy as jnp
from jax import lax
from jax.experimental import pallas as pl
from jax.experimental.pallas import tpu as pltpu
from jax.sharding import PartitionSpec as P

H = 16
DH = 64
RQ = 6
RK = 2
PAIR = 4
EPS = 1e-06
NEG = -1e30
BF = jnp.bfloat16
F32 = jnp.float32


def dims(left, right, left_dim, right_dim):
    return lax.dot_general(
        left, right, (((left_dim,), (right_dim,)), ((), ())), preferred_element_type=F32
    )


def flip(value, axis, bit):
    size = lax.axis_size(axis)
    return lax.ppermute(value, axis, [(i, i ^ bit) for i in range(size)])


def turn(value, steps):
    size = lax.axis_size("wide")
    return lax.ppermute(value, "wide", [(i, (i + 2 * steps) % size) for i in range(size)])


def small_mesh():
    return lax.axis_size("wide") == 8 and lax.axis_size("narrow") == 4


def wide_place():
    me = lax.axis_index("wide")
    return me // 2, me % 2


def tie(*values):
    return lax.optimization_barrier(values)


def after(value, *others):
    return lax.optimization_barrier((value, others))[0]


def ring_groups():
    size = lax.axis_size("wide")
    return [list(range(x, size, 2)) for x in range(2)]


def ring_all_to_all(value):
    return lax.all_to_all(value, "wide", 0, 0, axis_index_groups=ring_groups(), tiled=True)


def pick(value, index, axis):
    return lax.dynamic_index_in_dim(value, index, axis, keepdims=False)


def spread_high(blocks):
    return jnp.sum(ring_all_to_all(blocks).astype(F32), 0)


def scatter_wide(value):
    return lax.psum_scatter(value, "wide", scatter_dimension=0, tiled=True).astype(F32)


def turned(value):
    rounds = lax.axis_size("wide") // 2
    return [value] + [turn(value, k) for k in range(1, rounds)]


def joined(value, axis, bit):
    return jnp.concatenate([value, flip(value, axis, bit)], 0)


def relative_blocks(swapped=False):
    high, low = wide_place()
    rounds = lax.axis_size("wide") // 2
    near = lax.axis_index("narrow")
    return [
        (((high - k) % rounds) * 2 + (low ^ x)) * 4 + (near ^ (2 * y) ^ c)
        for c in (0, 1)
        for x, y in ([(0, 0), (1, 0), (0, 1), (1, 1)] if swapped else [(0, 0), (0, 1), (1, 0), (1, 1)])
        for k in range(rounds)
    ]


def scatter_all(value):
    return lax.psum_scatter(value, ("wide", "narrow"), scatter_dimension=0, tiled=True).astype(F32)


def scatter_order(turning):
    high, low = wide_place()
    rounds = lax.axis_size("wide") // 2
    near = lax.axis_index("narrow")
    return [
        (((high + k) % rounds if turning else k) * 2 + (low ^ x)) * 4 + (near ^ (2 * y) ^ c)
        for c in (0, 1)
        for y in (0, 1)
        for x in (0, 1)
        for k in range(rounds)
    ]


def spread_turns(blocks):
    total = blocks[0].astype(F32)
    for k in range(1, blocks.shape[0]):
        total = total + turn(blocks[k], k).astype(F32)
    return total


def add_low(kept, came):
    return (kept.astype(F32) + came.astype(F32)).astype(BF)


def gather_narrow(value):
    far = flip(value, "narrow", 2)
    return [value, far, flip(value, "narrow", 1), flip(far, "narrow", 1)]


def starts(stacks, where_ref, first, target, sem):
    copies = []
    for stack in stacks:
        for k in range(stack.shape[0]):
            at = len(copies)
            copies.append(
                pltpu.make_async_copy(
                    stack.at[k], target.at[where_ref[first + at]], sem.at[first + at]
                )
            )
            copies[-1].start()
    return copies


def count(stacks):
    return sum(stack.shape[0] for stack in stacks)


def whole(array):
    return pl.BlockSpec(array.shape, lambda *i: (0,) * len(array.shape))


ANYWHERE = pl.BlockSpec(memory_space=pl.ANY)


def pinned(*arrays):
    return [pltpu.with_memory_space_constraint(a, pltpu.HBM) for a in arrays]


SCALARS = pl.BlockSpec(memory_space=pltpu.SMEM)
SMALL = pl.CostEstimate(flops=3 * 10**9, bytes_accessed=2**22, transcendentals=0)


def scalars(*lists):
    return jnp.stack([jnp.asarray(v, jnp.int32) for one in lists for v in one])


def project_kernel(n, where, tokens_ref, cos_ref, sin_ref, *refs):
    packed, refs = refs[:n], refs[n:]
    hidden_ref, inverse_ref, gains_ref, packed_out, qm_ref, qt_ref, kv_ref = refs[:7]
    packed_ref, sem, out_sem = refs[7:]
    copies = starts(packed, where, 0, packed_ref, sem)
    source = tokens_ref[...].astype(F32)
    inverse = lax.rsqrt(jnp.mean(source * source, -1, keepdims=True) + EPS)
    inverse_ref[...] = inverse
    normed = source * inverse
    for copy in copies:
        copy.wait()
    outgoing = pltpu.make_async_copy(packed_ref, packed_out, out_sem)
    outgoing.start()
    width = source.shape[1]
    weights = packed_ref[...].reshape(width, PACKED)
    gains = weights[:, PACKED - 128 :].astype(F32).T
    at = GAINS - (PACKED - 128)
    gains_ref[...] = gains[at : at + 8]
    hidden = (normed * gains[at : at + 1]).astype(BF)
    hidden_ref[...] = hidden
    factors = dims(hidden, weights, 1, 0).T
    cosine, sine = cos_ref[...], sin_ref[...]
    half = DH // 2
    for r in range(RQ + RK):
        base = r * DH if r < RQ else LEFT + (r - RQ) * DH
        one = factors[base : base + half]
        two = factors[base + half : base + DH]
        a, b = one * cosine - two * sine, one * sine + two * cosine
        if r < RQ:
            qt_ref[base : base + half, :] = a
            qt_ref[base + half : base + DH, :] = b
        else:
            row = KM + (r - RQ) * DH
            kv_ref[row : row + half, :] = a.astype(BF)
            kv_ref[row + half : row + DH, :] = b.astype(BF)
    qm_ref[...] = factors[QB : QB + QM]
    base = LEFT + KB
    kv_ref[2 * KM + KB :, :] = factors[base : base + VB].astype(BF)
    base += VB
    kv_ref[0:KM, :] = factors[base : base + KM].astype(BF)
    kv_ref[KM + KB : 2 * KM + KB, :] = factors[base + KM : base + 2 * KM].astype(BF)
    outgoing.wait()


VMEM = pl.BlockSpec(memory_space=pltpu.VMEM)


def project(tokens, cosine, sine, packed, where):
    tok, width = tokens.shape
    outs = (
        jax.ShapeDtypeStruct((tok, width), BF),
        jax.ShapeDtypeStruct((tok, 1), F32),
        jax.ShapeDtypeStruct((8, width), F32),
        pltpu.HBM((count(packed),) + packed[0].shape[1:], BF),
        jax.ShapeDtypeStruct((QM, tok), F32),
        jax.ShapeDtypeStruct((QB, tok), F32),
        jax.ShapeDtypeStruct((2 * (KM + KB), tok), BF),
    )
    return pl.pallas_call(
        functools.partial(project_kernel, len(packed)),
        out_shape=outs,
        in_specs=[SCALARS] + [VMEM] * 3 + [ANYWHERE] * len(packed),
        out_specs=(VMEM,) * 3 + (ANYWHERE,) + (VMEM,) * 3,
        scratch_shapes=[
            pltpu.VMEM((count(packed),) + packed[0].shape[1:], BF),
            pltpu.SemaphoreType.DMA((count(packed),)),
            pltpu.SemaphoreType.DMA,
        ],
        compiler_params=pltpu.CompilerParams(vmem_limit_bytes=14 * 2**20),
        cost_estimate=SMALL,
    )(scalars(where), tokens, cosine, sine, *packed)


def halves_of(both_ref, width, hidden):
    rows = both_ref.shape[2] // 2
    return (
        both_ref[:, :, :rows, :].reshape(width, hidden),
        both_ref[:, :, rows:, :].reshape(width, hidden),
    )


def feed_kernel(nb, nd, where, *refs):
    pieces, refs = refs[:2], refs[2:]
    cots, refs = refs[:2], refs[2:]
    boths, refs = refs[:nb], refs[nb:]
    downs, refs = refs[:nd], refs[nd:]
    hf_out, sg_out, su_out, kept_ref, sent_ref, hid, cot, wgu, wd, held, sem, psem, osem = refs
    outgoing = []
    width, hidden = hid.shape[2], wgu.shape[3]
    loads = [
        [
            pltpu.make_async_copy(pieces[b], hid.at[b], psem.at[b]),
            pltpu.make_async_copy(cots[b], cot.at[b], psem.at[2 + b]),
        ]
        for b in range(2)
    ]
    loads[0][0].start()
    in_both = starts(boths, where, 0, wgu, sem)
    loads[0][1].start()
    in_down = starts(downs, where, count(boths), wd, sem)
    for copy in loads[1]:
        copy.start()
    for b in range(2):
        loads[b][0].wait()
        if b == 0:
            for copy in in_both:
                copy.wait()
        gate_all, up_all = halves_of(wgu, width, hidden)
        gate = dims(hid[b], gate_all, 1, 0)
        upward = dims(hid[b], up_all, 1, 0)
        loads[b][1].wait()
        if b == 0:
            for copy in in_down:
                copy.wait()
        down_all = wd[...].reshape(hidden, width)
        slope = dims(cot[b], down_all, 1, 1)
        sig = jax.nn.sigmoid(gate)
        silu = gate * sig
        held[0, b] = (silu * upward).astype(BF)
        slope_up = (slope * silu).astype(BF)
        slope_gate = (slope * upward * sig * (1.0 + gate * (1.0 - sig))).astype(BF)
        held[1, b] = slope_gate
        held[2, b] = slope_up
        for k, out in enumerate((hf_out, sg_out, su_out)):
            outgoing.append(pltpu.make_async_copy(held.at[k, b], out.at[b], osem.at[k, b]))
            outgoing[-1].start()
        back = dims(slope_gate, gate_all, 1, 1) + dims(slope_up, up_all, 1, 1)
        if b == 0:
            kept_ref[...] = back
        else:
            sent_ref[...] = back.astype(BF)
    for copy in outgoing:
        copy.wait()


def feed(pieces, cots, boths, both_where, downs, down_where):
    tok, width = pieces[0].shape
    hidden = boths[0].shape[3]
    low = pltpu.HBM((2, tok, hidden), BF)
    outs = (
        low,
        low,
        low,
        jax.ShapeDtypeStruct((tok, width), F32),
        jax.ShapeDtypeStruct((tok, width), BF),
    )
    blocks = lambda stacks: pltpu.VMEM((count(stacks),) + stacks[0].shape[1:], BF)
    total = count(boths) + count(downs)
    return pl.pallas_call(
        functools.partial(feed_kernel, len(boths), len(downs)),
        out_shape=outs,
        in_specs=[SCALARS] + [ANYWHERE] * (4 + len(boths) + len(downs)),
        out_specs=(ANYWHERE,) * 3 + (VMEM,) * 2,
        scratch_shapes=[
            pltpu.VMEM((2, tok, width), BF),
            pltpu.VMEM((2, tok, width), BF),
            blocks(boths),
            blocks(downs),
            pltpu.VMEM((3, 2, tok, hidden), BF),
            pltpu.SemaphoreType.DMA((total,)),
            pltpu.SemaphoreType.DMA((4,)),
            pltpu.SemaphoreType.DMA((3, 2)),
        ],
        compiler_params=pltpu.CompilerParams(vmem_limit_bytes=20 * 2**20),
        cost_estimate=SMALL,
    )(scalars(both_where, down_where), *pinned(*pieces, *cots, *boths, *downs))


def bring(sources, target, sem):
    copies = []
    at = 0
    for source in sources:
        parts = [source] if len(source.shape) == 2 else [source.at[k] for k in range(source.shape[0])]
        for part in parts:
            copies.append(pltpu.make_async_copy(part, target.at[at], sem.at[at]))
            copies[-1].start()
            at += 1
    return copies


def slopes_kernel(blocks, order, *refs):
    *outs, hid, gates, ups, hsem, gsem, usem = refs[8:]
    out = outs[0]
    copies = bring(refs[:4], hid, hsem) + bring(refs[4:6], gates, gsem)
    later = bring(refs[6:8], ups, usem)
    for copy in copies:
        copy.wait()
    rows, hidden = out.shape[-1], out.shape[-2]
    columns = []
    for k in range(blocks):
        at = pl.multiple_of(order[k] * rows, 128)
        columns.append(hid[:, :, pl.ds(at, rows)].reshape(-1, rows))
    chosen = jnp.concatenate(columns, 1)
    for side, held in enumerate((gates, ups)):
        if side == 1:
            for copy in later:
                copy.wait()
        result = dims(held[...].reshape(-1, hidden), chosen, 0, 0).astype(BF)
        for k in range(blocks):
            part = result[:, k * rows : (k + 1) * rows]
            if len(outs) == 2:
                outs[side][k] = part
            else:
                out[k, side] = part


def slopes_of(pieces, slope_gate, slope_up, order, apart=False):
    tok, width = pieces[0].shape
    hidden = slope_gate[0].shape[2]
    rows = 128
    return pl.pallas_call(
        functools.partial(slopes_kernel, len(order)),
        out_shape=(jax.ShapeDtypeStruct((len(order), hidden, rows), BF),) * 2
        if apart
        else jax.ShapeDtypeStruct((len(order), 2, hidden, rows), BF),
        in_specs=[SCALARS] + [ANYWHERE] * 8,
        out_specs=(VMEM, VMEM) if apart else VMEM,
        scratch_shapes=[
            pltpu.VMEM((4, tok, width), BF),
            pltpu.VMEM((4, tok, hidden), BF),
            pltpu.VMEM((4, tok, hidden), BF),
        ]
        + [pltpu.SemaphoreType.DMA((4,))] * 3,
        compiler_params=pltpu.CompilerParams(vmem_limit_bytes=18 * 2**20),
        cost_estimate=SMALL,
    )(scalars(order), *pinned(*pieces, *slope_gate, *slope_up))


def down_kernel(blocks, order, *refs):
    feeds, cots, fsem, csem = refs[-4:]
    for copy in bring(refs[:2], feeds, fsem) + bring(refs[2:6], cots, csem):
        copy.wait()
    outs = refs[6:-4]
    hidden, width = feeds.shape[2], cots.shape[2]
    total = dims(feeds[...].reshape(-1, hidden), cots[...].reshape(-1, width), 0, 0)
    if blocks == 1:
        outs[0][...] = total.astype(BF)
    else:
        sent_ref, kept_ref, held = outs
        held[...] = total.reshape(held.shape)
        for k in range(blocks // 2):
            kept_ref[k] = held[order[2 * k]].astype(BF)
            sent_ref[k] = held[order[2 * k + 1]].astype(BF)


def down_slopes(hidden_feed, cots, order, cut):
    tok, width = cots[0].shape
    hidden = hidden_feed[0].shape[2]
    if len(order) > 1:
        out = jax.ShapeDtypeStruct((len(order) // 2, cut, width), BF)
        outs, scratch = (out, out), [pltpu.VMEM((len(order), cut, width), F32)]
    else:
        outs, scratch = (jax.ShapeDtypeStruct((hidden, width), BF),), []
    return pl.pallas_call(
        functools.partial(down_kernel, len(order)),
        out_shape=outs,
        in_specs=[SCALARS] + [ANYWHERE] * 6,
        out_specs=(VMEM,) * len(outs),
        scratch_shapes=scratch
        + [
            pltpu.VMEM((4, tok, hidden), BF),
            pltpu.VMEM((4, tok, width), BF),
            pltpu.SemaphoreType.DMA((4,)),
            pltpu.SemaphoreType.DMA((4,)),
        ],
        compiler_params=pltpu.CompilerParams(vmem_limit_bytes=20 * 2**20),
        cost_estimate=SMALL,
    )(scalars(order), *pinned(*hidden_feed, *cots))


def feed_out_kernel(nd, where, *refs):
    downs, (f0, f1, kept_ref, sent_ref, wd, feeds, sem, fsem) = refs[:nd], refs[nd:]
    for copy in starts(downs, where, 0, wd, sem) + bring((f0, f1), feeds, fsem):
        copy.wait()
    down_all = wd[...].reshape(feeds.shape[2], wd.shape[2])
    for part in range(2):
        kept_ref[part] = dims(feeds[2 * part], down_all, 1, 0)
        sent_ref[part] = dims(feeds[2 * part + 1], down_all, 1, 0).astype(BF)


def feed_out(hidden_feed, downs, down_where):
    tok, hidden = hidden_feed[0].shape[1:]
    width = downs[0].shape[2]
    return pl.pallas_call(
        functools.partial(feed_out_kernel, len(downs)),
        out_shape=(
            jax.ShapeDtypeStruct((2, tok, width), F32),
            jax.ShapeDtypeStruct((2, tok, width), BF),
        ),
        in_specs=[SCALARS] + [ANYWHERE] * (len(downs) + 2),
        out_specs=(VMEM, VMEM),
        scratch_shapes=[
            pltpu.VMEM((count(downs),) + downs[0].shape[1:], BF),
            pltpu.VMEM((4, tok, hidden), BF),
            pltpu.SemaphoreType.DMA((count(downs),)),
            pltpu.SemaphoreType.DMA((4,)),
        ],
        compiler_params=pltpu.CompilerParams(vmem_limit_bytes=14 * 2**20),
        cost_estimate=SMALL,
    )(scalars(down_where), *pinned(*downs, *hidden_feed))


def finish_kernel(parts_ref, out_ref):
    rows = out_ref.shape[1] // 2
    for side in range(2):
        total = parts_ref[0, side].astype(F32)
        for k in range(1, parts_ref.shape[0]):
            total = total + parts_ref[k, side].astype(F32)
        total = total.T.astype(BF)
        for n in range(out_ref.shape[0]):
            out_ref[n, side * rows : (side + 1) * rows, :] = total[n * rows : (n + 1) * rows]


def finish(parts, group):
    _, _, hidden, rows = parts.shape
    return pl.pallas_call(
        finish_kernel,
        out_shape=jax.ShapeDtypeStruct((group, 2 * rows // group, hidden), BF),
        in_specs=[VMEM],
        out_specs=VMEM,
        compiler_params=pltpu.CompilerParams(vmem_limit_bytes=8 * 2**20),
        cost_estimate=SMALL,
    )(parts)


def unmix_kernel(cut, x_ref, gate_ref, up_ref):
    group, rows, hidden = x_ref.shape
    rows //= 2
    for side, ref in ((0, gate_ref), (1, up_ref)):
        parts = [x_ref[n, side * rows : (side + 1) * rows, :].astype(F32) for n in range(group)]
        ref[...] = jnp.concatenate(
            [part[:, w * cut : (w + 1) * cut] for w in range(hidden // cut) for part in parts], 1
        )


def unmix(value, cut):
    group, rows, hidden = value.shape
    out = jax.ShapeDtypeStruct((rows // 2, group * hidden), F32)
    return pl.pallas_call(
        functools.partial(unmix_kernel, cut),
        out_shape=(out, out),
        in_specs=[VMEM],
        out_specs=(VMEM, VMEM),
        compiler_params=pltpu.CompilerParams(vmem_limit_bytes=8 * 2**20),
        cost_estimate=SMALL,
    )(value)


def middle_kernel(n, where, attended_ref, tokens_ref, gains_ref, *refs):
    stacks, (hidden_ref, middle_ref, inverse_ref, merge, sem) = refs[:n], refs[n:]
    for copy in starts(stacks, where, 0, merge, sem):
        copy.wait()
    width = tokens_ref.shape[1]
    full = merge[...].reshape(attended_ref.shape[1], width)
    middle = tokens_ref[...].astype(F32) + dims(attended_ref[...], full, 1, 0)
    inverse = lax.rsqrt(jnp.mean(middle * middle, -1, keepdims=True) + EPS)
    middle_ref[...] = middle
    inverse_ref[...] = inverse
    hidden_ref[...] = (middle * inverse * gains_ref[1:2, :]).astype(BF)


def middle_of(attended, tokens, gains, stacks, where):
    tok, width = tokens.shape
    outs = (
        jax.ShapeDtypeStruct((tok, width), BF),
        jax.ShapeDtypeStruct((tok, width), F32),
        jax.ShapeDtypeStruct((tok, 1), F32),
    )
    return pl.pallas_call(
        functools.partial(middle_kernel, len(stacks)),
        out_shape=outs,
        in_specs=[SCALARS] + [VMEM] * 3 + [ANYWHERE] * len(stacks),
        out_specs=(VMEM,) * 3,
        scratch_shapes=[
            pltpu.VMEM((count(stacks),) + stacks[0].shape[1:], BF),
            pltpu.SemaphoreType.DMA((count(stacks),)),
        ],
        compiler_params=pltpu.CompilerParams(vmem_limit_bytes=10 * 2**20),
        cost_estimate=SMALL,
    )(scalars(where), attended, tokens, gains, *stacks)


def turn_back_kernel(
    n, where, kept_ref, near_ref, far_ref, middle_ref, inverse_ref, gains_ref, cot_ref, *refs
):
    stacks, (slope_ref, low_ref, attended_ref, gain_ref, merge, sem) = refs[:n], refs[n:]
    copies = starts(stacks, where, 0, merge, sem)
    slope = kept_ref[...] + near_ref[...].astype(F32) + far_ref[...].astype(F32)
    inverse = inverse_ref[...]
    normed = middle_ref[...] * inverse
    gain_ref[...] = jnp.sum(slope * normed, 0, keepdims=True)
    scaled = slope * gains_ref[1:2, :]
    mean = jnp.mean(scaled * normed, -1, keepdims=True)
    slope_middle = cot_ref[...].astype(F32) + inverse * (scaled - normed * mean)
    slope_ref[...] = slope_middle
    low = slope_middle.astype(BF)
    low_ref[...] = low
    for copy in copies:
        copy.wait()
    full = merge[...].reshape(attended_ref.shape[0], low.shape[1])
    attended_ref[...] = dims(full, low, 1, 1).astype(BF)


def turn_back(kept, came_near, came_far, middle, inverse, gains, cotangent, stacks, where):
    tok, width = middle.shape
    outs = (
        jax.ShapeDtypeStruct((tok, width), F32),
        jax.ShapeDtypeStruct((tok, width), BF),
        jax.ShapeDtypeStruct((width, tok), BF),
        jax.ShapeDtypeStruct((1, width), F32),
    )
    return pl.pallas_call(
        functools.partial(turn_back_kernel, len(stacks)),
        out_shape=outs,
        in_specs=[SCALARS] + [VMEM] * 7 + [ANYWHERE] * len(stacks),
        out_specs=(VMEM,) * 4,
        scratch_shapes=[
            pltpu.VMEM((count(stacks),) + stacks[0].shape[1:], BF),
            pltpu.SemaphoreType.DMA((count(stacks),)),
        ],
        compiler_params=pltpu.CompilerParams(vmem_limit_bytes=12 * 2**20),
        cost_estimate=SMALL,
    )(
        scalars(where), kept, came_near, came_far, middle, inverse, gains, cotangent, *stacks
    )


def emit(total, order, held, sent_ref, kept_ref):
    held[...] = total.reshape(held.shape)
    half = sent_ref.shape[0]
    first = sent_ref.shape[2] - total.shape[1]
    for k in range(half):
        kept_ref[k, :, first:] = held[order[k]].astype(BF)
        sent_ref[k, :, first:] = held[order[half + k]].astype(BF)


def outer_kernel(order, left_ref, right_ref, sent_ref, kept_ref, held):
    emit(dims(left_ref[...], right_ref[...], 0, 0), order, held, sent_ref, kept_ref)


def blocks_out(order, width, columns):
    half = len(order) // 2
    rows = width // len(order)
    out = jax.ShapeDtypeStruct((half, rows, columns), BF)
    return out, pltpu.VMEM((len(order), rows, columns), F32)


def outer_blocks(order, left, right):
    tok, width = left.shape
    columns = right.shape[1]
    out, held = blocks_out(order, width, columns)
    return pl.pallas_call(
        outer_kernel,
        out_shape=(out, out),
        in_specs=[SCALARS, VMEM, VMEM],
        out_specs=(VMEM, VMEM),
        scratch_shapes=[held],
        compiler_params=pltpu.CompilerParams(vmem_limit_bytes=10 * 2**20),
        cost_estimate=SMALL,
    )(scalars(order), left, right)


def unturn(value, cosine, sine):
    half = DH // 2
    one, two = value[:half], value[half:]
    return [one * cosine + two * sine, two * cosine - one * sine]


def query_end_kernel(
    order, qmix_ref, qbasis_ref, cos_ref, sin_ref, hidden_ref, weights_ref, *refs
):
    part_ref, outs, (held_weights, wsem) = refs[0], refs[1:-2], refs[-2:]
    coming = pltpu.make_async_copy(weights_ref, held_weights, wsem)
    coming.start()
    cosine, sine = cos_ref[...], sin_ref[...]
    parts = []
    for r in range(RQ):
        parts += unturn(qbasis_ref[r * DH : (r + 1) * DH, :], cosine, sine)
    tok = cosine.shape[1]
    parts += [qmix_ref[...], jnp.zeros((LEFT - QB - QM, tok), F32)]
    slopes = jnp.concatenate(parts, 0).astype(BF)
    coming.wait()
    weights = held_weights[...].reshape(hidden_ref.shape[1], PACKED)[:, :LEFT]
    part_ref[...] = dims(slopes, weights, 0, 1)
    total = dims(hidden_ref[...], slopes, 0, 1)
    if len(outs) == 1:
        outs[0][...] = total.astype(BF)
    else:
        emit(total, order, outs[2], outs[0], outs[1])


def query_end(order, qmix, qbasis, cosine, sine, hidden, weights):
    tok, width = hidden.shape
    outs = [jax.ShapeDtypeStruct((tok, width), F32)]
    scratch = []
    if len(order) > 1:
        out, held = blocks_out(order, width, LEFT)
        outs += [out, out]
        scratch = [held]
    else:
        outs += [jax.ShapeDtypeStruct((width, LEFT), BF)]
    return pl.pallas_call(
        query_end_kernel,
        out_shape=tuple(outs),
        in_specs=[SCALARS] + [VMEM] * 5 + [ANYWHERE],
        out_specs=(VMEM,) * len(outs),
        scratch_shapes=scratch + [pltpu.VMEM(weights.shape, BF), pltpu.SemaphoreType.DMA],
        compiler_params=pltpu.CompilerParams(vmem_limit_bytes=12 * 2**20),
        cost_estimate=SMALL,
    )(scalars(order), qmix, qbasis, cosine, sine, hidden, *pinned(weights))


def key_end_kernel(
    order,
    kept_ref,
    came_ref,
    cos_ref,
    sin_ref,
    hidden_ref,
    weights_ref,
    part_ref,
    tokens_ref,
    inverse_ref,
    gains_ref,
    middle_ref,
    feed_gain_ref,
    *refs
):
    *refs, held_weights, wsem = refs
    coming = pltpu.make_async_copy(weights_ref, held_weights, wsem)
    coming.start()
    if order.shape[0] > 1:
        query_sent, query_kept, out_ref, away_ref, stay_ref, held = refs
        away_ref[:, :, :LEFT] = query_sent[...]
        stay_ref[:, :, :LEFT] = query_kept[...]
    else:
        out_ref, total_ref = refs
    cosine, sine = cos_ref[...], sin_ref[...]
    own = kept_ref[...] + came_ref[...].astype(F32)
    parts = []
    for r in range(RK):
        parts += unturn(own[KM + r * DH : KM + (r + 1) * DH], cosine, sine)
    tok, width = hidden_ref.shape
    parts += [own[2 * KM + KB :], own[:KM], own[KM + KB : 2 * KM + KB]]
    parts += [jnp.zeros((PACKED - GAINS, tok), F32)]
    slopes = jnp.concatenate(parts, 0).astype(BF)
    coming.wait()
    weights = held_weights[...].reshape(width, PACKED)[:, LEFT:]
    slope = part_ref[...] + dims(slopes, weights, 0, 1)
    inverse = inverse_ref[...]
    normed = tokens_ref[...].astype(F32) * inverse
    scaled = slope * gains_ref[0:1, :]
    mean = jnp.mean(scaled * normed, -1, keepdims=True)
    out_ref[...] = middle_ref[...] + inverse * (scaled - normed * mean)
    gain_slope = jnp.sum(slope * normed, 0, keepdims=True)
    total = dims(hidden_ref[...], slopes, 0, 1)
    rows = jnp.concatenate(
        [gain_slope, feed_gain_ref[...], jnp.zeros((PACKED - GAINS - 2, width), F32)], 0
    )
    columns = jnp.concatenate([jnp.zeros((128 - rows.shape[0], width), F32), rows], 0).T
    total = jnp.concatenate([total[:, :-128], total[:, -128:] + columns], 1)
    if order.shape[0] > 1:
        emit(total, order, held, away_ref, stay_ref)
    else:
        total_ref[...] = total.astype(BF)


def key_end(order, *args):
    tok, width = args[4].shape
    outs = [jax.ShapeDtypeStruct((tok, width), F32)]
    scratch = []
    if len(order) > 1:
        _, held = blocks_out(order, width, PACKED - LEFT)
        out, _ = blocks_out(order, width, PACKED)
        outs += [out, out]
        scratch = [held]
    else:
        outs += [jax.ShapeDtypeStruct((width, PACKED - LEFT), BF)]
    return pl.pallas_call(
        key_end_kernel,
        out_shape=tuple(outs),
        in_specs=[SCALARS] + [VMEM] * 5 + [ANYWHERE] + [VMEM] * (len(args) - 6),
        out_specs=(VMEM,) * len(outs),
        scratch_shapes=scratch + [pltpu.VMEM(args[5].shape, BF), pltpu.SemaphoreType.DMA],
        compiler_params=pltpu.CompilerParams(vmem_limit_bytes=14 * 2**20),
        cost_estimate=SMALL,
    )(scalars(order), *args[:5], *pinned(args[5]), *args[6:])


def key_parts(kv_ref, head, at):
    base = at + H * RK
    row = at + head * RK
    total = kv_ref[pl.ds(row, 1), :] * kv_ref[base : base + DH, :]
    total = total + kv_ref[pl.ds(row + 1, 1), :] * kv_ref[base + DH : base + 2 * DH, :]
    return (total * (1.0 / RK)).astype(BF)


def query_parts(qm_ref, qt_ref, head):
    total = qm_ref[pl.ds(head * RQ, 1), :] * qt_ref[0:DH, :]
    for r in range(1, RQ):
        total = total + qm_ref[pl.ds(head * RQ + r, 1), :] * qt_ref[r * DH : (r + 1) * DH, :]
    queries = (total * (1.0 / RQ)).astype(BF)
    return (queries.astype(F32) * DH**-0.5).astype(BF)


def attend_kernel(
    place_ref, qm_ref, qt_ref, k0, k1, k2, k3, attended_ref, probs_ref, kv_ref, bias
):
    pair = pl.program_id(0)
    tok, slots = bias.shape

    @pl.when(pair == 0)
    def _():
        for block, part in enumerate((k0, k1, k2, k3)):
            kv_ref[:, block * tok : (block + 1) * tok] = part[...].astype(F32)
        near, length = place_ref[0], place_ref[1]
        rows = near * tok + lax.broadcasted_iota(jnp.int32, (tok, tok), 0)
        for block, bit in enumerate((0, 2, 1, 3)):
            keys = (near ^ bit) * tok + lax.broadcasted_iota(jnp.int32, (tok, tok), 1)
            allowed = (keys <= rows) & (keys < length)
            bias[:, block * tok : (block + 1) * tok] = jnp.where(allowed, 0.0, NEG)

    outs = []
    for inner in range(PAIR):
        head = pair * PAIR + inner
        keys = key_parts(kv_ref, head, 0)
        values = key_parts(kv_ref, head, H * RK + RK * DH)
        queries = query_parts(qm_ref, qt_ref, head)
        scores = dims(queries, keys, 0, 0) + bias[...]
        peak = jnp.max(scores, -1, keepdims=True)
        powers = jnp.exp(scores - peak)
        total = jnp.sum(powers, -1, keepdims=True)
        probs = (powers * (1.0 / total)).astype(BF)
        probs_ref[inner] = probs
        outs.append(dims(probs, values, 1, 1))
    attended_ref[...] = jnp.concatenate(outs, 1).astype(BF)


def attend(places, query_mix, query_turned, factors):
    tok = query_mix.shape[1]
    slots = 4 * tok
    table = pltpu.HBM((factors[0].shape[0], slots), F32)
    return pl.pallas_call(
        attend_kernel,
        grid=(H // PAIR,),
        out_shape=(
            jax.ShapeDtypeStruct((tok, H * DH), BF),
            pltpu.HBM((H, tok, slots), BF),
            table,
        ),
        in_specs=[SCALARS, whole(query_mix), whole(query_turned)] + [whole(f) for f in factors],
        out_specs=(
            pl.BlockSpec((tok, PAIR * DH), lambda i: (0, i)),
            pl.BlockSpec((PAIR, tok, slots), lambda i: (i, 0, 0)),
            whole(table),
        ),
        scratch_shapes=[pltpu.VMEM((tok, slots), F32)],
        compiler_params=pltpu.CompilerParams(vmem_limit_bytes=28 * 2**20),
        cost_estimate=SMALL,
    )(places, query_mix, query_turned, *pinned(*factors))


def attend_back_kernel(*refs):
    qm_ref, qt_ref, kv_ref, slope_ref, probs_all = refs[:5]
    kept_ref, sent_ref, qmix_ref, qbasis_ref, mix_ref, basis_ref, probs_held, psem = refs[5:]
    pair = pl.program_id(0)
    vm = H * RK + RK * DH
    kb = RK * DH

    def coming(at):
        return pltpu.make_async_copy(
            probs_all.at[pl.ds(at * PAIR, PAIR)], probs_held.at[at % 2], psem.at[at % 2]
        )

    @pl.when(pair == 0)
    def _():
        coming(pair).start()
        basis_ref[...] = jnp.zeros_like(basis_ref)
        qbasis_ref[...] = jnp.zeros_like(qbasis_ref)

    @pl.when(pair + 1 < pl.num_programs(0))
    def _():
        coming(pair + 1).start()

    coming(pair).wait()
    probs_ref = probs_held.at[pair % 2]
    for inner in range(PAIR):
        head = pair * PAIR + inner
        keys = key_parts(kv_ref, head, 0)
        values = key_parts(kv_ref, head, vm)
        queries = query_parts(qm_ref, qt_ref, head)
        slope = slope_ref[inner * DH : (inner + 1) * DH, :]
        probs_low = probs_ref[inner]
        slope_probs = dims(slope, values, 0, 0)
        probs = probs_low.astype(F32)
        weighted = probs * slope_probs
        total = jnp.sum(weighted, -1, keepdims=True)
        slope_scores = (weighted - probs * total).astype(BF)
        slope_query = dims(keys, slope_scores, 1, 1) * (DH**-0.5 / RQ)
        slope_key = dims(queries, slope_scores, 1, 0) * (1.0 / RK)
        slope_value = dims(slope, probs_low, 1, 0) * (1.0 / RK)
        for r in range(RK):
            row = head * RK + r
            for at, piece, side in ((0, slope_key, 0), (vm, slope_value, 1)):
                base = at + H * RK + r * DH
                here = side * RK + r
                basis_ref[here * DH : (here + 1) * DH, :] += kv_ref[pl.ds(at + row, 1), :] * piece
                mix_ref[pl.ds(side * H * RK + row, 1), :] = jnp.sum(
                    piece * kv_ref[base : base + DH, :], 0, keepdims=True
                )
        for r in range(RQ):
            row = head * RQ + r
            cut = slice(r * DH, (r + 1) * DH)
            qbasis_ref[cut, :] += qm_ref[pl.ds(row, 1), :] * slope_query
            qmix_ref[pl.ds(row, 1), :] = jnp.sum(slope_query * qt_ref[cut, :], 0, keepdims=True)

    @pl.when(pair == pl.num_programs(0) - 1)
    def _():
        half = kept_ref.shape[2] * 2
        tok = kept_ref.shape[2]
        km = H * RK
        for base, ref, begin, rows in (
            (0, mix_ref, 0, km),
            (km, basis_ref, 0, kb),
            (vm, mix_ref, km, km),
            (vm + km, basis_ref, kb, kb),
        ):
            part = ref[begin : begin + rows, :]
            for block in range(2):
                kept_ref[block, base : base + rows, :] = part[:, block * tok : (block + 1) * tok]
                sent_ref[block, base : base + rows, :] = part[
                    :, half + block * tok : half + (block + 1) * tok
                ].astype(BF)


def attend_back(query_mix, query_turned, row_factors, slope_attended, probs):
    tok = query_mix.shape[1]
    rows, slots = row_factors.shape
    outs = (
        jax.ShapeDtypeStruct((2, rows, tok), F32),
        jax.ShapeDtypeStruct((2, rows, tok), BF),
        jax.ShapeDtypeStruct((H * RQ, tok), F32),
        jax.ShapeDtypeStruct((RQ * DH, tok), F32),
    )
    return pl.pallas_call(
        attend_back_kernel,
        grid=(H // PAIR,),
        out_shape=outs,
        in_specs=[
            whole(query_mix),
            whole(query_turned),
            whole(row_factors),
            pl.BlockSpec((PAIR * DH, tok), lambda i: (i, 0)),
            pl.BlockSpec(memory_space=pltpu.HBM),
        ],
        out_specs=tuple(whole(o) for o in outs),
        scratch_shapes=[
            pltpu.VMEM((2 * H * RK, slots), F32),
            pltpu.VMEM((2 * RK * DH, slots), F32),
            pltpu.VMEM((2, PAIR, tok, slots), BF),
            pltpu.SemaphoreType.DMA((2,)),
        ],
        compiler_params=pltpu.CompilerParams(vmem_limit_bytes=28 * 2**20),
        cost_estimate=SMALL,
    )(query_mix, query_turned, *pinned(row_factors), slope_attended, *pinned(probs))


QB, KB, VB = RQ * DH, RK * DH, RK * DH
QM, KM, VM = H * RQ, H * RK, H * RK
LEFT = 512
GAINS = LEFT + KB + VB + KM + VM
PACKED = 896


def steps_of_any_mesh(
    tokens, places, cosine, sine, packed, merge_weight, both, down_weight, cotangent
):
    tok, width = tokens.shape
    group, twice, hidden = both.shape
    rows = twice // 2
    cut = down_weight.shape[0]
    axes = ("wide", "narrow")
    packed = [lax.all_gather(packed, axes, axis=0, tiled=True)[None]]
    merge = [lax.all_gather(merge_weight, axes, axis=0, tiled=True)[None]]
    downs = [lax.all_gather(down_weight, "wide", axis=0, tiled=True)[None]]
    both = lax.all_to_all(both, "narrow", 0, 0, tiled=True)
    both = lax.all_gather(both, "wide", axis=0, tiled=False)
    both = both.reshape(-1, 2, rows, hidden).transpose(1, 0, 2, 3)
    both = both.reshape(2, 8, 4, width // 32, hidden).transpose(1, 2, 0, 3, 4)
    weights_in = ([both.reshape(8, 4, width // 16, hidden)], list(range(8)), downs, [0])

    hidden_one, inverse_one, gains, weights, query_mix, query_turned, own_factors = project(
        tokens, cosine, sine, packed, [0]
    )
    attended, probs, row_factors = attend(
        places, query_mix, query_turned, gather_narrow(own_factors)
    )
    hidden_two, middle, inverse_two = middle_of(attended, tokens, gains, merge, [0])
    own, far, close, cross = gather_narrow(hidden_two)
    cot_own, cot_far, cot_near, cot_cross = gather_narrow(cotangent)
    parts = [
        feed((own, close), (cot_own, cot_near), *weights_in),
        feed((far, cross), (cot_far, cot_cross), *weights_in),
    ]
    hidden_feed, slope_gate, slope_up = zip(*(part[:3] for part in parts))
    came_near = flip(parts[0][4], "narrow", 1)
    came_far = flip(add_low(parts[1][3], flip(parts[1][4], "narrow", 1)), "narrow", 2)
    full = slopes_of((own, close, far, cross), slope_gate, slope_up, list(range(width // 128)))
    full = full.transpose(1, 0, 3, 2).reshape(2, width, hidden)
    slopes = jnp.concatenate([scatter_wide(s).reshape(group, rows, hidden) for s in full], 1)
    slopes = lax.all_to_all(slopes.astype(BF), "narrow", 0, 0, tiled=True)
    cots = (cot_own, cot_near, cot_far, cot_cross)
    down_slope = scatter_wide(down_slopes(hidden_feed, cots, [0], cut)[0])
    kept, sent = feed_out(hidden_feed, downs, [0])
    fed = kept + flip(sent, "narrow", 1).astype(F32)
    fed = fed[0] + flip(fed[1].astype(BF), "narrow", 2).astype(F32)
    output = (middle + fed).astype(BF)

    slope_middle, slope_low, slope_attended, feed_gain_slope = turn_back(
        parts[0][3], came_near, came_far, middle, inverse_two, gains, cotangent, merge, [0]
    )
    merge_slope = scatter_all(dims(attended, slope_low, 0, 0).astype(BF))
    factors_in = (query_mix, query_turned, row_factors, slope_attended, probs)
    key_kept, key_sent, query_mix_slope, query_basis_slope = attend_back(*factors_in)
    key_pair = key_kept + flip(key_sent, "narrow", 1).astype(F32)
    key_came = flip(key_pair[1].astype(BF), "narrow", 2)
    part, query_slopes = query_end(
        [0], query_mix_slope, query_basis_slope, cosine, sine, hidden_one, weights
    )
    tokens_slope, key_slopes = key_end(
        [0], key_pair[0], key_came, cosine, sine, hidden_one, weights, part, tokens, inverse_one,
        gains, slope_middle, feed_gain_slope,
    )
    query_slopes, key_slopes = scatter_all(query_slopes), scatter_all(key_slopes)
    return output, tokens_slope, query_slopes, key_slopes, merge_slope, slopes, down_slope


def steps_of_small_mesh(
    tokens, places, cosine, sine, packed, merge_weight, both_in, down_weight, cotangent
):
    tok, width = tokens.shape
    cut = down_weight.shape[0]
    high, low = wide_place()
    rounds = lax.axis_size("wide") // 2
    group = lax.axis_size("narrow")
    join = lambda a, b: jnp.concatenate([a, b], 0)

    first = turned(jnp.concatenate([packed, merge_weight], 1)[None])
    both = lax.all_to_all(both_in, "narrow", 0, 0, tiled=True)
    first = tie(*first)
    one = jnp.concatenate([f[:, :, :PACKED] for f in first], 0)
    two = jnp.concatenate([f[:, :, PACKED:] for f in first], 0)
    one, one_came, two, two_came, both = tie(
        one, flip(one, "narrow", 2), two, flip(two, "wide", 1), both
    )
    one, two = join(one, one_came), join(two, two_came)
    pieces = [both[None]]
    one, one_came, two, two_came, piece = tie(
        one, flip(one, "wide", 1), two, flip(two, "narrow", 2), turn(pieces[0], 1)
    )
    one, two = join(one, one_came), join(two, two_came)
    where, merge_where = relative_blocks(), relative_blocks(True)
    both_where = [((high - k) % rounds) * 2 + low for k in range(rounds)] + [
        ((high - k) % rounds) * 2 + 1 - low for k in range(rounds)
    ]
    one, piece, down_own, first = tie(one, piece, down_weight, pieces[0])
    pieces += [piece, turn(piece, 1)]
    down_came = flip(down_own, "wide", 1)
    others = [flip(first, "wide", 1)]
    hidden_one, inverse_one, gains, weights, query_mix, query_turned, factor = project(
        tokens, cosine, sine, [one, flip(one, "narrow", 1)], where
    )
    factor, two, first, down_came = tie(factor, two, pieces[1], down_came)
    merge = [two, flip(two, "narrow", 1)]
    others.append(flip(first, "wide", 1))
    factor_far, factor_near, pieces[2], others[0], down_came = tie(
        flip(factor, "narrow", 2), flip(factor, "narrow", 1), pieces[2], others[0], down_came
    )
    pieces.append(turn(pieces[2], 1))
    pair = jnp.where(low == 0, jnp.stack([down_own, down_came]), jnp.stack([down_came, down_own]))
    pair = jnp.stack([pair.reshape(2 * cut, width)] * rounds)
    factor_cross, cot_own, first, pieces[3], others[1], pair = tie(
        flip(factor_far, "narrow", 1), cotangent, pieces[2], pieces[3], others[1], pair
    )
    downs = [ring_all_to_all(pair)]
    down_where = list(range(rounds))

    cot_far = flip(cot_own, "narrow", 2)
    others += [flip(first, "wide", 1), flip(pieces[3], "wide", 1)]
    attended, probs, row_factors = attend(
        places, query_mix, query_turned, (factor, factor_far, factor_near, factor_cross)
    )
    attended, cot_far, others[2], others[3], merge[1] = tie(
        attended, cot_far, others[2], others[3], merge[1]
    )
    hidden_two, middle, inverse_two = middle_of(attended, tokens, gains, merge, merge_where)
    own, cot_far = tie(hidden_two, cot_far)

    far, close = flip(own, "narrow", 2), flip(own, "narrow", 1)
    cot_near, cot_cross = flip(cot_own, "narrow", 1), flip(cot_far, "narrow", 1)
    weights_in = (pieces + others, both_where, downs, down_where)
    one = feed((own, close), (cot_own, cot_near), *weights_in)
    far, one_sent = tie(far, one[4])
    came_near = flip(one_sent, "narrow", 1)
    cross = flip(far, "narrow", 1)
    two = feed((far, cross), (cot_far, cot_cross), *weights_in)
    for_far = add_low(two[3], flip(two[4], "narrow", 1))
    hidden_feed, slope_gate, slope_up = zip(one[:3], two[:3])
    for_far, slope_gate, slope_up, came_near = tie(for_far, slope_gate, slope_up, came_near)
    came_far = flip(for_far, "narrow", 2)
    slots = (own, close, far, cross)
    cots = (cot_own, cot_near, cot_far, cot_cross)
    order = [2 * k + 1 - low for k in range(rounds)]
    to_send = slopes_of(slots, slope_gate, slope_up, order, True)
    *hidden_feed, gate_sent, up_sent = tie(*hidden_feed, *to_send)
    gate_came = flip(gate_sent, "wide", 1)
    down_parts = down_slopes(hidden_feed, cots, [0], cut)[0]
    slope_gate, slope_up, down_parts = tie(slope_gate, slope_up, down_parts)
    down_parts = ring_all_to_all(down_parts.reshape(rounds, 2 * cut, width))
    to_keep = slopes_of(slots, slope_gate, slope_up, [2 * k + low for k in range(rounds)])
    came_far, to_keep = tie(came_far, to_keep)

    slope_middle, slope_low, slope_attended, feed_gain_slope = turn_back(
        one[3], came_near, came_far, middle, inverse_two, gains, cotangent, merge, merge_where
    )
    merge_sent, merge_kept = outer_blocks(scatter_order(True), attended, slope_low)
    merge_sent, slope_attended, gate_came, up_sent = tie(
        merge_sent, slope_attended, gate_came, up_sent
    )
    up_came = flip(up_sent, "wide", 1)
    merge_came = flip(merge_sent, "narrow", 1)
    merge_sum = add_low(merge_kept, merge_came)
    slope_attended, merge_sum = tie(slope_attended, merge_sum)
    merge_came = flip(merge_sum[8:], "narrow", 2)
    key_kept, key_sent, query_mix_slope, query_basis_slope = attend_back(
        query_mix, query_turned, row_factors, slope_attended, probs
    )
    key_kept, key_sent, query_basis_slope, merge_came, up_came, down_parts = tie(
        key_kept, key_sent, query_basis_slope, merge_came, up_came, down_parts
    )
    key_came = flip(key_sent, "narrow", 1)
    key_pair = key_kept + key_came.astype(F32)
    key_far, up_came, query_basis_slope, merge_came = tie(
        key_pair[1].astype(BF), up_came, query_basis_slope, merge_came
    )
    merge_sum = add_low(merge_sum[:8], merge_came)
    key_came = flip(key_far, "narrow", 2)
    parts = ring_all_to_all(add_low(to_keep, jnp.stack([gate_came, up_came], 1)))
    merge_came = flip(merge_sum[4:], "wide", 1)
    order = scatter_order(True)
    part, query_sent, query_kept = query_end(
        order, query_mix_slope, query_basis_slope, cosine, sine, hidden_one, weights
    )
    key_came, part = tie(key_came, part)
    tokens_slope, ends_sent, ends = key_end(
        order, key_pair[0], key_came, cosine, sine, hidden_one, weights, part, tokens, inverse_one,
        gains, slope_middle, feed_gain_slope, query_sent, query_kept,
    )

    ends = add_low(ends, flip(ends_sent, "narrow", 1))
    ends, hidden_feed = tie(ends, hidden_feed)
    ends_came = flip(ends[8:], "narrow", 2)
    kept, sent = feed_out(hidden_feed, downs, down_where)
    ends_came, kept, sent = tie(ends_came, kept, sent)
    ends = add_low(ends[:8], ends_came)
    ends, sent, parts, down_parts = tie(ends, sent, parts, down_parts)
    down_sum = jnp.sum(down_parts.astype(F32), 0).reshape(2, cut, width)
    down_came = flip(pick(down_sum, 1 - low, 0).astype(BF), "wide", 1)
    ends_came = flip(ends[4:], "wide", 1)
    fed = kept + flip(sent, "narrow", 1).astype(F32)
    slopes = lax.all_to_all(finish(parts, group), "narrow", 0, 0, tiled=True)
    merge_sum = add_low(merge_sum[:4], merge_came)
    ends_came, fed, merge_sum = tie(ends_came, fed, merge_sum)
    ends = jnp.concatenate([add_low(ends[:4], ends_came), merge_sum], 2)
    ends, fed_far = tie(ends, fed[1].astype(BF))
    sums = spread_turns(ends)
    slopes = after(slopes, sums)
    fed_came = flip(fed_far, "narrow", 2)
    down_slope = pick(down_sum, low, 0) + down_came.astype(F32)
    merge_slope = sums[:, PACKED:]
    output = (middle + fed[0] + fed_came.astype(F32)).astype(BF)
    query_slopes, key_slopes = sums[:, :LEFT], sums[:, LEFT:PACKED]
    return output, tokens_slope, query_slopes, key_slopes, merge_slope, slopes, down_slope


def per_device(
    tokens,
    lengths,
    attend_gain,
    query_heads,
    query_basis,
    key_heads,
    key_basis,
    value_heads,
    value_basis,
    merge_weight,
    feed_gain,
    gate_weight,
    up_weight,
    down_weight,
    cotangent,
):
    tok, width = tokens.shape
    wide_count = lax.axis_size("wide")
    narrow_count = lax.axis_size("narrow")
    near = lax.axis_index("narrow")
    rows = gate_weight.shape[0]
    cut = down_weight.shape[0]
    hidden = cut * wide_count
    small = small_mesh()

    positions = (near * tok + jnp.arange(tok, dtype=jnp.int32)).astype(F32)
    frequency = jnp.power(10000.0, -2.0 * jnp.arange(DH // 2, dtype=F32) / DH)
    angles = frequency[:, None] * positions[None, :]
    cosine, sine = jnp.cos(angles), jnp.sin(angles)

    packed = jnp.concatenate(
        [
            query_basis,
            query_heads,
            jnp.zeros((rows, LEFT - QB - QM), BF),
            key_basis,
            value_basis,
            key_heads,
            value_heads,
            attend_gain[:, None],
            feed_gain[:, None],
            jnp.zeros((rows, PACKED - GAINS - 2), BF),
        ],
        1,
    )

    def columns(weight):
        parts = weight.reshape(rows, wide_count, narrow_count, cut).transpose(2, 0, 1, 3)
        return parts.reshape(narrow_count, rows, hidden)

    both_in = jnp.concatenate([columns(gate_weight), columns(up_weight)], 1)
    places = jnp.stack([near.astype(jnp.int32), lengths[0].astype(jnp.int32)])
    if small:
        exact = steps_of_small_mesh
    else:
        exact = steps_of_any_mesh
    output, tokens_slope, query_slopes, key_slopes, merge_slope, slopes, down_slope = exact(
        tokens, places, cosine, sine, packed, merge_weight, both_in, down_weight, cotangent
    )
    if small:
        slopes = unmix(slopes, cut)
    else:
        slopes = slopes.reshape(narrow_count, 2, rows, wide_count, cut).transpose(1, 2, 3, 0, 4)
        slopes = slopes.reshape(2, rows, hidden * narrow_count).astype(F32)

    base = GAINS - LEFT
    return (
        output,
        tokens_slope,
        key_slopes[:, base],
        query_slopes[:, QB : QB + QM],
        query_slopes[:, :QB],
        key_slopes[:, KB + VB : KB + VB + KM],
        key_slopes[:, :KB],
        key_slopes[:, KB + VB + KM : KB + VB + KM + VM],
        key_slopes[:, KB : KB + VB],
        merge_slope,
        key_slopes[:, base + 1],
        slopes[0],
        slopes[1],
        down_slope,
    )


def solution(mesh):
    both = ("wide", "narrow")
    row, vector = P(both, None), P(both)
    return jax.shard_map(
        per_device,
        mesh=mesh,
        in_specs=(row, P("wide"), vector) + (row,) * 7 + (vector,) + (row,) * 4,
        out_specs=(row, row, vector) + (row,) * 7 + (vector,) + (row,) * 3,
        check_vma=False,
    )
```
